32 devices in a mesh: event: 2 (over x), phi: 16 (over z, y, core).
Axes of the slice: x: 2, y: 2, z: 4, core: 2. Of those that a mesh axis runs over, the one named last changes fastest.
Arguments:
- hit_feats: bfloat16 [12, 131072], P(None, ('event', 'phi')), parts along dimension 1, may hold values from -6 to 6
- layer_ids: int32 [131072], P(('event', 'phi')), parts along dimension 0, may hold values from 0 to 15
- edge_tiles: bfloat16 [1024, 8, 128, 128], P(('event', 'phi')), parts along dimension 0
- src_blocks: int32 [1024, 8], P(('event', 'phi')), parts along dimension 0, may hold values from 0 to 159
- live_slots: int32 [1024], P(('event', 'phi')), parts along dimension 0, may hold values from 1 to 8, as said below
- anchor_hits: int32 [32768], P(('event', 'phi')), parts along dimension 0, may hold values from 0 to 4095
- positive_hits: int32 [32768], P(('event', 'phi')), parts along dimension 0, may hold values from 0 to 20479
- negative_hits: int32 [32768], P(('event', 'phi')), parts along dimension 0, may hold values from 0 to 20479
- w_enc: bfloat16 [12, 128], replicated, may hold values from -1.75 to 1.75
- layer_table: bfloat16 [16, 128], replicated, may hold values from -3 to 3
- w_self: bfloat16 [2, 128, 128], replicated, may hold values from -0.5 to 0.5
- w_agg: bfloat16 [2, 128, 128], replicated, may hold values from -0.5 to 0.5
- w_out: bfloat16 [2, 128, 128], replicated, may hold values from -0.5 to 0.5
Outputs:
- loss: float32 [2], P('event'), parts along dimension 0
- grad_enc: float32 [24, 128], P('event'), parts along dimension 0
- grad_table: float32 [32, 128], P('event'), parts along dimension 0
- grad_self: float32 [4, 128, 128], P('event'), parts along dimension 0
- grad_agg: float32 [4, 128, 128], P('event'), parts along dimension 0
- grad_out: float32 [4, 128, 128], P('event'), parts along dimension 0
The draws below stay inside these ranges and needn't reach their ends.
There are 2 independent parts, one for each index of `event`. The reference program is written for one: setup_inputs(seed, part) draws one part's arguments, and reference() takes and returns one part's arrays. A program takes and returns all parts, laid end to end along the dimension named above; an argument that names none is the same for every part. Nothing has to cross between parts.
Inputs may be any that keep to these rules, and one draw needn't show every extreme that they name: `live_slots`: in every draw some node block has all 8 slots live.
All inputs are finite; a program needn't handle non-finite values.
Results may differ from the reference program's by a relative error of at most 0.0022.
Values may be sent and summed in bfloat16 or wider, within the bound.
No kernel may reach another device: no remote copies, remote signals or barrier semaphores. Data moves between devices by JAX's collectives and lax.ppermute only.
A program may use at most 128 MiB of HBM per device.

```python
import math
import jax
import jax.numpy as jnp
from jax import lax

WIDTH = 128
FEAT = 12
NLAY = 16
LAYERS = 2
BLK = 128
SLOTS = 8
REACH = 2
NB = 32
CON = 1024
NB_ALL = 512
HITS = 65536
CON_ALL = 16384
N_PHI = 16


def draw_edge_tiles(key, part):
    first_key, second_key = jax.random.split(key)
    shape = (NB_ALL, SLOTS, BLK, BLK)
    present = jax.random.uniform(first_key, shape, jnp.float32) < 0.25
    weights = jax.random.uniform(second_key, shape, jnp.float32, minval=0.05, maxval=0.25)
    return jnp.where(present, weights, 0.0).astype(jnp.bfloat16)


def draw_live_slots(key, part):
    sector_count = NB_ALL // NB
    first_key, second_key, third_key = jax.random.split(key, 3)
    order = jax.random.permutation(first_key, sector_count).astype(jnp.int32)
    level = 1 + order * SLOTS // sector_count
    level_rows = jnp.repeat(level, NB)
    dropped = jax.random.randint(second_key, (NB_ALL,), 0, level_rows // 2 + 1, dtype=jnp.int32)
    counts = level_rows - dropped
    chosen_block = jax.random.randint(third_key, (sector_count,), 0, NB, dtype=jnp.int32)
    filled = jnp.arange(NB_ALL, dtype=jnp.int32) % NB == jnp.repeat(chosen_block, NB)
    return jnp.where(filled, level_rows, counts).astype(jnp.int32)


def set_ends(result, own_key, smallest, top_value):
    spot = [jax.random.randint(jax.random.fold_in(own_key, axis), (), 0, length) for axis, length in enumerate(result.shape)]
    main_axis = result.shape.index(max(result.shape))
    next_to = spot[:main_axis] + [(spot[main_axis] + 1) % result.shape[main_axis]] + spot[main_axis + 1:]
    return result.at[tuple(spot)].set(smallest).at[tuple(next_to)].set(top_value)


def level_of(key, extent, cuts, low, largest):
    level, own = 1.0, jax.random.fold_in(key, 6)
    for position, parts in cuts:
        draws = jnp.exp(jax.random.uniform(jax.random.fold_in(own, position), (parts,), jnp.float32, low / len(cuts), largest / len(cuts)))
        level = level * jnp.repeat(draws, extent[position] // parts).reshape([-1 if axis == position else 1 for axis in range(len(extent))])
    return level


def normal_values(key, dims, width, most, cuts=(), kind=jnp.bfloat16):
    values = jax.random.normal(key, dims, jnp.float32) * width
    if len(cuts) > 0:
        values = level_of(key, dims, cuts, -0.22, 0.18) * values
    return jnp.clip(values, min=-most, max=most).astype(kind)


def setup_inputs(seed: int = 0, part: int = 0) -> dict:
    splits = jax.random.split(jax.random.key(seed), 14)
    part_splits = jax.random.split(jax.random.fold_in(splits[13], part), 14)
    hit_feats = normal_values(part_splits[0], (FEAT, HITS), 1.0, 6.0, ((1, 16),))
    layer_ids = set_ends(jax.random.randint(part_splits[1], (HITS,), 0, NLAY), jax.random.fold_in(part_splits[1], 1), 0, NLAY - 1).astype(jnp.int32)
    edge_tiles = draw_edge_tiles(jax.random.fold_in(jax.random.fold_in(splits[13], part), 71), part)
    src_blocks = set_ends(jax.random.randint(part_splits[3], (NB_ALL, SLOTS), 0, (2 * REACH + 1) * NB), jax.random.fold_in(part_splits[3], 1), 0, ((2 * REACH + 1) * NB) - 1).astype(jnp.int32)
    live_slots = draw_live_slots(jax.random.fold_in(jax.random.fold_in(splits[13], part), 71), part)
    anchor_hits = set_ends(jax.random.randint(part_splits[5], (CON_ALL,), 0, NB * BLK), jax.random.fold_in(part_splits[5], 1), 0, (NB * BLK) - 1).astype(jnp.int32)
    positive_hits = set_ends(jax.random.randint(part_splits[6], (CON_ALL,), 0, (2 * REACH + 1) * NB * BLK), jax.random.fold_in(part_splits[6], 1), 0, ((2 * REACH + 1) * NB * BLK) - 1).astype(jnp.int32)
    negative_hits = set_ends(jax.random.randint(part_splits[7], (CON_ALL,), 0, (2 * REACH + 1) * NB * BLK), jax.random.fold_in(part_splits[7], 1), 0, ((2 * REACH + 1) * NB * BLK) - 1).astype(jnp.int32)
    w_enc = normal_values(splits[8], (FEAT, WIDTH), FEAT ** -0.5, 1.75)
    layer_table = normal_values(splits[9], (NLAY, WIDTH), 0.5, 3.0)
    w_self = normal_values(splits[10], (LAYERS, WIDTH, WIDTH), WIDTH ** -0.5, 0.5)
    w_agg = normal_values(splits[11], (LAYERS, WIDTH, WIDTH), WIDTH ** -0.5, 0.5)
    w_out = normal_values(splits[12], (LAYERS, WIDTH, WIDTH), WIDTH ** -0.5, 0.5)
    return {"hit_feats": hit_feats, "layer_ids": layer_ids, "edge_tiles": edge_tiles, "src_blocks": src_blocks, "live_slots": live_slots, "anchor_hits": anchor_hits, "positive_hits": positive_hits, "negative_hits": negative_hits, "w_enc": w_enc, "layer_table": layer_table, "w_self": w_self, "w_agg": w_agg, "w_out": w_out}


loss_divisor = 64.0

def contract_rows(left_side, right_side):
    return lax.dot_general(left_side, right_side, (((0,), (0,)), ((), ())), preferred_element_type=jnp.float32)

def contract_cols(left_side, right_side):
    return lax.dot_general(left_side, right_side, (((1,), (1,)), ((), ())), preferred_element_type=jnp.float32)

def contract_inner(left_side, right_side):
    return lax.dot_general(left_side, right_side, (((1,), (0,)), ((), ())), preferred_element_type=jnp.float32)

def contrast_terms(window, anchor_here, positive_here, negative_here, centre, latent_width):
    anchor = window[centre + anchor_here].astype(jnp.float32)
    positive = window[positive_here].astype(jnp.float32)
    negative = window[negative_here].astype(jnp.float32)
    inv_root = 1.0 / math.sqrt(latent_width)
    score_gap = (lax.optimization_barrier(jnp.sum(anchor * negative, axis=1)) - lax.optimization_barrier(jnp.sum(anchor * positive, axis=1))) * inv_root
    return (score_gap, anchor, positive, negative)

def contrast_grad(window, anchor_here, positive_here, negative_here, centre, latent_width):
    score_gap, anchor, positive, negative = contrast_terms(window, anchor_here, positive_here, negative_here, centre, latent_width)
    weight_coef = (jax.nn.sigmoid(score_gap) * (1.0 / (loss_divisor * math.sqrt(latent_width))))[:, None]
    gradient = jnp.zeros(window.shape, jnp.float32)
    gradient = gradient.at[centre + anchor_here].add(weight_coef * (negative - positive))
    gradient = gradient.at[positive_here].add(-weight_coef * anchor)
    gradient = gradient.at[negative_here].add(weight_coef * anchor)
    return gradient

def reference(hit_feats, layer_ids, edge_tiles, src_blocks, live_slots, anchor_hits, positive_hits, negative_hits, w_enc, layer_table, w_self, w_agg, w_out):
    hit_count = NB * BLK
    span_count = 2 * REACH + 1
    sectors = jnp.arange(N_PHI, dtype=jnp.int32)
    offsets = jnp.arange(-REACH, REACH + 1, dtype=jnp.int32)
    onehot = (jnp.arange(NLAY, dtype=jnp.int32)[:, None] == layer_ids[None, :]).astype(jnp.bfloat16)
    encoded = contract_rows(hit_feats, w_enc) + contract_rows(onehot, layer_table)
    squashed = jnp.tanh(encoded)
    latents = squashed.astype(jnp.bfloat16)
    tiles = edge_tiles.reshape(N_PHI, NB, SLOTS, BLK, BLK)
    sources = src_blocks.reshape(N_PHI, NB, SLOTS)
    live_mask = jnp.arange(SLOTS, dtype=jnp.int32)[None, None, :] < live_slots.reshape(N_PHI, NB)[:, :, None]

    def window_of(grid, sector):
        return jnp.take(grid, (sector + offsets) % N_PHI, axis=0).reshape(span_count * hit_count, WIDTH)

    def aggregate(current):
        grid = current.reshape(N_PHI, hit_count, WIDTH)

        def one_sector(sector_items):
            sector, tiles_here, sources_here, live_here = sector_items
            blocks = window_of(grid, sector).reshape(span_count * NB, BLK, WIDTH)
            chosen = jnp.where(live_here[:, :, None, None], blocks[sources_here], jnp.zeros((), blocks.dtype))
            return jnp.einsum('bsij,bsjw->biw', tiles_here.astype(jnp.float32), chosen.astype(jnp.float32))
        return lax.map(one_sector, (sectors, tiles, sources, live_mask)).reshape(N_PHI * hit_count, WIDTH)

    def give_back(piece_fn, sector_items):

        def advance(running, item_now):
            pieces = piece_fn(item_now).reshape(span_count, hit_count, WIDTH)
            for slot_index in range(span_count):
                portion = pieces[slot_index]
                if slot_index != REACH:
                    portion = lax.optimization_barrier(portion.astype(jnp.bfloat16)).astype(jnp.float32)
                target = (item_now[0] + slot_index - REACH) % N_PHI
                current = lax.dynamic_index_in_dim(running, target, 0, keepdims=False)
                running = lax.dynamic_update_index_in_dim(running, current + portion, target, 0)
            return (running, None)
        running, _ = lax.scan(advance, jnp.zeros((N_PHI, hit_count, WIDTH), jnp.float32), sector_items)
        return running.reshape(N_PHI * hit_count, WIDTH)
    stored = []
    for layer_index in range(LAYERS):
        aggregated = aggregate(latents).astype(jnp.bfloat16)
        activation = jnp.dot(latents, w_self[layer_index], preferred_element_type=jnp.float32) + jnp.dot(aggregated, w_agg[layer_index], preferred_element_type=jnp.float32)
        hidden = jax.nn.relu(activation).astype(jnp.bfloat16)
        updated = (latents.astype(jnp.float32) + jnp.dot(hidden, w_out[layer_index], preferred_element_type=jnp.float32)).astype(jnp.bfloat16)
        stored.append((latents, aggregated, activation, hidden))
        latents = updated
    final_grid = latents.reshape(N_PHI, hit_count, WIDTH)
    centre = REACH * hit_count
    triplets = (sectors, anchor_hits.reshape(N_PHI, CON), positive_hits.reshape(N_PHI, CON), negative_hits.reshape(N_PHI, CON))

    def sector_loss(sector_items):
        sector, anchor_here, positive_here, negative_here = sector_items
        score_gap = contrast_terms(window_of(final_grid, sector), anchor_here, positive_here, negative_here, centre, WIDTH)[0]
        return jnp.sum(jax.nn.softplus(score_gap))
    loss = (jnp.sum(lax.map(sector_loss, triplets)) / CON_ALL).reshape(1)

    def contrast_piece(sector_items):
        sector, anchor_here, positive_here, negative_here = sector_items
        return contrast_grad(window_of(final_grid, sector), anchor_here, positive_here, negative_here, centre, WIDTH)
    gradient = give_back(contrast_piece, triplets)
    self_grads = [None] * LAYERS
    agg_grads = [None] * LAYERS
    out_grads = [None] * LAYERS
    for layer_index in range(LAYERS - 1, -1, -1):
        before, aggregated, activation, hidden = stored[layer_index]
        upstream = gradient.astype(jnp.bfloat16)
        out_grads[layer_index] = contract_rows(hidden, upstream)
        hidden_grad = contract_cols(upstream, w_out[layer_index])
        act_grad = jnp.where(activation > 0, hidden_grad, 0.0).astype(jnp.bfloat16)
        self_grads[layer_index] = contract_rows(before, act_grad)
        agg_grads[layer_index] = contract_rows(aggregated, act_grad)
        agg_grad = contract_cols(act_grad, w_agg[layer_index]).astype(jnp.bfloat16)
        direct = gradient + contract_cols(act_grad, w_self[layer_index])
        agg_grid = agg_grad.reshape(N_PHI, NB, BLK, WIDTH)

        def adjacency_piece(sector_items):
            sector, tiles_here, sources_here, live_here, grad_here = sector_items
            contrib = jnp.einsum('bsij,biw->bsjw', tiles_here.astype(jnp.float32), grad_here.astype(jnp.float32))
            contrib = jnp.where(live_here[:, :, None, None], contrib, 0.0)
            return jax.ops.segment_sum(contrib.reshape(NB * SLOTS, BLK, WIDTH), sources_here.reshape(NB * SLOTS), num_segments=span_count * NB)
        gradient = direct + give_back(adjacency_piece, (sectors, tiles, sources, live_mask, agg_grid))
    encoded_grad = (gradient * (1.0 - squashed * squashed)).astype(jnp.bfloat16)
    grad_enc = contract_inner(hit_feats, encoded_grad)
    grad_table = contract_inner(onehot, encoded_grad)
    return (loss, grad_enc, grad_table, jnp.stack(self_grads), jnp.stack(agg_grads), jnp.stack(out_grads))
```

```python
import math

import jax
import jax.numpy as jnp
from jax import lax
from jax.experimental import pallas as pl
from jax.experimental.pallas import tpu as pltpu
from jax.sharding import PartitionSpec as P

loss_divisor = 64.0
F32 = jnp.float32
BF16 = jnp.bfloat16
VMEM_LIMIT = 56 * 1024 * 1024
PACK_ROWS = 16
GROUP = 4

PIECES = 5


def vmem():
    return pl.BlockSpec(memory_space=pltpu.VMEM)


def smem():
    return pl.BlockSpec(memory_space=pltpu.SMEM)


def in_hbm():
    return pl.BlockSpec(memory_space=pl.ANY)


def params():
    return pltpu.CompilerParams(vmem_limit_bytes=VMEM_LIMIT)


def dot_nn(left, right):
    return lax.dot_general(left, right, (((1,), (0,)), ((), ())), preferred_element_type=F32)


def dot_tn(left, right):
    return lax.dot_general(left, right, (((0,), (0,)), ((), ())), preferred_element_type=F32)


def dot_nt(left, right):
    return lax.dot_general(left, right, (((1,), (1,)), ((), ())), preferred_element_type=F32)


def far_pairs(count):
    return [((p + 2) % count if p % 2 == 0 else (p - 2) % count, p) for p in range(count)]


def near_pairs(count):
    return [((p - 2) % count if p % 2 == 0 else (p + 2) % count, p) for p in range(count)]


def core_pairs(count):
    return [(p ^ 1, p) for p in range(count)]


def send(value, pairs):
    return lax.ppermute(value, "phi", pairs)


def turned(pairs):
    return [(target, source) for source, target in pairs]


def gather_window(value):
    count = lax.axis_size("phi")
    far = send(value, far_pairs(count))
    near = send(value, near_pairs(count))
    other = send(value, core_pairs(count))
    passed = send(far, core_pairs(count))
    return (value, far, near, other, passed)


def return_pieces(far, near, other, passed):
    count = lax.axis_size("phi")
    from_core = send(passed, core_pairs(count))
    from_near = send(near, turned(near_pairs(count)))
    from_other = send(other, core_pairs(count))
    joined = (far.astype(F32) + from_core.astype(F32)).astype(BF16)
    from_far = send(joined, turned(far_pairs(count)))
    return (from_far, from_near, from_other)


def total_over_phi(value):
    count = lax.axis_size("phi")
    if count & (count - 1) or count < 4:
        return lax.psum(value, "phi")
    half = value.shape[0] // 2
    odd = lax.axis_index("phi") % 2
    kept = lax.dynamic_slice_in_dim(value, odd * half, half, 0)
    given = lax.dynamic_slice_in_dim(value, (1 - odd) * half, half, 0)
    part = kept + send(given, core_pairs(count))
    step = 2
    while step < count:
        part = part + send(part, [(p, p ^ step) for p in range(count)])
        step *= 2
    back = send(part, core_pairs(count))
    return jnp.where(odd == 0, jnp.concatenate([part, back]), jnp.concatenate([back, part]))


def fetch_tiles(tiles_hbm, tiles, sems, groups):
    for g in range(groups):
        pltpu.make_async_copy(
            tiles_hbm.at[pl.ds(g * GROUP, GROUP)], tiles.at[pl.ds(g * GROUP, GROUP)], sems.at[g]
        ).start()


def await_tiles(tiles_hbm, tiles, sems, g):
    first = pl.multiple_of(g * GROUP, GROUP)
    pltpu.make_async_copy(
        tiles_hbm.at[pl.ds(first, GROUP)], tiles.at[pl.ds(first, GROUP)], sems.at[g]
    ).wait()


def encode_operand(pack_ref, start, width):
    rows = pack_ref[:, pl.ds(start, width)]
    ids = rows.astype(F32)[12:13, :]
    layers = lax.broadcasted_iota(jnp.int32, (PACK_ROWS, width), 0).astype(F32)
    onehot = (layers == ids).astype(BF16)
    return jnp.concatenate([rows, onehot], axis=0)


def forward_group(g, src, tiles, window, w_self, w_agg, w_out, agg_ref, hidden_t_ref, new_ref):
    slots = tiles.shape[1]
    sums = []
    for q in range(GROUP):
        b = g * GROUP + q
        left = jnp.concatenate([tiles[b, s] for s in range(slots)], axis=1)
        right = jnp.concatenate([window[src[b * slots + s]] for s in range(slots)], axis=0)
        sums.append(dot_nn(left, right))
    first = pl.multiple_of(g * GROUP, GROUP)
    agg = jnp.concatenate(sums, axis=0).astype(BF16)
    rows, width = agg.shape
    here = window[pl.ds(first, GROUP)].reshape(rows, width)
    activation = dot_nn(here, w_self[...]) + dot_nn(agg, w_agg[...])
    hidden = jnp.maximum(activation, 0.0)
    hidden_b = hidden.astype(BF16)
    updated = (here.astype(F32) + dot_nn(hidden_b, w_out[...])).astype(BF16)
    agg_ref[pl.ds(first, GROUP)] = agg.reshape(GROUP, rows // GROUP, width)
    new_ref[pl.ds(first, GROUP)] = updated.reshape(GROUP, rows // GROUP, width)
    for q in range(GROUP):
        block = hidden[q * (rows // GROUP) : (q + 1) * (rows // GROUP)]
        hidden_t_ref[first + q] = block.T.astype(BF16)


def first_layer_kernel(
    src, tiles_hbm, p0, p1, p2, p3, p4, w_in, w_self, w_agg, w_out,
    own_ref, agg_ref, hidden_t_ref, new_ref, tiles, window, sems,
):
    blocks, block_rows = tiles.shape[0], tiles.shape[2]
    groups = blocks // GROUP
    fetch_tiles(tiles_hbm, tiles, sems, groups)
    span = GROUP * block_rows
    for k, pack in enumerate((p0, p1, p2, p3, p4)):

        def encode(g, carry, pack=pack, k=k):
            operand = encode_operand(pack, pl.multiple_of(g * span, span), span)
            latents = jnp.tanh(dot_tn(operand, w_in[...])).astype(BF16)
            first = k * blocks + g * GROUP
            window[pl.ds(first, GROUP)] = latents.reshape(GROUP, block_rows, latents.shape[1])
            return carry

        lax.fori_loop(0, groups, encode, 0)
    window[PIECES * blocks] = jnp.zeros(window.shape[1:], BF16)
    own_ref[...] = window[pl.ds(0, blocks)]

    def step(g, carry):
        await_tiles(tiles_hbm, tiles, sems, g)
        forward_group(g, src, tiles, window, w_self, w_agg, w_out, agg_ref, hidden_t_ref, new_ref)
        return carry

    lax.fori_loop(0, groups, step, 0)


def next_layer_kernel(
    src, tiles_hbm, l0, l1, l2, l3, l4, w_self, w_agg, w_out,
    agg_ref, hidden_t_ref, new_ref, tiles, window, sems, piece_sems,
):
    blocks = tiles.shape[0]
    groups = blocks // GROUP
    copies = [
        pltpu.make_async_copy(piece, window.at[pl.ds(k * blocks, blocks)], piece_sems.at[k])
        for k, piece in enumerate((l0, l1, l2, l3, l4))
    ]
    for copy in copies:
        copy.start()
    fetch_tiles(tiles_hbm, tiles, sems, groups)
    window[PIECES * blocks] = jnp.zeros(window.shape[1:], BF16)
    for copy in copies:
        copy.wait()

    def step(g, carry):
        await_tiles(tiles_hbm, tiles, sems, g)
        forward_group(g, src, tiles, window, w_self, w_agg, w_out, agg_ref, hidden_t_ref, new_ref)
        return carry

    lax.fori_loop(0, groups, step, 0)


def list_kernel(row_bits, triplets, part_of, indices, negative_list, positive_list, counts):
    low = (1 << row_bits) - 1
    dummy = (PIECES * triplets) << row_bits

    def scan(k, carry):
        part = part_of[k]
        base = k * 2 * triplets

        def one(t, tops):
            top_n, top_p = tops
            code = (k * triplets + t) << row_bits
            positive = indices[base + t]
            negative = indices[base + triplets + t]
            negative_list[top_n] = code | (negative & low)
            positive_list[top_p] = code | (positive & low)
            top_n = top_n + ((negative >> row_bits) == part).astype(jnp.int32)
            top_p = top_p + ((positive >> row_bits) == part).astype(jnp.int32)
            return top_n, top_p

        return lax.fori_loop(0, triplets, one, carry, unroll=8)

    top_n, top_p = lax.fori_loop(0, PIECES, scan, (jnp.int32(0), jnp.int32(0)))
    longest = ((jnp.maximum(top_n, top_p) + 7) >> 3) << 3

    def pad(values):
        def put(i, carry):
            values[i] = jnp.int32(dummy)
            return carry

        return put

    lax.fori_loop(top_n, longest, pad(negative_list), 0)
    lax.fori_loop(top_p, longest, pad(positive_list), 0)
    counts[0] = longest >> 3


def gather_kernel(
    row_bits, negative_list, positive_list, counts, anchors, latents,
    d0, d1, d2, d3, d4, anchor_ref, wide, negative, positive, anchor_rows,
):
    low = (1 << row_bits) - 1
    triplets = anchor_ref.shape[0]
    blocks, block_rows, width = latents.shape
    wide[...] = latents[...].reshape(blocks * block_rows, width).astype(F32)
    negative[...] = jnp.zeros(negative.shape, F32)
    positive[...] = jnp.zeros(positive.shape, F32)

    def pick(i, carry):
        for u in range(8):
            code_n = negative_list[i * 8 + u]
            code_p = positive_list[i * 8 + u]
            negative[pl.ds(code_n >> row_bits, 1), :] = wide[pl.ds(code_n & low, 1), :]
            positive[pl.ds(code_p >> row_bits, 1), :] = wide[pl.ds(code_p & low, 1), :]
        return carry

    lax.fori_loop(0, counts[0], pick, 0)

    def pick_anchor(i, carry):
        for u in range(8):
            anchor_rows[pl.ds(i * 8 + u, 1), :] = wide[pl.ds(anchors[i * 8 + u], 1), :]
        return carry

    lax.fori_loop(0, triplets // 8, pick_anchor, 0)
    anchor_ref[...] = anchor_rows[...].astype(BF16)
    for k, out in enumerate((d0, d1, d2, d3, d4)):
        here = pl.ds(k * triplets, triplets)
        out[...] = (negative[here, :] - positive[here, :]).astype(BF16)


def score_kernel(own, far, near, other, anchors, loss_ref, weighted_ref, weighted_b_ref, anchor_grad_ref):
    triplets, width = anchors.shape
    inv_root = 1.0 / math.sqrt(width)
    scale = 1.0 / (loss_divisor * math.sqrt(width))
    chunk = 128
    loss = jnp.zeros((chunk, 1), F32)
    for c in range(triplets // chunk):
        here = pl.ds(c * chunk, chunk)
        gap = own[here, :].astype(F32) + far[here, :].astype(F32)
        gap = gap + near[here, :].astype(F32) + other[here, :].astype(F32)
        anchor = anchors[here, :].astype(F32)
        score = jnp.sum(anchor * gap, axis=1, keepdims=True) * inv_root
        loss = loss + jnp.maximum(score, 0.0) + jnp.log1p(jnp.exp(-jnp.abs(score)))
        coef = scale / (1.0 + jnp.exp(-score))
        weighted = coef * anchor
        weighted_ref[here, :] = weighted
        weighted_b_ref[here, :] = weighted.astype(BF16)
        anchor_grad_ref[here, :] = coef * gap
    loss_ref[...] = jnp.broadcast_to(jnp.sum(loss, axis=0, keepdims=True), loss_ref.shape)


def backward_group(g, src, tiles, gradient, hidden_t, latents, agg, w_self, w_agg, w_out,
                   grads, spread):
    slots = tiles.shape[1]
    first = pl.multiple_of(g * GROUP, GROUP)
    rows, width = tiles.shape[2], latents.shape[2]
    upstream = gradient.astype(BF16)
    hidden = jnp.concatenate([hidden_t[first + q] for q in range(GROUP)], axis=1)
    grads[2] += dot_nt(hidden, upstream)
    hidden_grad = dot_nn(w_out[...], upstream)
    act_grad = jnp.where(hidden > 0, hidden_grad, 0.0).astype(BF16)
    grads[0] += dot_nn(act_grad, latents[pl.ds(first, GROUP)].reshape(GROUP * rows, width))
    grads[1] += dot_nn(act_grad, agg[pl.ds(first, GROUP)].reshape(GROUP * rows, width))
    agg_grad = dot_nn(w_agg[...], act_grad).astype(BF16)
    direct = gradient + dot_nn(w_self[...], act_grad)
    for q in range(GROUP):
        b = g * GROUP + q
        spread[b] += direct[:, q * rows : (q + 1) * rows]
        right = jnp.concatenate([tiles[b, s] for s in range(slots)], axis=1)
        parts = dot_nn(agg_grad[:, q * rows : (q + 1) * rows], right)
        for s in range(slots):
            spread[src[b * slots + s]] += parts[:, s * rows : (s + 1) * rows]


def contrast_layer_kernel(
    row_bits, src, negative_list, positive_list, counts, anchors, tiles_hbm,
    weighted, e1, e2, e3, e4, anchor_grad, hidden_t, latents, agg, w_self, w_agg, w_out,
    own_ref, far_ref, near_ref, other_ref, passed_ref, grads_ref,
    tiles, spread, all_weighted, rows_a, rows_b, rows_c, rows_d, sems,
):
    low = (1 << row_bits) - 1
    blocks, block_rows = tiles.shape[0], tiles.shape[2]
    groups = blocks // GROUP
    triplets = weighted.shape[0]
    fetch_tiles(tiles_hbm, tiles, sems, groups)
    held = (rows_a, rows_b, rows_c, rows_d)
    for rows in held:
        rows[...] = jnp.zeros(rows.shape, F32)
    spread[...] = jnp.zeros(spread.shape, F32)
    grads_ref[...] = jnp.zeros(grads_ref.shape, F32)
    all_weighted[pl.ds(0, triplets), :] = weighted[...]
    for k, piece in enumerate((e1, e2, e3, e4)):
        all_weighted[pl.ds((k + 1) * triplets, triplets), :] = piece[...].astype(F32)
    all_weighted[pl.ds(PIECES * triplets, 8), :] = jnp.zeros((8, weighted.shape[1]), F32)

    def put_anchor(i, carry):
        for u in range(8):
            here = pl.ds(anchors[i * 8 + u], 1)
            held[u % 4][here, :] += anchor_grad[pl.ds(i * 8 + u, 1), :]
        return carry

    lax.fori_loop(0, triplets // 8, put_anchor, 0)

    def put(i, carry):
        for u in range(8):
            code_n = negative_list[i * 8 + u]
            code_p = positive_list[i * 8 + u]
            held[u % 2][pl.ds(code_n & low, 1), :] += all_weighted[pl.ds(code_n >> row_bits, 1), :]
            held[2 + u % 2][pl.ds(code_p & low, 1), :] -= all_weighted[pl.ds(code_p >> row_bits, 1), :]
        return carry

    lax.fori_loop(0, counts[0], put, 0)

    def step(g, carry):
        pieces = []
        for q in range(GROUP):
            here = pl.ds(pl.multiple_of((g * GROUP + q) * block_rows, block_rows), block_rows)
            block = (rows_a[here, :] + rows_b[here, :]) + (rows_c[here, :] + rows_d[here, :])
            pieces.append(block.T)
        await_tiles(tiles_hbm, tiles, sems, g)
        backward_group(g, src, tiles, jnp.concatenate(pieces, axis=1), hidden_t, latents, agg,
                       w_self, w_agg, w_out, grads_ref, spread)
        return carry

    lax.fori_loop(0, groups, step, 0)
    own_ref[...] = spread[pl.ds(0, blocks)]
    for k, out in enumerate((far_ref, near_ref, other_ref, passed_ref)):
        out[...] = spread[pl.ds((k + 1) * blocks, blocks)].astype(BF16)


def last_layer_kernel(
    src, tiles_hbm, own, r1, r2, r3, hidden_t, latents, agg, w_self, w_agg, w_out, w_in_t,
    p0, p1, p2, p3, p4,
    grads_ref, grad_in_ref, tiles, spread, sems,
):
    blocks, block_rows = tiles.shape[0], tiles.shape[2]
    groups = blocks // GROUP
    fetch_tiles(tiles_hbm, tiles, sems, groups)
    spread[...] = jnp.zeros(spread.shape, F32)
    grads_ref[...] = jnp.zeros(grads_ref.shape, F32)
    grad_in_ref[...] = jnp.zeros(grad_in_ref.shape, F32)

    def step(g, carry):
        pieces = []
        for q in range(GROUP):
            b = g * GROUP + q
            received = r1[b].astype(F32) + r2[b].astype(F32) + r3[b].astype(F32)
            pieces.append(own[b] + received)
        await_tiles(tiles_hbm, tiles, sems, g)
        backward_group(g, src, tiles, jnp.concatenate(pieces, axis=1), hidden_t, latents, agg,
                       w_self, w_agg, w_out, grads_ref, spread)
        return carry

    lax.fori_loop(0, groups, step, 0)
    span = GROUP * block_rows
    for k, pack in enumerate((p0, p1, p2, p3, p4)):

        def finish(g, carry, pack=pack, k=k):
            operand = encode_operand(pack, pl.multiple_of(g * span, span), span)
            squashed = jnp.tanh(dot_nn(w_in_t[...], operand))
            first = k * blocks + g * GROUP
            gradient = jnp.concatenate([spread[first + q] for q in range(GROUP)], axis=1)
            encoded_grad = (gradient * (1.0 - squashed * squashed)).astype(BF16)
            grad_in_ref[...] += dot_nt(operand, encoded_grad)
            return carry

        lax.fori_loop(0, groups, finish, 0)


def body(
    hit_feats, layer_ids, edge_tiles, src_blocks, live_slots,
    anchor_hits, positive_hits, negative_hits, w_enc, layer_table, w_self, w_agg, w_out,
):
    blocks, slots, block_rows = edge_tiles.shape[0], edge_tiles.shape[1], edge_tiles.shape[2]
    feats, width = w_enc.shape
    kinds = layer_table.shape[0]
    hits = blocks * block_rows
    triplets = anchor_hits.shape[0]
    layers = w_self.shape[0]
    row_bits = hits.bit_length() - 1
    assert hits == 1 << row_bits and feats < PACK_ROWS and kinds == PACK_ROWS and layers == 2
    assert 4 * triplets == hits and blocks % GROUP == 0
    groups = blocks // GROUP
    odd = lax.axis_index("phi") % 2

    positive_high, positive_low = positive_hits // 128, positive_hits % 128
    negative_high, negative_low = negative_hits // 128, negative_hits % 128
    codes = jnp.concatenate([positive_high, negative_high, positive_low, negative_low])
    pack = jnp.concatenate(
        [
            hit_feats,
            layer_ids.astype(BF16)[None, :],
            codes.astype(BF16)[None, :],
            jnp.zeros((PACK_ROWS - feats - 2, hits), BF16),
        ]
    )
    packs = gather_window(pack)
    w_in = jnp.concatenate([w_enc, jnp.zeros((PACK_ROWS - feats, width), BF16), layer_table])

    piece_of_part = jnp.where(odd == 0, jnp.array([2, 4, 0, 3, 1]), jnp.array([1, 3, 0, 4, 2]))
    part_back = jnp.where(odd == 0, jnp.array([2, 0, 4, 1, 3]), jnp.array([2, 4, 0, 3, 1]))
    part = src_blocks // blocks
    piece = jnp.zeros_like(part)
    for j in range(PIECES):
        piece = jnp.where(part == j, piece_of_part[j], piece)
    live = jnp.arange(slots, dtype=jnp.int32)[None, :] < live_slots[:, None]
    src = jnp.where(live, piece * blocks + src_blocks % blocks, PIECES * blocks).reshape(-1)
    src = src.astype(jnp.int32)

    block_shape = (blocks, block_rows, width)
    tile_scratch = pltpu.VMEM(edge_tiles.shape, BF16)
    group_sems = pltpu.SemaphoreType.DMA((groups,))
    window_scratch = pltpu.VMEM((PIECES * blocks + 1, block_rows, width), BF16)
    blocked = jax.ShapeDtypeStruct(block_shape, BF16)

    latents_0, agg_0, hidden_0, latents_1 = pl.pallas_call(
        first_layer_kernel,
        out_shape=(blocked,) * 4,
        in_specs=[smem(), in_hbm()] + [vmem()] * 9,
        out_specs=(vmem(),) * 4,
        scratch_shapes=[tile_scratch, window_scratch, group_sems],
        compiler_params=params(),
        name="first_layer",
    )(src, edge_tiles, *packs, w_in, w_self[0], w_agg[0], w_out[0])

    indices = jnp.stack([each[feats + 1] for each in packs]).astype(jnp.int32)
    indices = indices.reshape(PIECES, 2, 2 * triplets)
    indices = (indices[:, 0] * 128 + indices[:, 1]).reshape(-1)
    capacity = PIECES * triplets + 16
    negative_list, positive_list, counts = pl.pallas_call(
        lambda *refs: list_kernel(row_bits, triplets, *refs),
        out_shape=(
            jax.ShapeDtypeStruct((capacity,), jnp.int32),
            jax.ShapeDtypeStruct((capacity,), jnp.int32),
            jax.ShapeDtypeStruct((8,), jnp.int32),
        ),
        in_specs=[smem(), smem()],
        out_specs=(smem(),) * 3,
        compiler_params=params(),
        name="row_lists",
    )(part_back.astype(jnp.int32), indices)

    window_1 = gather_window(latents_1)
    agg_1, hidden_1, latents_2 = pl.pallas_call(
        next_layer_kernel,
        out_shape=(blocked,) * 3,
        in_specs=[smem(), in_hbm()] + [in_hbm()] * 5 + [vmem()] * 3,
        out_specs=(vmem(),) * 3,
        scratch_shapes=[
            tile_scratch, window_scratch, group_sems, pltpu.SemaphoreType.DMA((PIECES,)),
        ],
        compiler_params=params(),
        name="next_layer",
    )(src, edge_tiles, *window_1, w_self[1], w_agg[1], w_out[1])

    triplet_rows = jax.ShapeDtypeStruct((triplets, width), BF16)
    wide_rows = jax.ShapeDtypeStruct((triplets, width), F32)
    gathered = pl.pallas_call(
        lambda *refs: gather_kernel(row_bits, *refs),
        out_shape=(triplet_rows,) * 6,
        in_specs=[smem()] * 4 + [vmem()],
        out_specs=(vmem(),) * 6,
        scratch_shapes=[
            pltpu.VMEM((hits, width), F32),
            pltpu.VMEM((PIECES * triplets + 8, width), F32),
            pltpu.VMEM((PIECES * triplets + 8, width), F32),
            pltpu.VMEM((triplets, width), F32),
        ],
        compiler_params=params(),
        name="gather_rows",
    )(negative_list, positive_list, counts, anchor_hits, latents_2)
    gap_own, gap_far, gap_near, gap_other, gap_passed, anchor_rows = gathered
    gaps = return_pieces(gap_far, gap_near, gap_other, gap_passed)

    loss_part, weighted, weighted_b, anchor_grad = pl.pallas_call(
        score_kernel,
        out_shape=(jax.ShapeDtypeStruct((8, width), F32), wide_rows, triplet_rows, wide_rows),
        in_specs=[vmem()] * 5,
        out_specs=(vmem(),) * 4,
        compiler_params=params(),
        name="scores",
    )(gap_own, *gaps, anchor_rows)
    weighted_window = gather_window(weighted_b)

    wide_blocked = jax.ShapeDtypeStruct(block_shape, F32)
    spread_scratch = pltpu.VMEM((PIECES * blocks + 1, width, block_rows), F32)
    grads_shape = jax.ShapeDtypeStruct((3, width, width), F32)
    own_1, far_1, near_1, other_1, passed_1, grads_1 = pl.pallas_call(
        lambda *refs: contrast_layer_kernel(row_bits, *refs),
        out_shape=(wide_blocked,) + (blocked,) * 4 + (grads_shape,),
        in_specs=[smem()] * 5 + [in_hbm()] + [vmem()] * 12,
        out_specs=(vmem(),) * 6,
        scratch_shapes=[
            tile_scratch, spread_scratch, pltpu.VMEM((PIECES * triplets + 8, width), F32),
        ]
        + [pltpu.VMEM((hits, width), F32)] * 4
        + [group_sems],
        compiler_params=params(),
        name="contrast_layer",
    )(
        src, negative_list, positive_list, counts, anchor_hits, edge_tiles,
        weighted, *weighted_window[1:], anchor_grad, hidden_1, latents_1, agg_1,
        w_self[1], w_agg[1], w_out[1],
    )
    returned = return_pieces(far_1, near_1, other_1, passed_1)
    summed_1 = total_over_phi(jnp.concatenate([grads_1.reshape(3 * width, width), loss_part]))

    grads_0, grad_in = pl.pallas_call(
        last_layer_kernel,
        out_shape=(grads_shape, jax.ShapeDtypeStruct((2 * PACK_ROWS, width), F32)),
        in_specs=[smem(), in_hbm()] + [vmem()] * 16,
        out_specs=(vmem(),) * 2,
        scratch_shapes=[tile_scratch, spread_scratch, group_sems],
        compiler_params=params(),
        name="last_layer",
    )(
        src, edge_tiles, own_1, *returned, hidden_0, latents_0, agg_0,
        w_self[0], w_agg[0], w_out[0], w_in.T, *packs,
    )
    summed_0 = total_over_phi(jnp.concatenate([grads_0.reshape(3 * width, width), grad_in]))

    grads_1 = summed_1[: 3 * width].reshape(3, width, width)
    grads_0 = summed_0[: 3 * width].reshape(3, width, width)
    grad_in = summed_0[3 * width :]
    loss = (summed_1[3 * width, 0] / (triplets * lax.axis_size("phi"))).reshape(1)
    grad_self = jnp.stack([grads_0[0].T, grads_1[0].T])
    grad_agg = jnp.stack([grads_0[1].T, grads_1[1].T])
    grad_out = jnp.stack([grads_0[2], grads_1[2]])
    return (loss, grad_in[:feats], grad_in[PACK_ROWS:], grad_self, grad_agg, grad_out)


def solution(mesh):
    both = ("event", "phi")
    in_specs = (
        P(None, both), P(both), P(both, None, None, None), P(both, None), P(both),
        P(both), P(both), P(both), P(), P(), P(), P(), P(),
    )
    out_specs = (
        P("event"), P("event", None), P("event", None),
        P("event", None, None), P("event", None, None), P("event", None, None),
    )
    return jax.shard_map(body, mesh=mesh, in_specs=in_specs, out_specs=out_specs, check_vma=False)
```

```python
import math

import jax
import jax.numpy as jnp
from jax import lax
from jax.experimental import pallas as pl
from jax.experimental.pallas import tpu as pltpu
from jax.sharding import PartitionSpec as P

loss_divisor = 64.0
F32 = jnp.float32
BF16 = jnp.bfloat16
VMEM_LIMIT = 56 * 1024 * 1024
PACK_ROWS = 16
GROUP = 4

PIECES = 5


def vmem():
    return pl.BlockSpec(memory_space=pltpu.VMEM)


def smem():
    return pl.BlockSpec(memory_space=pltpu.SMEM)


def in_hbm():
    return pl.BlockSpec(memory_space=pl.ANY)


def params():
    return pltpu.CompilerParams(vmem_limit_bytes=VMEM_LIMIT)


def cost(microseconds):
    return pl.CostEstimate(flops=0, transcendentals=0, bytes_accessed=int(microseconds * 3.6e6))


def dot_nn(left, right):
    return lax.dot_general(left, right, (((1,), (0,)), ((), ())), preferred_element_type=F32)


def dot_tn(left, right):
    return lax.dot_general(left, right, (((0,), (0,)), ((), ())), preferred_element_type=F32)


def dot_nt(left, right):
    return lax.dot_general(left, right, (((1,), (1,)), ((), ())), preferred_element_type=F32)


def far_pairs(count):
    return [((p + 2) % count if p % 2 == 0 else (p - 2) % count, p) for p in range(count)]


def near_pairs(count):
    return [((p - 2) % count if p % 2 == 0 else (p + 2) % count, p) for p in range(count)]


def core_pairs(count):
    return [(p ^ 1, p) for p in range(count)]


def send(value, pairs):
    return lax.ppermute(value, "phi", pairs)


def turned(pairs):
    return [(target, source) for source, target in pairs]


def after(value, *earlier):
    return lax.optimization_barrier((value, *earlier))[0]


def gather_window(value, *meanwhile):
    count = lax.axis_size("phi")
    far = send(value, far_pairs(count))
    near = send(value, near_pairs(count))
    other = send(value, core_pairs(count))
    passed = send(after(far, *meanwhile) if meanwhile else far, core_pairs(count))
    return (value, far, near, other, passed)


def return_pieces(far, near, other, passed):
    count = lax.axis_size("phi")
    from_core = send(passed, core_pairs(count))
    from_near = send(near, turned(near_pairs(count)))
    from_other = send(other, core_pairs(count))
    joined = (far.astype(F32) + from_core.astype(F32)).astype(BF16)
    from_far = send(joined, turned(far_pairs(count)))
    return (from_far, from_near, from_other)


def total_over_phi(value):
    count = lax.axis_size("phi")
    if count & (count - 1) or count < 4:
        return lax.psum(value, "phi")
    half = value.shape[0] // 2
    odd = lax.axis_index("phi") % 2
    kept = lax.dynamic_slice_in_dim(value, odd * half, half, 0)
    given = lax.dynamic_slice_in_dim(value, (1 - odd) * half, half, 0)
    part = kept + send(given, core_pairs(count))
    step = 2
    while step < count:
        part = part + send(part, [(p, p ^ step) for p in range(count)])
        step *= 2
    back = send(part, core_pairs(count))
    return jnp.where(odd == 0, jnp.concatenate([part, back]), jnp.concatenate([back, part]))


def fetch_tiles(tiles_hbm, tiles, sems, groups):
    for g in range(groups):
        pltpu.make_async_copy(
            tiles_hbm.at[pl.ds(g * GROUP, GROUP)], tiles.at[pl.ds(g * GROUP, GROUP)], sems.at[g]
        ).start()


def await_tiles(tiles_hbm, tiles, sems, g):
    first = pl.multiple_of(g * GROUP, GROUP)
    pltpu.make_async_copy(
        tiles_hbm.at[pl.ds(first, GROUP)], tiles.at[pl.ds(first, GROUP)], sems.at[g]
    ).wait()


def encode_operand(pack_ref, start, width):
    rows = pack_ref[:, pl.ds(start, width)]
    ids = rows.astype(F32)[12:13, :]
    layers = lax.broadcasted_iota(jnp.int32, (PACK_ROWS, width), 0).astype(F32)
    onehot = (layers == ids).astype(BF16)
    return jnp.concatenate([rows, onehot], axis=0)


def forward_group(g, src, tiles, window, w_self, w_agg, w_out, agg_ref, hidden_t_ref, new_ref):
    slots = tiles.shape[1]
    sums = []
    for q in range(GROUP):
        b = g * GROUP + q
        left = jnp.concatenate([tiles[b, s] for s in range(slots)], axis=1)
        right = jnp.concatenate([window[src[b * slots + s]] for s in range(slots)], axis=0)
        sums.append(dot_nn(left, right))
    first = pl.multiple_of(g * GROUP, GROUP)
    agg = jnp.concatenate(sums, axis=0).astype(BF16)
    rows, width = agg.shape
    here = window[pl.ds(first, GROUP)].reshape(rows, width)
    activation = dot_nn(here, w_self[...]) + dot_nn(agg, w_agg[...])
    hidden = jnp.maximum(activation, 0.0)
    hidden_b = hidden.astype(BF16)
    updated = (here.astype(F32) + dot_nn(hidden_b, w_out[...])).astype(BF16)
    agg_ref[pl.ds(first, GROUP)] = agg.reshape(GROUP, rows // GROUP, width)
    new_ref[pl.ds(first, GROUP)] = updated.reshape(GROUP, rows // GROUP, width)
    for q in range(GROUP):
        block = hidden[q * (rows // GROUP) : (q + 1) * (rows // GROUP)]
        hidden_t_ref[first + q] = block.T.astype(BF16)


def first_layer_kernel(
    src, tiles_hbm, p0, p1, p2, p3, p4, w_in, w_self, w_agg, w_out,
    own_ref, agg_ref, hidden_t_ref, new_ref, tiles, window, sems,
):
    blocks, block_rows = tiles.shape[0], tiles.shape[2]
    groups = blocks // GROUP
    fetch_tiles(tiles_hbm, tiles, sems, groups)
    span = GROUP * block_rows
    for k, pack in enumerate((p0, p1, p2, p3, p4)):

        def encode(g, carry, pack=pack, k=k):
            operand = encode_operand(pack, pl.multiple_of(g * span, span), span)
            latents = jnp.tanh(dot_tn(operand, w_in[...])).astype(BF16)
            first = k * blocks + g * GROUP
            window[pl.ds(first, GROUP)] = latents.reshape(GROUP, block_rows, latents.shape[1])
            return carry

        lax.fori_loop(0, groups, encode, 0)
    window[PIECES * blocks] = jnp.zeros(window.shape[1:], BF16)
    own_ref[...] = window[pl.ds(0, blocks)]

    def step(g, carry):
        await_tiles(tiles_hbm, tiles, sems, g)
        forward_group(g, src, tiles, window, w_self, w_agg, w_out, agg_ref, hidden_t_ref, new_ref)
        return carry

    lax.fori_loop(0, groups, step, 0)


def next_layer_kernel(
    src, tiles_hbm, l0, l1, l2, l3, l4, w_self, w_agg, w_out,
    agg_ref, hidden_t_ref, new_ref, tiles, window, sems, piece_sems,
):
    blocks = tiles.shape[0]
    groups = blocks // GROUP
    copies = [
        pltpu.make_async_copy(piece, window.at[pl.ds(k * blocks, blocks)], piece_sems.at[k])
        for k, piece in enumerate((l0, l1, l2, l3, l4))
    ]
    for copy in copies:
        copy.start()
    fetch_tiles(tiles_hbm, tiles, sems, groups)
    window[PIECES * blocks] = jnp.zeros(window.shape[1:], BF16)
    for copy in copies:
        copy.wait()

    def step(g, carry):
        await_tiles(tiles_hbm, tiles, sems, g)
        forward_group(g, src, tiles, window, w_self, w_agg, w_out, agg_ref, hidden_t_ref, new_ref)
        return carry

    lax.fori_loop(0, groups, step, 0)


def list_kernel(row_bits, triplets, part_of, indices, negative_list, positive_list, counts):
    low = (1 << row_bits) - 1
    dummy = (PIECES * triplets) << row_bits

    def scan(k, carry):
        part = part_of[k]
        base = k * 2 * triplets

        def one(t, tops):
            top_n, top_p = tops
            code = (k * triplets + t) << row_bits
            positive = indices[base + t]
            negative = indices[base + triplets + t]
            negative_list[top_n] = code | (negative & low)
            positive_list[top_p] = code | (positive & low)
            top_n = top_n + ((negative >> row_bits) == part).astype(jnp.int32)
            top_p = top_p + ((positive >> row_bits) == part).astype(jnp.int32)
            return top_n, top_p

        return lax.fori_loop(0, triplets, one, carry, unroll=8)

    top_n, top_p = lax.fori_loop(0, PIECES, scan, (jnp.int32(0), jnp.int32(0)))
    longest = ((jnp.maximum(top_n, top_p) + 7) >> 3) << 3

    def pad(values):
        def put(i, carry):
            values[i] = jnp.int32(dummy)
            return carry

        return put

    lax.fori_loop(top_n, longest, pad(negative_list), 0)
    lax.fori_loop(top_p, longest, pad(positive_list), 0)
    counts[0] = longest >> 3


def gather_kernel(
    row_bits, negative_list, positive_list, counts, anchors, latents,
    d0, d1, d2, d3, d4, anchor_ref, wide, negative, positive, anchor_rows,
):
    low = (1 << row_bits) - 1
    triplets = anchor_ref.shape[0]
    blocks, block_rows, width = latents.shape
    wide[...] = latents[...].reshape(blocks * block_rows, width).astype(F32)
    negative[...] = jnp.zeros(negative.shape, F32)
    positive[...] = jnp.zeros(positive.shape, F32)

    def pick(i, carry):
        for u in range(8):
            code_n = negative_list[i * 8 + u]
            code_p = positive_list[i * 8 + u]
            negative[pl.ds(code_n >> row_bits, 1), :] = wide[pl.ds(code_n & low, 1), :]
            positive[pl.ds(code_p >> row_bits, 1), :] = wide[pl.ds(code_p & low, 1), :]
        return carry

    lax.fori_loop(0, counts[0], pick, 0)

    def pick_anchor(i, carry):
        for u in range(8):
            anchor_rows[pl.ds(i * 8 + u, 1), :] = wide[pl.ds(anchors[i * 8 + u], 1), :]
        return carry

    lax.fori_loop(0, triplets // 8, pick_anchor, 0)
    anchor_ref[...] = anchor_rows[...].astype(BF16)
    for k, out in enumerate((d0, d1, d2, d3, d4)):
        here = pl.ds(k * triplets, triplets)
        out[...] = (negative[here, :] - positive[here, :]).astype(BF16)


def score_kernel(own, far, near, other, anchors, loss_ref, weighted_ref, weighted_b_ref, anchor_grad_ref):
    triplets, width = anchors.shape
    inv_root = 1.0 / math.sqrt(width)
    scale = 1.0 / (loss_divisor * math.sqrt(width))
    chunk = 128
    loss = jnp.zeros((chunk, 1), F32)
    for c in range(triplets // chunk):
        here = pl.ds(c * chunk, chunk)
        gap = own[here, :].astype(F32) + far[here, :].astype(F32)
        gap = gap + near[here, :].astype(F32) + other[here, :].astype(F32)
        anchor = anchors[here, :].astype(F32)
        score = jnp.sum(anchor * gap, axis=1, keepdims=True) * inv_root
        loss = loss + jnp.maximum(score, 0.0) + jnp.log1p(jnp.exp(-jnp.abs(score)))
        coef = scale / (1.0 + jnp.exp(-score))
        weighted = coef * anchor
        weighted_ref[here, :] = weighted
        weighted_b_ref[here, :] = weighted.astype(BF16)
        anchor_grad_ref[here, :] = coef * gap
    loss_ref[...] = jnp.broadcast_to(jnp.sum(loss, axis=0, keepdims=True), loss_ref.shape)


def backward_group(g, src, tiles, gradient, hidden_t, latents, agg, w_self, w_agg, w_out,
                   grads, spread):
    slots = tiles.shape[1]
    first = pl.multiple_of(g * GROUP, GROUP)
    rows, width = tiles.shape[2], latents.shape[2]
    upstream = gradient.astype(BF16)
    hidden = jnp.concatenate([hidden_t[first + q] for q in range(GROUP)], axis=1)
    grads[2] += dot_nt(hidden, upstream)
    hidden_grad = dot_nn(w_out[...], upstream)
    act_grad = jnp.where(hidden > 0, hidden_grad, 0.0).astype(BF16)
    grads[0] += dot_nn(act_grad, latents[pl.ds(first, GROUP)].reshape(GROUP * rows, width))
    grads[1] += dot_nn(act_grad, agg[pl.ds(first, GROUP)].reshape(GROUP * rows, width))
    agg_grad = dot_nn(w_agg[...], act_grad).astype(BF16)
    direct = gradient + dot_nn(w_self[...], act_grad)
    for q in range(GROUP):
        b = g * GROUP + q
        spread[b] += direct[:, q * rows : (q + 1) * rows]
        right = jnp.concatenate([tiles[b, s] for s in range(slots)], axis=1)
        parts = dot_nn(agg_grad[:, q * rows : (q + 1) * rows], right)
        for s in range(slots):
            spread[src[b * slots + s]] += parts[:, s * rows : (s + 1) * rows]


def contrast_layer_kernel(
    row_bits, src, negative_list, positive_list, counts, anchors, tiles_hbm,
    weighted, e1, e2, e3, e4, anchor_grad, hidden_t, latents, agg, w_self, w_agg, w_out,
    own_ref, far_ref, near_ref, other_ref, passed_ref, grads_ref,
    tiles, spread, all_weighted, rows_a, rows_b, rows_c, rows_d, sems,
):
    low = (1 << row_bits) - 1
    blocks, block_rows = tiles.shape[0], tiles.shape[2]
    groups = blocks // GROUP
    triplets = weighted.shape[0]
    fetch_tiles(tiles_hbm, tiles, sems, groups)
    held = (rows_a, rows_b, rows_c, rows_d)
    for rows in held:
        rows[...] = jnp.zeros(rows.shape, F32)
    spread[...] = jnp.zeros(spread.shape, F32)
    grads_ref[...] = jnp.zeros(grads_ref.shape, F32)
    all_weighted[pl.ds(0, triplets), :] = weighted[...]
    for k, piece in enumerate((e1, e2, e3, e4)):
        all_weighted[pl.ds((k + 1) * triplets, triplets), :] = piece[...].astype(F32)
    all_weighted[pl.ds(PIECES * triplets, 8), :] = jnp.zeros((8, weighted.shape[1]), F32)

    def put_anchor(i, carry):
        for u in range(8):
            here = pl.ds(anchors[i * 8 + u], 1)
            held[u % 4][here, :] += anchor_grad[pl.ds(i * 8 + u, 1), :]
        return carry

    lax.fori_loop(0, triplets // 8, put_anchor, 0)

    def put(i, carry):
        for u in range(8):
            code_n = negative_list[i * 8 + u]
            code_p = positive_list[i * 8 + u]
            held[u % 2][pl.ds(code_n & low, 1), :] += all_weighted[pl.ds(code_n >> row_bits, 1), :]
            held[2 + u % 2][pl.ds(code_p & low, 1), :] -= all_weighted[pl.ds(code_p >> row_bits, 1), :]
        return carry

    lax.fori_loop(0, counts[0], put, 0)

    def step(g, carry):
        pieces = []
        for q in range(GROUP):
            here = pl.ds(pl.multiple_of((g * GROUP + q) * block_rows, block_rows), block_rows)
            block = (rows_a[here, :] + rows_b[here, :]) + (rows_c[here, :] + rows_d[here, :])
            pieces.append(block.T)
        await_tiles(tiles_hbm, tiles, sems, g)
        backward_group(g, src, tiles, jnp.concatenate(pieces, axis=1), hidden_t, latents, agg,
                       w_self, w_agg, w_out, grads_ref, spread)
        return carry

    lax.fori_loop(0, groups, step, 0)
    own_ref[...] = spread[pl.ds(0, blocks)]
    for k, out in enumerate((far_ref, near_ref, other_ref, passed_ref)):
        out[...] = spread[pl.ds((k + 1) * blocks, blocks)].astype(BF16)


def last_layer_kernel(
    src, tiles_hbm, own, r1, r2, r3, hidden_t, latents, agg, w_self, w_agg, w_out, w_in_t,
    p0, p1, p2, p3, p4,
    grads_ref, grad_in_ref, tiles, spread, sems,
):
    blocks, block_rows = tiles.shape[0], tiles.shape[2]
    groups = blocks // GROUP
    fetch_tiles(tiles_hbm, tiles, sems, groups)
    spread[...] = jnp.zeros(spread.shape, F32)
    grads_ref[...] = jnp.zeros(grads_ref.shape, F32)
    grad_in_ref[...] = jnp.zeros(grad_in_ref.shape, F32)

    def step(g, carry):
        pieces = []
        for q in range(GROUP):
            b = g * GROUP + q
            received = r1[b].astype(F32) + r2[b].astype(F32) + r3[b].astype(F32)
            pieces.append(own[b] + received)
        await_tiles(tiles_hbm, tiles, sems, g)
        backward_group(g, src, tiles, jnp.concatenate(pieces, axis=1), hidden_t, latents, agg,
                       w_self, w_agg, w_out, grads_ref, spread)
        return carry

    lax.fori_loop(0, groups, step, 0)
    span = GROUP * block_rows
    for k, pack in enumerate((p0, p1, p2, p3, p4)):

        def finish(g, carry, pack=pack, k=k):
            operand = encode_operand(pack, pl.multiple_of(g * span, span), span)
            squashed = jnp.tanh(dot_nn(w_in_t[...], operand))
            first = k * blocks + g * GROUP
            gradient = jnp.concatenate([spread[first + q] for q in range(GROUP)], axis=1)
            encoded_grad = (gradient * (1.0 - squashed * squashed)).astype(BF16)
            grad_in_ref[...] += dot_nt(operand, encoded_grad)
            return carry

        lax.fori_loop(0, groups, finish, 0)


def body(
    hit_feats, layer_ids, edge_tiles, src_blocks, live_slots,
    anchor_hits, positive_hits, negative_hits, w_enc, layer_table, w_self, w_agg, w_out,
):
    blocks, slots, block_rows = edge_tiles.shape[0], edge_tiles.shape[1], edge_tiles.shape[2]
    feats, width = w_enc.shape
    kinds = layer_table.shape[0]
    hits = blocks * block_rows
    triplets = anchor_hits.shape[0]
    layers = w_self.shape[0]
    row_bits = hits.bit_length() - 1
    assert hits == 1 << row_bits and feats < PACK_ROWS and kinds == PACK_ROWS and layers == 2
    assert 4 * triplets == hits and blocks % GROUP == 0
    groups = blocks // GROUP
    odd = lax.axis_index("phi") % 2

    positive_high, positive_low = positive_hits // 128, positive_hits % 128
    negative_high, negative_low = negative_hits // 128, negative_hits % 128
    codes = jnp.concatenate([positive_high, negative_high, positive_low, negative_low])
    pack = jnp.concatenate(
        [
            hit_feats,
            layer_ids.astype(BF16)[None, :],
            codes.astype(BF16)[None, :],
            jnp.zeros((PACK_ROWS - feats - 2, hits), BF16),
        ]
    )
    packs = gather_window(pack)
    w_in = jnp.concatenate([w_enc, jnp.zeros((PACK_ROWS - feats, width), BF16), layer_table])

    piece_of_part = jnp.where(odd == 0, jnp.array([2, 4, 0, 3, 1]), jnp.array([1, 3, 0, 4, 2]))
    part_back = jnp.where(odd == 0, jnp.array([2, 0, 4, 1, 3]), jnp.array([2, 4, 0, 3, 1]))
    part = src_blocks // blocks
    piece = jnp.zeros_like(part)
    for j in range(PIECES):
        piece = jnp.where(part == j, piece_of_part[j], piece)
    live = jnp.arange(slots, dtype=jnp.int32)[None, :] < live_slots[:, None]
    src = jnp.where(live, piece * blocks + src_blocks % blocks, PIECES * blocks).reshape(-1)
    src = src.astype(jnp.int32)

    block_shape = (blocks, block_rows, width)
    tile_scratch = pltpu.VMEM(edge_tiles.shape, BF16)
    group_sems = pltpu.SemaphoreType.DMA((groups,))
    window_scratch = pltpu.VMEM((PIECES * blocks + 1, block_rows, width), BF16)
    blocked = jax.ShapeDtypeStruct(block_shape, BF16)

    latents_0, agg_0, hidden_0, latents_1 = pl.pallas_call(
        first_layer_kernel,
        out_shape=(blocked,) * 4,
        in_specs=[smem(), in_hbm()] + [vmem()] * 9,
        out_specs=(vmem(),) * 4,
        scratch_shapes=[tile_scratch, window_scratch, group_sems],
        compiler_params=params(),
        name="first_layer",
        cost_estimate=cost(18),
    )(src, edge_tiles, *packs, w_in, w_self[0], w_agg[0], w_out[0])

    indices = jnp.stack([each[feats + 1] for each in packs]).astype(jnp.int32)
    indices = indices.reshape(PIECES, 2, 2 * triplets)
    indices = (indices[:, 0] * 128 + indices[:, 1]).reshape(-1)
    capacity = PIECES * triplets + 16
    negative_list, positive_list, counts = pl.pallas_call(
        lambda *refs: list_kernel(row_bits, triplets, *refs),
        out_shape=(
            jax.ShapeDtypeStruct((capacity,), jnp.int32),
            jax.ShapeDtypeStruct((capacity,), jnp.int32),
            jax.ShapeDtypeStruct((8,), jnp.int32),
        ),
        in_specs=[smem(), smem()],
        out_specs=(smem(),) * 3,
        compiler_params=params(),
        name="row_lists",
        cost_estimate=cost(39),
    )(part_back.astype(jnp.int32), indices)

    window_1 = gather_window(latents_1, counts)
    agg_1, hidden_1, latents_2 = pl.pallas_call(
        next_layer_kernel,
        out_shape=(blocked,) * 3,
        in_specs=[smem(), in_hbm()] + [in_hbm()] * 5 + [vmem()] * 3,
        out_specs=(vmem(),) * 3,
        scratch_shapes=[
            tile_scratch, window_scratch, group_sems, pltpu.SemaphoreType.DMA((PIECES,)),
        ],
        compiler_params=params(),
        name="next_layer",
        cost_estimate=cost(13),
    )(src, edge_tiles, *window_1, w_self[1], w_agg[1], w_out[1])

    triplet_rows = jax.ShapeDtypeStruct((triplets, width), BF16)
    wide_rows = jax.ShapeDtypeStruct((triplets, width), F32)
    gathered = pl.pallas_call(
        lambda *refs: gather_kernel(row_bits, *refs),
        out_shape=(triplet_rows,) * 6,
        in_specs=[smem()] * 4 + [vmem()],
        out_specs=(vmem(),) * 6,
        scratch_shapes=[
            pltpu.VMEM((hits, width), F32),
            pltpu.VMEM((PIECES * triplets + 8, width), F32),
            pltpu.VMEM((PIECES * triplets + 8, width), F32),
            pltpu.VMEM((triplets, width), F32),
        ],
        compiler_params=params(),
        name="gather_rows",
        cost_estimate=cost(8),
    )(negative_list, positive_list, counts, anchor_hits, latents_2)
    gap_own, gap_far, gap_near, gap_other, gap_passed, anchor_rows = gathered
    gaps = return_pieces(gap_far, gap_near, gap_other, gap_passed)

    loss_part, weighted, weighted_b, anchor_grad = pl.pallas_call(
        score_kernel,
        out_shape=(jax.ShapeDtypeStruct((8, width), F32), wide_rows, triplet_rows, wide_rows),
        in_specs=[vmem()] * 5,
        out_specs=(vmem(),) * 4,
        compiler_params=params(),
        name="scores",
        cost_estimate=cost(3),
    )(gap_own, *gaps, anchor_rows)
    weighted_window = gather_window(weighted_b)

    wide_blocked = jax.ShapeDtypeStruct(block_shape, F32)
    spread_scratch = pltpu.VMEM((PIECES * blocks + 1, width, block_rows), F32)
    grads_shape = jax.ShapeDtypeStruct((3, width, width), F32)
    own_1, far_1, near_1, other_1, passed_1, grads_1 = pl.pallas_call(
        lambda *refs: contrast_layer_kernel(row_bits, *refs),
        out_shape=(wide_blocked,) + (blocked,) * 4 + (grads_shape,),
        in_specs=[smem()] * 5 + [in_hbm()] + [vmem()] * 12,
        out_specs=(vmem(),) * 6,
        scratch_shapes=[
            tile_scratch, spread_scratch, pltpu.VMEM((PIECES * triplets + 8, width), F32),
        ]
        + [pltpu.VMEM((hits, width), F32)] * 4
        + [group_sems],
        compiler_params=params(),
        name="contrast_layer",
        cost_estimate=cost(20),
    )(
        src, negative_list, positive_list, counts, anchor_hits, edge_tiles,
        weighted, *weighted_window[1:], anchor_grad, hidden_1, latents_1, agg_1,
        w_self[1], w_agg[1], w_out[1],
    )
    returned = return_pieces(far_1, near_1, other_1, passed_1)
    summed_1 = total_over_phi(jnp.concatenate([grads_1.reshape(3 * width, width), loss_part]))

    grads_0, grad_in = pl.pallas_call(
        last_layer_kernel,
        out_shape=(grads_shape, jax.ShapeDtypeStruct((2 * PACK_ROWS, width), F32)),
        in_specs=[smem(), in_hbm()] + [vmem()] * 16,
        out_specs=(vmem(),) * 2,
        scratch_shapes=[tile_scratch, spread_scratch, group_sems],
        compiler_params=params(),
        name="last_layer",
        cost_estimate=cost(25),
    )(
        src, edge_tiles, own_1, *returned, hidden_0, latents_0, agg_0,
        w_self[0], w_agg[0], w_out[0], w_in.T, *packs,
    )
    summed_0 = total_over_phi(jnp.concatenate([grads_0.reshape(3 * width, width), grad_in]))

    grads_1 = summed_1[: 3 * width].reshape(3, width, width)
    grads_0 = summed_0[: 3 * width].reshape(3, width, width)
    grad_in = summed_0[3 * width :]
    loss = (summed_1[3 * width, 0] / (triplets * lax.axis_size("phi"))).reshape(1)
    grad_self = jnp.stack([grads_0[0].T, grads_1[0].T])
    grad_agg = jnp.stack([grads_0[1].T, grads_1[1].T])
    grad_out = jnp.stack([grads_0[2], grads_1[2]])
    return (loss, grad_in[:feats], grad_in[PACK_ROWS:], grad_self, grad_agg, grad_out)


def solution(mesh):
    both = ("event", "phi")
    in_specs = (
        P(None, both), P(both), P(both, None, None, None), P(both, None), P(both),
        P(both), P(both), P(both), P(), P(), P(), P(), P(),
    )
    out_specs = (
        P("event"), P("event", None), P("event", None),
        P("event", None, None), P("event", None, None), P("event", None, None),
    )
    return jax.shard_map(body, mesh=mesh, in_specs=in_specs, out_specs=out_specs, check_vma=False)
```

```python
import math

import jax
import jax.numpy as jnp
from jax import lax
from jax.experimental import pallas as pl
from jax.experimental.pallas import tpu as pltpu
from jax.sharding import PartitionSpec as P

loss_divisor = 64.0
F32 = jnp.float32
BF16 = jnp.bfloat16
VMEM_LIMIT = 56 * 1024 * 1024
PACK_ROWS = 16
GROUP = 8

PIECES = 5


def vmem():
    return pl.BlockSpec(memory_space=pltpu.VMEM)


def smem():
    return pl.BlockSpec(memory_space=pltpu.SMEM)


def in_hbm():
    return pl.BlockSpec(memory_space=pl.ANY)


def params():
    return pltpu.CompilerParams(vmem_limit_bytes=VMEM_LIMIT)


def cost(microseconds):
    return pl.CostEstimate(flops=0, transcendentals=0, bytes_accessed=int(microseconds * 3.6e6))


def dot_nn(left, right):
    return lax.dot_general(left, right, (((1,), (0,)), ((), ())), preferred_element_type=F32)


def dot_tn(left, right):
    return lax.dot_general(left, right, (((0,), (0,)), ((), ())), preferred_element_type=F32)


def dot_nt(left, right):
    return lax.dot_general(left, right, (((1,), (1,)), ((), ())), preferred_element_type=F32)


def second(p):
    return (p >> 1) & 1


def pair_links(count):
    return [(p, p ^ 2) for p in range(count)]


def cross_links(count):
    return [(p, (p + (2 if second(p) else -2)) % count) for p in range(count)]


def relay_links(count):
    return [(p, (p + (-4 if second(p) else 4)) % count) for p in range(count)]


def core_links(count):
    return [(p, p ^ 1) for p in range(count)]


def extra_links(count, from_pair):
    return [(p ^ 1, p) for p in range(count) if ((p & 1) != second(p)) == from_pair]


def turned(links):
    return [(target, source) for source, target in links]


def place_table():
    rows = []
    for kind in range(4):
        odd, on_second = kind & 1, kind >> 1
        pair, core = (-2 if on_second else 2), (-1 if odd else 1)
        offsets = [0, pair, -pair, core, -core]
        rows.append(
            [odd, on_second]
            + [offsets.index(part - 2) for part in range(PIECES)]
            + [2 - offset for offset in offsets]
            + [0] * 4
        )
    return jnp.array(rows, jnp.int32)


def send(value, links):
    return lax.ppermute(value, "phi", links)


def after(value, *earlier):
    return lax.optimization_barrier((value, *earlier))[0]


def gather_small(value, meanwhile=None):
    count = lax.axis_size("phi")
    pair = send(value, pair_links(count))
    cross = send(value, cross_links(count))
    other = send(value, core_links(count))
    if meanwhile is not None:
        pair = after(pair, meanwhile)
    extra_p = send(pair, extra_links(count, True))
    extra_c = send(cross, extra_links(count, False))
    return (value, pair, cross, other, extra_p, extra_c)


def join_extra(pair, cross, received, sends_pair):
    to_pair = jnp.where(sends_pair, received, jnp.zeros_like(received))
    to_cross = jnp.where(sends_pair, jnp.zeros_like(received), received)
    pair = (pair.astype(F32) + to_pair.astype(F32)).astype(BF16)
    cross = (cross.astype(F32) + to_cross.astype(F32)).astype(BF16)
    return pair, cross


def return_small(pair, cross, other, extra, sends_pair):
    count = lax.axis_size("phi")
    received = send(extra, core_links(count))
    from_other = send(other, core_links(count))
    pair, cross = join_extra(pair, cross, received, sends_pair)
    from_pair = send(pair, pair_links(count))
    from_cross = send(cross, turned(cross_links(count)))
    return (from_pair, from_cross, from_other), (pair, cross)


def first_sums(kept, given):
    count = lax.axis_size("phi")
    part = kept + send(given, core_links(count))
    if count & (count - 1) == 0:
        part = part + send(part, pair_links(count))
    return part


def last_sums(part):
    count = lax.axis_size("phi")
    if count & (count - 1):
        moved = part
        for _ in range(count // 2 - 1):
            moved = send(moved, [(p, (p + 2) % count) for p in range(count)])
            part = part + moved
    else:
        step = 4
        while step < count:
            part = part + send(part, [(p, p ^ step) for p in range(count)])
            step *= 2
    return part, send(part, core_links(count))


def fetch_tiles(tiles_hbm, tiles, sems, groups):
    for g in range(groups):
        pltpu.make_async_copy(
            tiles_hbm.at[pl.ds(g * GROUP, GROUP)], tiles.at[pl.ds(g * GROUP, GROUP)], sems.at[g]
        ).start()


def await_tiles(tiles_hbm, tiles, sems, g):
    first = pl.multiple_of(g * GROUP, GROUP)
    pltpu.make_async_copy(
        tiles_hbm.at[pl.ds(first, GROUP)], tiles.at[pl.ds(first, GROUP)], sems.at[g]
    ).wait()


def encode_operand(*pack_refs):
    rows = sum(pack_ref[...] for pack_ref in pack_refs)
    ids = rows.astype(F32)[12:13, :]
    layers = lax.broadcasted_iota(jnp.int32, rows.shape, 0).astype(F32)
    onehot = (layers == ids).astype(BF16)
    return jnp.concatenate([rows, onehot], axis=0)


def block_of(place, src, live, b, s, blocks):
    bits = blocks.bit_length() - 1
    named = src[b, s]
    block = (place[2 + (named >> bits)] << bits) + (named & (blocks - 1))
    return jnp.where(s < live[b], block, PIECES * blocks)


def forward_group(layer, g, place, src, live, tiles, window, w_self, w_agg, w_out, agg_ref, hidden_t_ref, new_ref):
    blocks, slots = tiles.shape[0], tiles.shape[1]
    sums = []
    for q in range(GROUP):
        b = g * GROUP + q
        left = jnp.concatenate([tiles[b, s] for s in range(slots)], axis=1)
        right = [window[block_of(place, src, live, b, s, blocks)] for s in range(slots)]
        sums.append(dot_nn(left, jnp.concatenate(right, axis=0)))
    first = pl.multiple_of(g * GROUP, GROUP)
    agg = jnp.concatenate(sums, axis=0).astype(BF16)
    rows, width = agg.shape
    here = window[pl.ds(first, GROUP)].reshape(rows, width)
    activation = dot_nn(here, w_self[layer]) + dot_nn(agg, w_agg[layer])
    hidden = jnp.maximum(activation, 0.0)
    hidden_b = hidden.astype(BF16)
    updated = (here.astype(F32) + dot_nn(hidden_b, w_out[layer])).astype(BF16)
    agg_ref[pl.ds(first, GROUP)] = agg.reshape(GROUP, rows // GROUP, width)
    new_ref[pl.ds(first, GROUP)] = updated.reshape(GROUP, rows // GROUP, width)
    for q in range(GROUP):
        block = hidden[q * (rows // GROUP) : (q + 1) * (rows // GROUP)]
        hidden_t_ref[first + q] = block.T.astype(BF16)


def input_weights(w_enc, layer_table):
    feats, width = w_enc.shape
    gap = jnp.zeros((PACK_ROWS - feats, width), F32)
    return jnp.concatenate([w_enc[...].astype(F32), gap, layer_table[...].astype(F32)], axis=0).astype(BF16)


def first_layer_kernel(
    place, src, live, tiles_hbm, p0, p1, p2, p3, p4, p5, w_enc, layer_table, w_self, w_agg, w_out,
    own_ref, agg_ref, hidden_t_ref, new_ref, new_a_ref, new_b_ref, tiles, window, sems,
):
    blocks, block_rows = tiles.shape[0], tiles.shape[2]
    groups = blocks // GROUP
    fetch_tiles(tiles_hbm, tiles, sems, groups)
    w_in = input_weights(w_enc, layer_table)
    for k, pack in enumerate(((p0,), (p1,), (p2,), (p3,), (p4, p5))):
        latents = jnp.tanh(dot_tn(encode_operand(*pack), w_in)).astype(BF16)
        window[pl.ds(k * blocks, blocks)] = latents.reshape(blocks, block_rows, latents.shape[1])
    window[PIECES * blocks] = jnp.zeros(window.shape[1:], BF16)
    own_ref[...] = window[pl.ds(0, blocks)]

    def step(g, carry):
        await_tiles(tiles_hbm, tiles, sems, g)
        forward_group(0, g, place, src, live, tiles, window, w_self, w_agg, w_out, agg_ref, hidden_t_ref, new_ref)
        return carry

    lax.fori_loop(0, groups, step, 0)
    cut = new_a_ref.shape[0]
    new_a_ref[...] = new_ref[pl.ds(0, cut)]
    new_b_ref[...] = new_ref[pl.ds(cut, blocks - cut)]


def next_layer_kernel(
    place, src, live, tiles_hbm, own_a, own_b, pair_a, pair_b, cross_a, cross_b, other_a, other_b,
    extra_pa, extra_pb, extra_ca, extra_cb, w_self, w_agg, w_out,
    agg_ref, hidden_t_ref, new_ref, tiles, window, sems, piece_sems,
):
    blocks, cut = tiles.shape[0], own_a.shape[0]
    groups = blocks // GROUP

    def copies(pieces, first):
        for k, (head, tail) in enumerate(pieces):
            start = (first + k) * blocks
            yield pltpu.make_async_copy(
                head, window.at[pl.ds(start, cut)], piece_sems.at[2 * (first + k)]
            )
            yield pltpu.make_async_copy(
                tail, window.at[pl.ds(start + cut, blocks - cut)], piece_sems.at[2 * (first + k) + 1]
            )

    plain = list(copies([(own_a, own_b), (pair_a, pair_b), (cross_a, cross_b), (other_a, other_b)], 0))
    for copy in plain:
        copy.start()

    def extra_is_pair(do):
        @pl.when(place[0] != place[1])
        def _():
            for copy in copies([(extra_pa, extra_pb)], 4):
                do(copy)

        @pl.when(place[0] == place[1])
        def _():
            for copy in copies([(extra_ca, extra_cb)], 4):
                do(copy)

    extra_is_pair(lambda copy: copy.start())
    fetch_tiles(tiles_hbm, tiles, sems, groups)
    window[PIECES * blocks] = jnp.zeros(window.shape[1:], BF16)
    for copy in plain:
        copy.wait()
    extra_is_pair(lambda copy: copy.wait())

    def step(g, carry):
        await_tiles(tiles_hbm, tiles, sems, g)
        forward_group(1, g, place, src, live, tiles, window, w_self, w_agg, w_out, agg_ref, hidden_t_ref, new_ref)
        return carry

    lax.fori_loop(0, groups, step, 0)


def pair_of_lists(lists, counts, k, triplets):
    longest = jnp.maximum(counts[2 * k], counts[2 * k + 1])
    return 2 * k * triplets, (2 * k + 1) * triplets, (longest + 7) >> 3


def gather_kernel(row_bits, lists, counts, latents, d0, d1, d2, d3, d4, wide, negative, positive):
    low = (1 << row_bits) - 1
    triplets = d0.shape[0]
    blocks, block_rows, width = latents.shape
    wide[...] = latents[...].reshape(blocks * block_rows, width).astype(F32)
    negative[...] = jnp.zeros(negative.shape, F32)
    positive[...] = jnp.zeros(positive.shape, F32)
    for k, out in enumerate((d0, d1, d2, d3, d4)):
        first_p, first_n, eights = pair_of_lists(lists, counts, k, triplets)

        def pick(i, carry, first_p=first_p, first_n=first_n):
            for u in range(8):
                code_n = lists[first_n + i * 8 + u]
                code_p = lists[first_p + i * 8 + u]
                negative[pl.ds(code_n >> row_bits, 1), :] = wide[pl.ds(code_n & low, 1), :]
                positive[pl.ds(code_p >> row_bits, 1), :] = wide[pl.ds(code_p & low, 1), :]
            return carry

        lax.fori_loop(0, eights, pick, 0)
        here = pl.ds(k * triplets, triplets)
        out[...] = (negative[here, :] - positive[here, :]).astype(BF16)


def anchor_kernel(anchors, latents, anchor_ref, wide):
    blocks, block_rows, width = latents.shape
    wide[...] = latents[...].reshape(blocks * block_rows, width).astype(F32)

    def pick(i, carry):
        for u in range(8):
            anchor_ref[pl.ds(i * 8 + u, 1), :] = wide[pl.ds(anchors[i * 8 + u], 1), :]
        return carry

    lax.fori_loop(0, anchor_ref.shape[0] // 8, pick, 0)


def own_rows_kernel(row_bits, lists, counts, anchors, weighted, anchor_grad, rows_ref, rows_b, rows_c, rows_d):
    low = (1 << row_bits) - 1
    triplets = anchor_grad.shape[0]
    held = (rows_ref, rows_b, rows_c, rows_d)
    for rows in held:
        rows[...] = jnp.zeros(rows.shape, F32)

    def put_anchor(i, carry):
        for u in range(8):
            here = pl.ds(anchors[i * 8 + u], 1)
            held[u % 4][here, :] += anchor_grad[pl.ds(i * 8 + u, 1), :]
        return carry

    lax.fori_loop(0, triplets // 8, put_anchor, 0)
    first_p, first_n, eights = pair_of_lists(lists, counts, 0, triplets)

    def put(i, carry):
        for u in range(8):
            code_n = lists[first_n + i * 8 + u]
            code_p = lists[first_p + i * 8 + u]
            from_n = pl.ds(jnp.minimum(code_n >> row_bits, triplets), 1)
            from_p = pl.ds(jnp.minimum(code_p >> row_bits, triplets), 1)
            held[u % 2][pl.ds(code_n & low, 1), :] += weighted[from_n, :]
            held[2 + u % 2][pl.ds(code_p & low, 1), :] -= weighted[from_p, :]
        return carry

    lax.fori_loop(0, eights, put, 0)
    rows_ref[...] = (rows_ref[...] + rows_b[...]) + (rows_c[...] + rows_d[...])


def score_kernel(own, pair, cross, other, anchors, loss_ref, weighted_ref, weighted_b_ref, anchor_grad_ref):
    triplets, width = anchors.shape
    inv_root = 1.0 / math.sqrt(width)
    scale = 1.0 / (loss_divisor * math.sqrt(width))
    chunk = 128
    loss = jnp.zeros((chunk, 1), F32)
    weighted_ref[pl.ds(triplets, 8), :] = jnp.zeros((8, width), F32)
    for c in range(triplets // chunk):
        here = pl.ds(c * chunk, chunk)
        gap = own[here, :].astype(F32) + pair[here, :].astype(F32)
        gap = gap + cross[here, :].astype(F32) + other[here, :].astype(F32)
        anchor = anchors[here, :]
        score = jnp.sum(anchor * gap, axis=1, keepdims=True) * inv_root
        loss = loss + jnp.maximum(score, 0.0) + jnp.log1p(jnp.exp(-jnp.abs(score)))
        coef = scale / (1.0 + jnp.exp(-score))
        weighted = coef * anchor
        weighted_ref[here, :] = weighted
        weighted_b_ref[here, :] = weighted.astype(BF16)
        anchor_grad_ref[here, :] = coef * gap
    loss_ref[...] = jnp.broadcast_to(jnp.sum(loss, axis=0, keepdims=True), loss_ref.shape)


def backward_group(layer, g, place, src, live, tiles, gradient, hidden_t, latents, agg, w_self, w_agg, w_out, grads, spread):
    blocks, slots = tiles.shape[0], tiles.shape[1]
    first = pl.multiple_of(g * GROUP, GROUP)
    rows, width = tiles.shape[2], latents.shape[2]
    upstream = gradient.astype(BF16)
    hidden = jnp.concatenate([hidden_t[first + q] for q in range(GROUP)], axis=1)
    grads[2] += dot_nt(hidden, upstream)
    hidden_grad = dot_nn(w_out[layer], upstream)
    act_grad = jnp.where(hidden > 0, hidden_grad, 0.0).astype(BF16)
    grads[0] += dot_nn(act_grad, latents[pl.ds(first, GROUP)].reshape(GROUP * rows, width))
    grads[1] += dot_nn(act_grad, agg[pl.ds(first, GROUP)].reshape(GROUP * rows, width))
    agg_grad = dot_nn(w_agg[layer], act_grad).astype(BF16)
    direct = gradient + dot_nn(w_self[layer], act_grad)
    for q in range(GROUP):
        b = g * GROUP + q
        spread[b] += direct[:, q * rows : (q + 1) * rows]
        right = jnp.concatenate([tiles[b, s] for s in range(slots)], axis=1)
        parts = dot_nn(agg_grad[:, q * rows : (q + 1) * rows], right)
        for s in range(slots):
            spread[block_of(place, src, live, b, s, blocks)] += parts[:, s * rows : (s + 1) * rows]


def put_halves(place, whole, kept_ref, given_ref):
    half = kept_ref.shape[0]
    kept_ref[...] = whole[pl.ds(pl.multiple_of(place[0] * half, 8), half), :]
    given_ref[...] = whole[pl.ds(pl.multiple_of((1 - place[0]) * half, 8), half), :]


def put_grads(grads, whole):
    width = grads.shape[1]
    whole[pl.ds(0, width), :] = grads[0].T
    whole[pl.ds(width, width), :] = grads[1].T
    whole[pl.ds(2 * width, width), :] = grads[2]


def contrast_layer_kernel(
    row_bits, place, src, live, lists, counts, tiles_hbm,
    own_rows, e1, e2, e3, e4, e5, loss_part, hidden_t, latents, agg, w_self, w_agg, w_out,
    own_ref, pair_a_ref, pair_b_ref, cross_a_ref, cross_b_ref, other_ref, extra_a_ref, extra_b_ref,
    kept_ref, given_ref,
    tiles, spread, grads, whole, weighted, rows_a, rows_b, rows_c, rows_d, sems,
):
    low = (1 << row_bits) - 1
    blocks, block_rows = tiles.shape[0], tiles.shape[2]
    groups = blocks // GROUP
    triplets = e1.shape[0]
    fetch_tiles(tiles_hbm, tiles, sems, groups)
    held = (rows_a, rows_b, rows_c, rows_d)
    rows_a[...] = own_rows[...]
    for rows in held[1:]:
        rows[...] = jnp.zeros(rows.shape, F32)
    spread[...] = jnp.zeros(spread.shape, F32)
    grads[...] = jnp.zeros(grads.shape, F32)
    for k, piece in enumerate((e1, e2, e3)):
        weighted[pl.ds(k * triplets, triplets), :] = piece[...].astype(F32)
    weighted[pl.ds(3 * triplets, triplets), :] = e4[...].astype(F32) + e5[...].astype(F32)
    weighted[pl.ds(4 * triplets, 8), :] = jnp.zeros((8, weighted.shape[1]), F32)
    for k in range(1, PIECES):
        first_p, first_n, eights = pair_of_lists(lists, counts, k, triplets)

        def put(i, carry, first_p=first_p, first_n=first_n):
            for u in range(8):
                code_n = lists[first_n + i * 8 + u]
                code_p = lists[first_p + i * 8 + u]
                from_n = pl.ds((code_n >> row_bits) - triplets, 1)
                from_p = pl.ds((code_p >> row_bits) - triplets, 1)
                held_n, held_p = held[u % 2], held[2 + u % 2]
                held_n[pl.ds(code_n & low, 1), :] += weighted[from_n, :]
                held_p[pl.ds(code_p & low, 1), :] -= weighted[from_p, :]
            return carry

        lax.fori_loop(0, eights, put, 0)

    def step(g, carry):
        pieces = []
        for q in range(GROUP):
            here = pl.ds(pl.multiple_of((g * GROUP + q) * block_rows, block_rows), block_rows)
            block = (rows_a[here, :] + rows_b[here, :]) + (rows_c[here, :] + rows_d[here, :])
            pieces.append(block.T)
        await_tiles(tiles_hbm, tiles, sems, g)
        backward_group(1, g, place, src, live, tiles, jnp.concatenate(pieces, axis=1), hidden_t, latents, agg,
                       w_self, w_agg, w_out, grads, spread)
        return carry

    lax.fori_loop(0, groups, step, 0)
    cut = pair_a_ref.shape[0]
    own_ref[...] = spread[pl.ds(0, blocks)]
    for k, (head, tail) in enumerate(((pair_a_ref, pair_b_ref), (cross_a_ref, cross_b_ref))):
        head[...] = spread[pl.ds((k + 1) * blocks, cut)].astype(BF16)
        tail[...] = spread[pl.ds((k + 1) * blocks + cut, blocks - cut)].astype(BF16)
    other_ref[...] = spread[pl.ds(3 * blocks, blocks)].astype(BF16)
    extra_a_ref[...] = spread[pl.ds(4 * blocks, cut)].astype(BF16)
    extra_b_ref[...] = spread[pl.ds(4 * blocks + cut, blocks - cut)].astype(BF16)
    put_grads(grads, whole)
    top = 3 * grads.shape[1]
    whole[pl.ds(top, 8), :] = loss_part[...]
    whole[pl.ds(top + 8, 8), :] = jnp.zeros((8, whole.shape[1]), F32)
    put_halves(place, whole, kept_ref, given_ref)


def last_layer_kernel(
    place, src, live, tiles_hbm, own, pair_a, pair_b, cross_b, other, hidden_t, latents, agg,
    w_self, w_agg, w_out, w_enc, layer_table, p0, p1, p2, p3, p4, p5,
    kept_ref, given_ref, tiles, spread, grads, whole, received, sems,
):
    blocks = tiles.shape[0]
    groups = blocks // GROUP
    cut = pair_a.shape[0]
    fetch_tiles(tiles_hbm, tiles, sems, groups)
    spread[...] = jnp.zeros(spread.shape, F32)
    grads[...] = jnp.zeros(grads.shape, F32)
    head, tail = pl.ds(0, cut), pl.ds(cut, blocks - cut)
    received[head] = own[head] + other[head].astype(F32) + pair_a[...].astype(F32)
    from_far = pair_b[...].astype(F32) + cross_b[...].astype(F32)
    received[tail] = own[tail] + other[tail].astype(F32) + from_far

    def step(g, carry):
        pieces = [received[g * GROUP + q] for q in range(GROUP)]
        await_tiles(tiles_hbm, tiles, sems, g)
        backward_group(0, g, place, src, live, tiles, jnp.concatenate(pieces, axis=1), hidden_t, latents, agg,
                       w_self, w_agg, w_out, grads, spread)
        return carry

    lax.fori_loop(0, groups, step, 0)
    w_in = input_weights(w_enc, layer_table)
    grad_in = jnp.zeros(w_in.shape, F32)
    for k, pack in enumerate(((p0,), (p1,), (p2,), (p3,), (p4, p5))):
        operand = encode_operand(*pack)
        squashed = jnp.tanh(dot_tn(w_in, operand))
        gradient = jnp.concatenate([spread[k * blocks + q] for q in range(blocks)], axis=1)
        encoded_grad = (gradient * (1.0 - squashed * squashed)).astype(BF16)
        grad_in = grad_in + dot_nt(operand, encoded_grad)
    put_grads(grads, whole)
    whole[pl.ds(3 * grads.shape[1], 2 * PACK_ROWS), :] = grad_in
    put_halves(place, whole, kept_ref, given_ref)


def result_kernel(
    scale, feats, place, part_0, back_0, part_1, back_1,
    loss_ref, enc_ref, table_ref, self_ref, agg_ref, out_ref, whole_0, whole_1,
):
    for whole, part, back in ((whole_0, part_0, back_0), (whole_1, part_1, back_1)):
        half = part.shape[0]
        whole[pl.ds(pl.multiple_of(place[0] * half, 8), half), :] = part[...]
        whole[pl.ds(pl.multiple_of((1 - place[0]) * half, 8), half), :] = back[...]
    width = whole_0.shape[1]
    top = 3 * width
    for layer, whole in enumerate((whole_0, whole_1)):
        for k, out in enumerate((self_ref, agg_ref, out_ref)):
            out[layer] = whole[pl.ds(k * width, width), :]
    enc_ref[...] = whole_0[pl.ds(top, feats), :]
    table_ref[...] = whole_0[pl.ds(top + PACK_ROWS, PACK_ROWS), :]
    loss_ref[0] = jnp.max(whole_1[pl.ds(top, 8), :]) * scale


def body(
    hit_feats, layer_ids, edge_tiles, src_blocks, live_slots,
    anchor_hits, positive_hits, negative_hits, w_enc, layer_table, w_self, w_agg, w_out,
):
    blocks, slots, block_rows = edge_tiles.shape[0], edge_tiles.shape[1], edge_tiles.shape[2]
    feats, width = w_enc.shape
    kinds = layer_table.shape[0]
    hits = blocks * block_rows
    triplets = anchor_hits.shape[0]
    layers = w_self.shape[0]
    row_bits = hits.bit_length() - 1
    count = lax.axis_size("phi")
    assert hits == 1 << row_bits and blocks & (blocks - 1) == 0 and blocks % GROUP == 0
    assert feats < PACK_ROWS - 3 and kinds == PACK_ROWS and layers == 2 and 4 * triplets == hits
    assert count % 4 == 0
    groups = blocks // GROUP
    cut, back_cut = blocks // 2, blocks * 5 // 8
    place = lax.dynamic_slice_in_dim(place_table(), lax.axis_index("phi") & 3, 1, 0).reshape(-1)
    sends_pair = place[0] == place[1]

    codes = jnp.concatenate([positive_hits, negative_hits])
    codes = jnp.concatenate([codes >> 7, codes & 127])
    pack = jnp.concatenate(
        [
            hit_feats,
            layer_ids.astype(BF16)[None, :],
            codes.astype(BF16)[None, :],
            jnp.zeros((PACK_ROWS - feats - 2, hits), BF16),
        ]
    )
    packs = gather_small(pack)

    block_shape = (blocks, block_rows, width)
    tile_scratch = pltpu.VMEM(edge_tiles.shape, BF16)
    group_sems = pltpu.SemaphoreType.DMA((groups,))
    window_scratch = pltpu.VMEM((PIECES * blocks + 1, block_rows, width), BF16)
    blocked = jax.ShapeDtypeStruct(block_shape, BF16)
    head = jax.ShapeDtypeStruct((cut, block_rows, width), BF16)
    tail = jax.ShapeDtypeStruct((blocks - cut, block_rows, width), BF16)
    back_head = jax.ShapeDtypeStruct((back_cut, block_rows, width), BF16)
    back_tail = jax.ShapeDtypeStruct((blocks - back_cut, block_rows, width), BF16)
    slots_in = (place, src_blocks, live_slots)

    latents_0, agg_0, hidden_0, latents_1, new_a, new_b = pl.pallas_call(
        first_layer_kernel,
        out_shape=(blocked,) * 4 + (head, tail),
        in_specs=[smem()] * 3 + [in_hbm()] + [vmem()] * 11,
        out_specs=(vmem(),) * 6,
        scratch_shapes=[tile_scratch, window_scratch, group_sems],
        compiler_params=params(),
        name="first_layer",
    )(*slots_in, edge_tiles, *packs, w_enc, layer_table, w_self, w_agg, w_out)

    held_codes = jnp.stack([packs[1], packs[2], packs[3], packs[4] + packs[5]])[:, feats + 1]
    held_codes = after(held_codes, new_a).astype(jnp.int32).reshape(PIECES - 1, 2, 2 * triplets)
    own_codes = jnp.concatenate([positive_hits, negative_hits]).reshape(1, 2 * triplets)
    named = jnp.concatenate([own_codes, (held_codes[:, 0] << 7) + held_codes[:, 1]]).reshape(PIECES, 2, triplets)
    mine = (named >> row_bits) == place[7 : 7 + PIECES, None, None]
    numbers = jnp.arange(PIECES * triplets, dtype=jnp.int32).reshape(PIECES, 1, triplets)
    coded = jnp.where(mine, (numbers << row_bits) | (named & (hits - 1)), (PIECES * triplets) << row_bits)
    lists = lax.sort(coded.reshape(2 * PIECES, triplets).T, dimension=0, is_stable=False).T.reshape(-1)
    counts = jnp.sum(mine.astype(jnp.int32), axis=2).reshape(-1)

    pair_a = send(new_a, pair_links(count))
    late_b = after(new_b, lists, counts)
    pair_b = send(late_b, pair_links(count))
    cross_b = send(late_b, cross_links(count))
    other_a = send(new_a, core_links(count))
    other_b = send(new_b, core_links(count))
    pair_a = after(pair_a, lists, counts)
    cross_a = send(pair_a, relay_links(count))
    extra_pa = send(pair_a, extra_links(count, True))
    extra_pb = send(pair_b, extra_links(count, True))
    extra_cb = send(cross_b, extra_links(count, False))
    extra_ca = send(cross_a, extra_links(count, False))

    agg_1, hidden_1, latents_2 = pl.pallas_call(
        next_layer_kernel,
        out_shape=(blocked,) * 3,
        in_specs=[smem()] * 3 + [in_hbm()] * 13 + [vmem()] * 3,
        out_specs=(vmem(),) * 3,
        scratch_shapes=[
            tile_scratch, window_scratch, group_sems, pltpu.SemaphoreType.DMA((2 * PIECES,)),
        ],
        compiler_params=params(),
        name="next_layer",
    )(
        *slots_in, edge_tiles, new_a, new_b, pair_a, pair_b, cross_a, cross_b, other_a, other_b,
        extra_pa, extra_pb, extra_ca, extra_cb, w_self, w_agg, w_out,
    )

    triplet_rows = jax.ShapeDtypeStruct((triplets, width), BF16)
    wide_rows = jax.ShapeDtypeStruct((triplets, width), F32)
    hit_rows = pltpu.VMEM((hits, width), F32)
    gap_own, *gap_pieces = pl.pallas_call(
        lambda *refs: gather_kernel(row_bits, *refs),
        out_shape=(triplet_rows,) * 5,
        in_specs=[smem()] * 2 + [vmem()],
        out_specs=(vmem(),) * 5,
        scratch_shapes=[
            hit_rows,
            pltpu.VMEM((PIECES * triplets + 8, width), F32),
            pltpu.VMEM((PIECES * triplets + 8, width), F32),
        ],
        compiler_params=params(),
        name="gather_rows",
    )(lists, counts, latents_2)
    gaps, joined = return_small(*gap_pieces, sends_pair)

    anchor_rows = pl.pallas_call(
        anchor_kernel,
        out_shape=wide_rows,
        in_specs=[smem(), vmem()],
        out_specs=vmem(),
        scratch_shapes=[hit_rows],
        compiler_params=params(),
        name="anchor_rows",
    )(anchor_hits, after(latents_2, *joined))

    loss_part, weighted, weighted_b, anchor_grad = pl.pallas_call(
        score_kernel,
        out_shape=(
            jax.ShapeDtypeStruct((8, width), F32),
            jax.ShapeDtypeStruct((triplets + 8, width), F32),
            triplet_rows,
            wide_rows,
        ),
        in_specs=[vmem()] * 5,
        out_specs=(vmem(),) * 4,
        compiler_params=params(),
        name="scores",
    )(gap_own, *gaps, anchor_rows)

    own_rows = pl.pallas_call(
        lambda *refs: own_rows_kernel(row_bits, *refs),
        out_shape=jax.ShapeDtypeStruct((hits, width), F32),
        in_specs=[smem()] * 3 + [vmem()] * 2,
        out_specs=vmem(),
        scratch_shapes=[hit_rows] * 3,
        compiler_params=params(),
        name="own_rows",
    )(lists, counts, anchor_hits, weighted, anchor_grad)
    weighted_window = gather_small(weighted_b, own_rows)

    wide_blocked = jax.ShapeDtypeStruct(block_shape, F32)
    spread_scratch = pltpu.VMEM((PIECES * blocks + 1, width, block_rows), F32)
    grads_scratch = pltpu.VMEM((3, width, width), F32)
    rows_0, rows_1 = 3 * width + 2 * PACK_ROWS, 3 * width + 16
    half_0 = jax.ShapeDtypeStruct((rows_0 // 2, width), F32)
    half_1 = jax.ShapeDtypeStruct((rows_1 // 2, width), F32)
    own_1, ret_pa, ret_pb, ret_ca, ret_cb, ret_other, ret_ea, ret_eb, kept_1, given_1 = pl.pallas_call(
        lambda *refs: contrast_layer_kernel(row_bits, *refs),
        out_shape=(wide_blocked,)
        + (back_head, back_tail) * 2
        + (blocked, back_head, back_tail, half_1, half_1),
        in_specs=[smem()] * 5 + [in_hbm()] + [vmem()] * 13,
        out_specs=(vmem(),) * 10,
        scratch_shapes=[
            tile_scratch, spread_scratch, grads_scratch, pltpu.VMEM((rows_1, width), F32),
            pltpu.VMEM((4 * triplets + 8, width), F32), hit_rows, hit_rows, hit_rows, hit_rows, group_sems,
        ],
        compiler_params=params(),
        name="contrast_layer",
    )(
        *slots_in, lists, counts, edge_tiles,
        own_rows, *weighted_window[1:], loss_part,
        hidden_1, latents_1, agg_1, w_self, w_agg, w_out,
    )

    got_a = send(ret_ea, core_links(count))
    got_b = send(ret_eb, core_links(count))
    from_other = send(ret_other, core_links(count))
    ret_pa, ret_ca = join_extra(ret_pa, ret_ca, got_a, sends_pair)
    relayed = send(ret_ca, turned(relay_links(count)))
    ret_pb, ret_cb = join_extra(ret_pb, ret_cb, got_b, sends_pair)
    from_pair_b = send(ret_pb, pair_links(count))
    from_cross_b = send(ret_cb, turned(cross_links(count)))
    ret_pa = (ret_pa.astype(F32) + relayed.astype(F32)).astype(BF16)
    part_1 = first_sums(kept_1, given_1)
    from_pair_a = send(after(ret_pa, from_pair_b, from_cross_b, part_1), pair_links(count))
    part_1, back_1 = last_sums(part_1)
    own_1 = after(own_1, part_1, back_1)

    kept_0, given_0 = pl.pallas_call(
        last_layer_kernel,
        out_shape=(half_0, half_0),
        in_specs=[smem()] * 3 + [in_hbm()] + [vmem()] * 19,
        out_specs=(vmem(),) * 2,
        scratch_shapes=[
            tile_scratch, spread_scratch, grads_scratch, pltpu.VMEM((rows_0, width), F32),
            pltpu.VMEM(block_shape, F32), group_sems,
        ],
        compiler_params=params(),
        name="last_layer",
    )(
        *slots_in, edge_tiles, own_1, from_pair_a, from_pair_b, from_cross_b, from_other,
        hidden_0, latents_0, agg_0, w_self, w_agg, w_out, w_enc, layer_table, *packs,
    )
    part_0, back_0 = last_sums(first_sums(kept_0, given_0))

    square = jax.ShapeDtypeStruct((layers, width, width), F32)
    return pl.pallas_call(
        lambda *refs: result_kernel(1.0 / (triplets * count), feats, *refs),
        out_shape=(
            jax.ShapeDtypeStruct((1,), F32),
            jax.ShapeDtypeStruct((feats, width), F32),
            jax.ShapeDtypeStruct((PACK_ROWS, width), F32),
            square, square, square,
        ),
        in_specs=[smem()] + [vmem()] * 4,
        out_specs=(smem(),) + (vmem(),) * 5,
        scratch_shapes=[pltpu.VMEM((rows_0, width), F32), pltpu.VMEM((rows_1, width), F32)],
        compiler_params=params(),
        name="results",
    )(place, part_0, back_0, part_1, back_1)


def solution(mesh):
    both = ("event", "phi")
    in_specs = (
        P(None, both), P(both), P(both, None, None, None), P(both, None), P(both),
        P(both), P(both), P(both), P(), P(), P(), P(), P(),
    )
    out_specs = (
        P("event"), P("event", None), P("event", None),
        P("event", None, None), P("event", None, None), P("event", None, None),
    )
    return jax.shard_map(body, mesh=mesh, in_specs=in_specs, out_specs=out_specs, check_vma=False)
```

```python
import math

import jax
import jax.numpy as jnp
from jax import lax
from jax.experimental import pallas as pl
from jax.experimental.pallas import tpu as pltpu
from jax.sharding import PartitionSpec as P

loss_divisor = 64.0
F32 = jnp.float32
BF16 = jnp.bfloat16
PACK_ROWS = 16
GROUP = 8

PIECES = 5


def vmem():
    return pl.BlockSpec(memory_space=pltpu.VMEM)


def smem():
    return pl.BlockSpec(memory_space=pltpu.SMEM)


def in_hbm():
    return pl.BlockSpec(memory_space=pl.ANY)


def kept_in_hbm():
    return pl.BlockSpec(memory_space=pltpu.HBM)


def params(mebibytes):
    return pltpu.CompilerParams(vmem_limit_bytes=mebibytes * 1024 * 1024)


def cost(microseconds):
    return pl.CostEstimate(flops=0, transcendentals=0, bytes_accessed=int(microseconds * 3.6e6))


def dot_nn(left, right):
    return lax.dot_general(left, right, (((1,), (0,)), ((), ())), preferred_element_type=F32)


def dot_tn(left, right):
    return lax.dot_general(left, right, (((0,), (0,)), ((), ())), preferred_element_type=F32)


def dot_nt(left, right):
    return lax.dot_general(left, right, (((1,), (1,)), ((), ())), preferred_element_type=F32)


def second(p):
    return (p >> 1) & 1


def pair_links(count):
    return [(p, p ^ 2) for p in range(count)]


def cross_links(count):
    return [(p, (p + (2 if second(p) else -2)) % count) for p in range(count)]


def relay_links(count):
    return [(p, (p + (-4 if second(p) else 4)) % count) for p in range(count)]


def core_links(count):
    return [(p, p ^ 1) for p in range(count)]


def turned(links):
    return [(target, source) for source, target in links]


def place_table():
    rows = []
    for kind in range(4):
        odd, on_second = kind & 1, kind >> 1
        pair, core = (-2 if on_second else 2), (-1 if odd else 1)
        offsets = [0, pair, -pair, core, -core]
        rows.append(
            [odd, on_second]
            + [offsets.index(part - 2) for part in range(PIECES)]
            + [2 - offset for offset in offsets]
            + [0] * 4
        )
    return jnp.array(rows, jnp.int32)


def send(value, links):
    return lax.ppermute(value, "phi", links)


def after(value, *earlier):
    return lax.optimization_barrier((value, *earlier))[0]


def gather_small(value, meanwhile=None):
    count = lax.axis_size("phi")
    pair = send(value, pair_links(count))
    cross = send(value, cross_links(count))
    other = send(value, core_links(count))
    if meanwhile is not None:
        pair = after(pair, meanwhile)
    extra_p = send(pair, core_links(count))
    extra_c = send(cross, core_links(count))
    return (value, pair, cross, other, extra_p, extra_c)


def join_extra(pair, cross, received, sends_pair):
    to_pair = jnp.where(sends_pair, received, jnp.zeros_like(received))
    to_cross = jnp.where(sends_pair, jnp.zeros_like(received), received)
    pair = (pair.astype(F32) + to_pair.astype(F32)).astype(BF16)
    cross = (cross.astype(F32) + to_cross.astype(F32)).astype(BF16)
    return pair, cross


def return_small(pair, cross, other, extra, sends_pair):
    count = lax.axis_size("phi")
    received = send(extra, core_links(count))
    from_other = send(other, core_links(count))
    pair, cross = join_extra(pair, cross, received, sends_pair)
    from_pair = send(pair, pair_links(count))
    from_cross = send(cross, turned(cross_links(count)))
    return (from_pair, from_cross, from_other), (pair, cross)


def first_sums(kept, given):
    count = lax.axis_size("phi")
    part = kept + send(given, core_links(count))
    if count & (count - 1) == 0:
        part = part + send(part, pair_links(count))
    return part


def last_sums(part):
    count = lax.axis_size("phi")
    if count & (count - 1):
        moved = part
        for _ in range(count // 2 - 1):
            moved = send(moved, [(p, (p + 2) % count) for p in range(count)])
            part = part + moved
    else:
        step = 4
        while step < count:
            part = part + send(part, [(p, p ^ step) for p in range(count)])
            step *= 2
    return part, send(part, core_links(count))


def fetch_tiles(tiles_hbm, tiles, sems, groups):
    for g in range(groups):
        pltpu.make_async_copy(
            tiles_hbm.at[pl.ds(g * GROUP, GROUP)], tiles.at[pl.ds(g * GROUP, GROUP)], sems.at[g]
        ).start()


def await_tiles(tiles_hbm, tiles, sems, g):
    first = pl.multiple_of(g * GROUP, GROUP)
    pltpu.make_async_copy(
        tiles_hbm.at[pl.ds(first, GROUP)], tiles.at[pl.ds(first, GROUP)], sems.at[g]
    ).wait()


def extra_of(place, from_pair, from_cross):
    return jnp.where(place[0] != place[1], from_pair, from_cross)


def encode_operand(place, *pack_refs):
    pieces = [pack_ref[...].astype(F32) for pack_ref in pack_refs]
    rows = pieces[0] if len(pieces) == 1 else extra_of(place, *pieces)
    ids = rows[12:13, :]
    layers = lax.broadcasted_iota(jnp.int32, rows.shape, 0).astype(F32)
    onehot = (layers == ids).astype(BF16)
    return jnp.concatenate([rows.astype(BF16), onehot], axis=0)


def block_of(place, src, live, b, s, blocks):
    bits = blocks.bit_length() - 1
    named = src[b, s]
    block = (place[2 + (named >> bits)] << bits) + (named & (blocks - 1))
    return jnp.where(s < live[b], block, PIECES * blocks)


def forward_group(layer, g, place, src, live, tiles, window, w_self, w_agg, w_out, agg_ref, hidden_t_ref, new_ref):
    blocks, slots = tiles.shape[0], tiles.shape[1]
    sums = []
    for q in range(GROUP):
        b = g * GROUP + q
        left = jnp.concatenate([tiles[b, s] for s in range(slots)], axis=1)
        right = [window[block_of(place, src, live, b, s, blocks)] for s in range(slots)]
        sums.append(dot_nn(left, jnp.concatenate(right, axis=0)))
    first = pl.multiple_of(g * GROUP, GROUP)
    agg = jnp.concatenate(sums, axis=0).astype(BF16)
    rows, width = agg.shape
    here = window[pl.ds(first, GROUP)].reshape(rows, width)
    activation = dot_nn(here, w_self[layer]) + dot_nn(agg, w_agg[layer])
    hidden = jnp.maximum(activation, 0.0)
    hidden_b = hidden.astype(BF16)
    updated = (here.astype(F32) + dot_nn(hidden_b, w_out[layer])).astype(BF16)
    agg_ref[pl.ds(first, GROUP)] = agg.reshape(GROUP, rows // GROUP, width)
    new_ref[pl.ds(first, GROUP)] = updated.reshape(GROUP, rows // GROUP, width)
    for q in range(GROUP):
        block = hidden[q * (rows // GROUP) : (q + 1) * (rows // GROUP)]
        hidden_t_ref[first + q] = block.T.astype(BF16)


def input_weights(w_enc, layer_table):
    feats, width = w_enc.shape
    gap = jnp.zeros((PACK_ROWS - feats, width), F32)
    return jnp.concatenate([w_enc[...].astype(F32), gap, layer_table[...].astype(F32)], axis=0).astype(BF16)


def first_layer_kernel(
    place, src, live, tiles_hbm, p0, p1, p2, p3, p4, p5, w_enc, layer_table, w_self, w_agg, w_out,
    own_ref, agg_ref, hidden_t_ref, new_ref, new_a_ref, new_b_ref, tiles, window, sems,
):
    blocks, block_rows = tiles.shape[0], tiles.shape[2]
    groups = blocks // GROUP
    fetch_tiles(tiles_hbm, tiles, sems, groups)
    w_in = input_weights(w_enc, layer_table)
    for k, pack in enumerate(((p0,), (p1,), (p2,), (p3,), (p4, p5))):
        latents = jnp.tanh(dot_tn(encode_operand(place, *pack), w_in)).astype(BF16)
        window[pl.ds(k * blocks, blocks)] = latents.reshape(blocks, block_rows, latents.shape[1])
    window[PIECES * blocks] = jnp.zeros(window.shape[1:], BF16)
    own_ref[...] = window[pl.ds(0, blocks)]

    def step(g, carry):
        await_tiles(tiles_hbm, tiles, sems, g)
        forward_group(0, g, place, src, live, tiles, window, w_self, w_agg, w_out, agg_ref, hidden_t_ref, new_ref)
        return carry

    lax.fori_loop(0, groups, step, 0)
    cut = new_a_ref.shape[0]
    new_a_ref[...] = new_ref[pl.ds(0, cut)]
    new_b_ref[...] = new_ref[pl.ds(cut, blocks - cut)]


def next_layer_kernel(
    place, src, live, tiles_hbm, own_a, own_b, pair_a, pair_b, cross_a, cross_b, other_a, other_b,
    extra_pa, extra_pb, extra_ca, extra_cb, w_self, w_agg, w_out,
    agg_ref, hidden_t_ref, new_ref, tiles, window, sems, piece_sems,
):
    blocks, cut = tiles.shape[0], own_a.shape[0]
    groups = blocks // GROUP

    def copies(pieces, first):
        for k, (head, tail) in enumerate(pieces):
            start = (first + k) * blocks
            yield pltpu.make_async_copy(
                head, window.at[pl.ds(start, cut)], piece_sems.at[2 * (first + k)]
            )
            yield pltpu.make_async_copy(
                tail, window.at[pl.ds(start + cut, blocks - cut)], piece_sems.at[2 * (first + k) + 1]
            )

    plain = list(copies([(own_a, own_b), (pair_a, pair_b), (cross_a, cross_b), (other_a, other_b)], 0))
    for copy in plain:
        copy.start()

    def extra_is_pair(do):
        @pl.when(place[0] != place[1])
        def _():
            for copy in copies([(extra_pa, extra_pb)], 4):
                do(copy)

        @pl.when(place[0] == place[1])
        def _():
            for copy in copies([(extra_ca, extra_cb)], 4):
                do(copy)

    extra_is_pair(lambda copy: copy.start())
    fetch_tiles(tiles_hbm, tiles, sems, groups)
    window[PIECES * blocks] = jnp.zeros(window.shape[1:], BF16)
    for copy in plain:
        copy.wait()
    extra_is_pair(lambda copy: copy.wait())

    def step(g, carry):
        await_tiles(tiles_hbm, tiles, sems, g)
        forward_group(1, g, place, src, live, tiles, window, w_self, w_agg, w_out, agg_ref, hidden_t_ref, new_ref)
        return carry

    lax.fori_loop(0, groups, step, 0)


def pair_of_lists(lists, counts, k, triplets):
    longest = jnp.maximum(counts[2 * k], counts[2 * k + 1])
    return 2 * k * triplets, (2 * k + 1) * triplets, (longest + 7) >> 3


def gather_kernel(row_bits, lists, counts, latents, d0, d1, d2, d3, d4, wide, negative, positive):
    low = (1 << row_bits) - 1
    triplets = d0.shape[0]
    blocks, block_rows, width = latents.shape
    wide[...] = latents[...].reshape(blocks * block_rows, width).astype(F32)
    negative[...] = jnp.zeros(negative.shape, F32)
    positive[...] = jnp.zeros(positive.shape, F32)
    for k, out in enumerate((d0, d1, d2, d3, d4)):
        first_p, first_n, eights = pair_of_lists(lists, counts, k, triplets)

        def pick(i, carry, first_p=first_p, first_n=first_n):
            for u in range(8):
                code_n = lists[first_n + i * 8 + u]
                code_p = lists[first_p + i * 8 + u]
                negative[pl.ds(code_n >> row_bits, 1), :] = wide[pl.ds(code_n & low, 1), :]
                positive[pl.ds(code_p >> row_bits, 1), :] = wide[pl.ds(code_p & low, 1), :]
            return carry

        lax.fori_loop(0, eights, pick, 0)
        here = pl.ds(k * triplets, triplets)
        out[...] = (negative[here, :] - positive[here, :]).astype(BF16)


def anchor_kernel(anchors, latents, anchor_ref, wide):
    blocks, block_rows, width = latents.shape
    wide[...] = latents[...].reshape(blocks * block_rows, width).astype(F32)

    def pick(i, carry):
        for u in range(8):
            anchor_ref[pl.ds(i * 8 + u, 1), :] = wide[pl.ds(anchors[i * 8 + u], 1), :]
        return carry

    lax.fori_loop(0, anchor_ref.shape[0] // 8, pick, 0)


def own_rows_kernel(row_bits, lists, counts, anchors, weighted, anchor_grad, rows_ref, rows_b, rows_c, rows_d):
    low = (1 << row_bits) - 1
    triplets = anchor_grad.shape[0]
    held = (rows_ref, rows_b, rows_c, rows_d)
    for rows in held:
        rows[...] = jnp.zeros(rows.shape, F32)

    def put_anchor(i, carry):
        for u in range(8):
            here = pl.ds(anchors[i * 8 + u], 1)
            held[u % 4][here, :] += anchor_grad[pl.ds(i * 8 + u, 1), :]
        return carry

    lax.fori_loop(0, triplets // 8, put_anchor, 0)
    first_p, first_n, eights = pair_of_lists(lists, counts, 0, triplets)

    def put(i, carry):
        for u in range(8):
            code_n = lists[first_n + i * 8 + u]
            code_p = lists[first_p + i * 8 + u]
            from_n = pl.ds(jnp.minimum(code_n >> row_bits, triplets), 1)
            from_p = pl.ds(jnp.minimum(code_p >> row_bits, triplets), 1)
            held[u % 2][pl.ds(code_n & low, 1), :] += weighted[from_n, :]
            held[2 + u % 2][pl.ds(code_p & low, 1), :] -= weighted[from_p, :]
        return carry

    lax.fori_loop(0, eights, put, 0)
    rows_ref[...] = (rows_ref[...] + rows_b[...]) + (rows_c[...] + rows_d[...])


def score_kernel(own, pair, cross, other, anchors, loss_ref, weighted_ref, weighted_b_ref, anchor_grad_ref):
    triplets, width = anchors.shape
    inv_root = 1.0 / math.sqrt(width)
    scale = 1.0 / (loss_divisor * math.sqrt(width))
    chunk = 128
    loss = jnp.zeros((chunk, 1), F32)
    weighted_ref[pl.ds(triplets, 8), :] = jnp.zeros((8, width), F32)
    for c in range(triplets // chunk):
        here = pl.ds(c * chunk, chunk)
        gap = own[here, :].astype(F32) + pair[here, :].astype(F32)
        gap = gap + cross[here, :].astype(F32) + other[here, :].astype(F32)
        anchor = anchors[here, :]
        score = jnp.sum(anchor * gap, axis=1, keepdims=True) * inv_root
        loss = loss + jnp.maximum(score, 0.0) + jnp.log1p(jnp.exp(-jnp.abs(score)))
        coef = scale / (1.0 + jnp.exp(-score))
        weighted = coef * anchor
        weighted_ref[here, :] = weighted
        weighted_b_ref[here, :] = weighted.astype(BF16)
        anchor_grad_ref[here, :] = coef * gap
    loss_ref[...] = jnp.broadcast_to(jnp.sum(loss, axis=0, keepdims=True), loss_ref.shape)


def backward_group(layer, g, place, src, live, tiles, gradient, hidden_t, latents, agg, w_self, w_agg, w_out, grads, spread):
    blocks, slots = tiles.shape[0], tiles.shape[1]
    first = pl.multiple_of(g * GROUP, GROUP)
    rows, width = tiles.shape[2], latents.shape[2]
    upstream = gradient.astype(BF16)
    hidden = jnp.concatenate([hidden_t[first + q] for q in range(GROUP)], axis=1)
    grads[2] += dot_nt(hidden, upstream)
    hidden_grad = dot_nn(w_out[layer], upstream)
    act_grad = jnp.where(hidden > 0, hidden_grad, 0.0).astype(BF16)
    grads[0] += dot_nn(act_grad, latents[pl.ds(first, GROUP)].reshape(GROUP * rows, width))
    grads[1] += dot_nn(act_grad, agg[pl.ds(first, GROUP)].reshape(GROUP * rows, width))
    agg_grad = dot_nn(w_agg[layer], act_grad).astype(BF16)
    direct = gradient + dot_nn(w_self[layer], act_grad)
    for q in range(GROUP):
        b = g * GROUP + q
        spread[b] += direct[:, q * rows : (q + 1) * rows]
        right = jnp.concatenate([tiles[b, s] for s in range(slots)], axis=1)
        parts = dot_nn(agg_grad[:, q * rows : (q + 1) * rows], right)
        for s in range(slots):
            spread[block_of(place, src, live, b, s, blocks)] += parts[:, s * rows : (s + 1) * rows]


def put_halves(place, whole, kept_ref, given_ref):
    half = kept_ref.shape[0]
    kept_ref[...] = whole[pl.ds(pl.multiple_of(place[0] * half, 8), half), :]
    given_ref[...] = whole[pl.ds(pl.multiple_of((1 - place[0]) * half, 8), half), :]


def put_grads(grads, whole):
    width = grads.shape[1]
    whole[pl.ds(0, width), :] = grads[0].T
    whole[pl.ds(width, width), :] = grads[1].T
    whole[pl.ds(2 * width, width), :] = grads[2]


def contrast_layer_kernel(
    row_bits, place, src, live, lists, counts, tiles_hbm,
    own_rows, e1, e2, e3, e4, e5, loss_part, hidden_t, latents, agg, w_self, w_agg, w_out,
    own_ref, pair_a_ref, pair_b_ref, cross_a_ref, cross_b_ref, other_ref, extra_a_ref, extra_b_ref,
    kept_ref, given_ref,
    tiles, spread, grads, whole, weighted, rows_a, rows_b, rows_c, rows_d, sems,
):
    low = (1 << row_bits) - 1
    blocks, block_rows = tiles.shape[0], tiles.shape[2]
    groups = blocks // GROUP
    triplets = e1.shape[0]
    fetch_tiles(tiles_hbm, tiles, sems, groups)
    held = (rows_a, rows_b, rows_c, rows_d)
    rows_a[...] = own_rows[...]
    for rows in held[1:]:
        rows[...] = jnp.zeros(rows.shape, F32)
    spread[...] = jnp.zeros(spread.shape, F32)
    grads[...] = jnp.zeros(grads.shape, F32)
    for k, piece in enumerate((e1, e2, e3)):
        weighted[pl.ds(k * triplets, triplets), :] = piece[...].astype(F32)
    weighted[pl.ds(3 * triplets, triplets), :] = extra_of(place, e4[...].astype(F32), e5[...].astype(F32))
    weighted[pl.ds(4 * triplets, 8), :] = jnp.zeros((8, weighted.shape[1]), F32)
    for k in range(1, PIECES):
        first_p, first_n, eights = pair_of_lists(lists, counts, k, triplets)

        def put(i, carry, first_p=first_p, first_n=first_n):
            for u in range(8):
                code_n = lists[first_n + i * 8 + u]
                code_p = lists[first_p + i * 8 + u]
                from_n = pl.ds((code_n >> row_bits) - triplets, 1)
                from_p = pl.ds((code_p >> row_bits) - triplets, 1)
                held_n, held_p = held[u % 2], held[2 + u % 2]
                held_n[pl.ds(code_n & low, 1), :] += weighted[from_n, :]
                held_p[pl.ds(code_p & low, 1), :] -= weighted[from_p, :]
            return carry

        lax.fori_loop(0, eights, put, 0)

    def step(g, carry):
        pieces = []
        for q in range(GROUP):
            here = pl.ds(pl.multiple_of((g * GROUP + q) * block_rows, block_rows), block_rows)
            block = (rows_a[here, :] + rows_b[here, :]) + (rows_c[here, :] + rows_d[here, :])
            pieces.append(block.T)
        await_tiles(tiles_hbm, tiles, sems, g)
        backward_group(1, g, place, src, live, tiles, jnp.concatenate(pieces, axis=1), hidden_t, latents, agg,
                       w_self, w_agg, w_out, grads, spread)
        return carry

    lax.fori_loop(0, groups, step, 0)
    cut = pair_a_ref.shape[0]
    own_ref[...] = spread[pl.ds(0, blocks)]
    for k, (head, tail) in enumerate(((pair_a_ref, pair_b_ref), (cross_a_ref, cross_b_ref))):
        head[...] = spread[pl.ds((k + 1) * blocks, cut)].astype(BF16)
        tail[...] = spread[pl.ds((k + 1) * blocks + cut, blocks - cut)].astype(BF16)
    other_ref[...] = spread[pl.ds(3 * blocks, blocks)].astype(BF16)
    extra_a_ref[...] = spread[pl.ds(4 * blocks, cut)].astype(BF16)
    extra_b_ref[...] = spread[pl.ds(4 * blocks + cut, blocks - cut)].astype(BF16)
    put_grads(grads, whole)
    top = 3 * grads.shape[1]
    whole[pl.ds(top, 8), :] = loss_part[...]
    whole[pl.ds(top + 8, 8), :] = jnp.zeros((8, whole.shape[1]), F32)
    put_halves(place, whole, kept_ref, given_ref)


def last_layer_kernel(
    place, src, live, tiles_hbm, own, pair_a, pair_b, cross_b, other, hidden_t, latents, agg,
    w_self, w_agg, w_out, w_enc, layer_table, p0, p1, p2, p3, p4, p5,
    kept_ref, given_ref, tiles, spread, grads, whole, received, sems,
):
    blocks = tiles.shape[0]
    groups = blocks // GROUP
    cut = pair_a.shape[0]
    fetch_tiles(tiles_hbm, tiles, sems, groups)
    spread[...] = jnp.zeros(spread.shape, F32)
    grads[...] = jnp.zeros(grads.shape, F32)
    head, tail = pl.ds(0, cut), pl.ds(cut, blocks - cut)
    received[head] = own[head] + other[head].astype(F32) + pair_a[...].astype(F32)
    from_far = pair_b[...].astype(F32) + cross_b[...].astype(F32)
    received[tail] = own[tail] + other[tail].astype(F32) + from_far

    def step(g, carry):
        pieces = [received[g * GROUP + q] for q in range(GROUP)]
        await_tiles(tiles_hbm, tiles, sems, g)
        backward_group(0, g, place, src, live, tiles, jnp.concatenate(pieces, axis=1), hidden_t, latents, agg,
                       w_self, w_agg, w_out, grads, spread)
        return carry

    lax.fori_loop(0, groups, step, 0)
    w_in = input_weights(w_enc, layer_table)
    grad_in = jnp.zeros(w_in.shape, F32)
    for k, pack in enumerate(((p0,), (p1,), (p2,), (p3,), (p4, p5))):
        operand = encode_operand(place, *pack)
        squashed = jnp.tanh(dot_tn(w_in, operand))
        gradient = jnp.concatenate([spread[k * blocks + q] for q in range(blocks)], axis=1)
        encoded_grad = (gradient * (1.0 - squashed * squashed)).astype(BF16)
        grad_in = grad_in + dot_nt(operand, encoded_grad)
    put_grads(grads, whole)
    whole[pl.ds(3 * grads.shape[1], 2 * PACK_ROWS), :] = grad_in
    put_halves(place, whole, kept_ref, given_ref)


def result_kernel(
    scale, feats, place, part_0, back_0, part_1, back_1,
    loss_ref, enc_ref, table_ref, self_ref, agg_ref, out_ref, whole_0, whole_1,
):
    for whole, part, back in ((whole_0, part_0, back_0), (whole_1, part_1, back_1)):
        half = part.shape[0]
        whole[pl.ds(pl.multiple_of(place[0] * half, 8), half), :] = part[...]
        whole[pl.ds(pl.multiple_of((1 - place[0]) * half, 8), half), :] = back[...]
    width = whole_0.shape[1]
    top = 3 * width
    for layer, whole in enumerate((whole_0, whole_1)):
        for k, out in enumerate((self_ref, agg_ref, out_ref)):
            out[layer] = whole[pl.ds(k * width, width), :]
    enc_ref[...] = whole_0[pl.ds(top, feats), :]
    table_ref[...] = whole_0[pl.ds(top + PACK_ROWS, PACK_ROWS), :]
    loss_ref[0] = jnp.max(whole_1[pl.ds(top, 8), :]) * scale


def body(
    hit_feats, layer_ids, edge_tiles, src_blocks, live_slots,
    anchor_hits, positive_hits, negative_hits, w_enc, layer_table, w_self, w_agg, w_out,
):
    blocks, slots, block_rows = edge_tiles.shape[0], edge_tiles.shape[1], edge_tiles.shape[2]
    feats, width = w_enc.shape
    kinds = layer_table.shape[0]
    hits = blocks * block_rows
    triplets = anchor_hits.shape[0]
    layers = w_self.shape[0]
    row_bits = hits.bit_length() - 1
    count = lax.axis_size("phi")
    assert hits == 1 << row_bits and blocks & (blocks - 1) == 0 and blocks % GROUP == 0
    assert feats < PACK_ROWS - 3 and kinds == PACK_ROWS and layers == 2 and 4 * triplets == hits
    assert count % 4 == 0
    groups = blocks // GROUP
    cut, back_cut = blocks // 2, blocks * 11 // 16
    place = lax.dynamic_slice_in_dim(place_table(), lax.axis_index("phi") & 3, 1, 0).reshape(-1)
    sends_pair = place[0] == place[1]

    codes = jnp.concatenate([positive_hits, negative_hits])
    codes = jnp.concatenate([codes >> 7, codes & 127])
    pack = jnp.concatenate(
        [
            hit_feats,
            layer_ids.astype(BF16)[None, :],
            codes.astype(BF16)[None, :],
            jnp.zeros((PACK_ROWS - feats - 2, hits), BF16),
        ]
    )
    packs = gather_small(pack)

    block_shape = (blocks, block_rows, width)
    tile_scratch = pltpu.VMEM(edge_tiles.shape, BF16)
    group_sems = pltpu.SemaphoreType.DMA((groups,))
    window_scratch = pltpu.VMEM((PIECES * blocks + 1, block_rows, width), BF16)
    blocked = jax.ShapeDtypeStruct(block_shape, BF16)
    head = jax.ShapeDtypeStruct((cut, block_rows, width), BF16)
    tail = jax.ShapeDtypeStruct((blocks - cut, block_rows, width), BF16)
    back_head = jax.ShapeDtypeStruct((back_cut, block_rows, width), BF16)
    back_tail = jax.ShapeDtypeStruct((blocks - back_cut, block_rows, width), BF16)
    slots_in = (place, src_blocks, live_slots)

    latents_0, agg_0, hidden_0, latents_1, new_a, new_b = pl.pallas_call(
        first_layer_kernel,
        out_shape=(blocked,) * 4 + (head, tail),
        in_specs=[smem()] * 3 + [in_hbm()] + [vmem()] * 11,
        out_specs=(vmem(),) * 6,
        scratch_shapes=[tile_scratch, window_scratch, group_sems],
        compiler_params=params(56),
        name="first_layer",
    )(*slots_in, edge_tiles, *packs, w_enc, layer_table, w_self, w_agg, w_out)

    held_codes = jnp.stack([each[feats + 1] for each in (*packs[1:4], jnp.where(sends_pair, packs[5], packs[4]))])
    held_codes = after(held_codes, new_a).astype(jnp.int32).reshape(PIECES - 1, 2, 2 * triplets)
    own_codes = jnp.concatenate([positive_hits, negative_hits]).reshape(1, 2 * triplets)
    named = jnp.concatenate([own_codes, (held_codes[:, 0] << 7) + held_codes[:, 1]]).reshape(PIECES, 2, triplets)
    mine = (named >> row_bits) == place[7 : 7 + PIECES, None, None]
    numbers = jnp.arange(PIECES * triplets, dtype=jnp.int32).reshape(PIECES, 1, triplets)
    coded = jnp.where(mine, (numbers << row_bits) | (named & (hits - 1)), (PIECES * triplets) << row_bits)
    lists = lax.sort(coded.reshape(2 * PIECES, triplets).T, dimension=0, is_stable=False).T.reshape(-1)
    counts = jnp.sum(mine.astype(jnp.int32), axis=2).reshape(-1)

    pair_a = send(new_a, pair_links(count))
    late_b = after(new_b, lists, counts)
    pair_b = send(late_b, pair_links(count))
    cross_b = send(late_b, cross_links(count))
    other_a = send(new_a, core_links(count))
    other_b = send(new_b, core_links(count))
    pair_a = after(pair_a, lists, counts)
    cross_a = send(pair_a, relay_links(count))
    extra_pa = send(pair_a, core_links(count))
    extra_pb = send(pair_b, core_links(count))
    extra_cb = send(cross_b, core_links(count))
    extra_ca = send(cross_a, core_links(count))

    agg_1, hidden_1, latents_2 = pl.pallas_call(
        next_layer_kernel,
        out_shape=(blocked,) * 3,
        in_specs=[smem()] * 3 + [kept_in_hbm()] + [in_hbm()] * 12 + [vmem()] * 3,
        out_specs=(vmem(),) * 3,
        scratch_shapes=[
            tile_scratch, window_scratch, group_sems, pltpu.SemaphoreType.DMA((2 * PIECES,)),
        ],
        compiler_params=params(26),
        name="next_layer",
    )(
        *slots_in, edge_tiles, new_a, new_b, pair_a, pair_b, cross_a, cross_b, other_a, other_b,
        extra_pa, extra_pb, extra_ca, extra_cb, w_self, w_agg, w_out,
    )

    triplet_rows = jax.ShapeDtypeStruct((triplets, width), BF16)
    wide_rows = jax.ShapeDtypeStruct((triplets, width), F32)
    hit_rows = pltpu.VMEM((hits, width), F32)
    gap_own, *gap_pieces = pl.pallas_call(
        lambda *refs: gather_kernel(row_bits, *refs),
        out_shape=(triplet_rows,) * 5,
        in_specs=[smem()] * 2 + [vmem()],
        out_specs=(vmem(),) * 5,
        scratch_shapes=[
            hit_rows,
            pltpu.VMEM((PIECES * triplets + 8, width), F32),
            pltpu.VMEM((PIECES * triplets + 8, width), F32),
        ],
        compiler_params=params(18),
        name="gather_rows",
    )(lists, counts, latents_2)
    gaps, joined = return_small(*gap_pieces, sends_pair)

    anchor_rows = pl.pallas_call(
        anchor_kernel,
        out_shape=wide_rows,
        in_specs=[smem(), vmem()],
        out_specs=vmem(),
        scratch_shapes=[hit_rows],
        compiler_params=params(10),
        name="anchor_rows",
    )(anchor_hits, after(latents_2, *joined))

    loss_part, weighted, weighted_b, anchor_grad = pl.pallas_call(
        score_kernel,
        out_shape=(
            jax.ShapeDtypeStruct((8, width), F32),
            jax.ShapeDtypeStruct((triplets + 8, width), F32),
            triplet_rows,
            wide_rows,
        ),
        in_specs=[vmem()] * 5,
        out_specs=(vmem(),) * 4,
        compiler_params=params(10),
        name="scores",
    )(gap_own, *gaps, anchor_rows)

    own_rows = pl.pallas_call(
        lambda *refs: own_rows_kernel(row_bits, *refs),
        out_shape=jax.ShapeDtypeStruct((hits, width), F32),
        in_specs=[smem()] * 3 + [vmem()] * 2,
        out_specs=vmem(),
        scratch_shapes=[hit_rows] * 3,
        compiler_params=params(18),
        name="own_rows",
    )(lists, counts, anchor_hits, weighted, anchor_grad)
    weighted_window = gather_small(weighted_b, own_rows)

    wide_blocked = jax.ShapeDtypeStruct(block_shape, F32)
    spread_scratch = pltpu.VMEM((PIECES * blocks + 1, width, block_rows), F32)
    grads_scratch = pltpu.VMEM((3, width, width), F32)
    rows_0, rows_1 = 3 * width + 2 * PACK_ROWS, 3 * width + 16
    half_0 = jax.ShapeDtypeStruct((rows_0 // 2, width), F32)
    half_1 = jax.ShapeDtypeStruct((rows_1 // 2, width), F32)
    own_1, ret_pa, ret_pb, ret_ca, ret_cb, ret_other, ret_ea, ret_eb, kept_1, given_1 = pl.pallas_call(
        lambda *refs: contrast_layer_kernel(row_bits, *refs),
        out_shape=(wide_blocked,)
        + (back_head, back_tail) * 2
        + (blocked, back_head, back_tail, half_1, half_1),
        in_specs=[smem()] * 5 + [in_hbm()] + [vmem()] * 13,
        out_specs=(vmem(),) * 10,
        scratch_shapes=[
            tile_scratch, spread_scratch, grads_scratch, pltpu.VMEM((rows_1, width), F32),
            pltpu.VMEM((4 * triplets + 8, width), F32), hit_rows, hit_rows, hit_rows, hit_rows, group_sems,
        ],
        compiler_params=params(52),
        name="contrast_layer",
    )(
        *slots_in, lists, counts, edge_tiles,
        own_rows, *weighted_window[1:], loss_part,
        hidden_1, latents_1, agg_1, w_self, w_agg, w_out,
    )

    got_a = send(ret_ea, core_links(count))
    got_b = send(ret_eb, core_links(count))
    from_other = send(ret_other, core_links(count))
    ret_pa, ret_ca = join_extra(ret_pa, ret_ca, got_a, sends_pair)
    relayed = send(ret_ca, turned(relay_links(count)))
    ret_pb, ret_cb = join_extra(ret_pb, ret_cb, got_b, sends_pair)
    from_pair_b = send(ret_pb, pair_links(count))
    from_cross_b = send(ret_cb, turned(cross_links(count)))
    ret_pa = (ret_pa.astype(F32) + relayed.astype(F32)).astype(BF16)
    part_1 = first_sums(kept_1, given_1)
    from_pair_a = send(after(ret_pa, from_pair_b, from_cross_b, part_1), pair_links(count))
    part_1, back_1 = last_sums(part_1)
    own_1 = after(own_1, part_1, back_1)

    kept_0, given_0 = pl.pallas_call(
        last_layer_kernel,
        out_shape=(half_0, half_0),
        in_specs=[smem()] * 3 + [in_hbm()] + [vmem()] * 19,
        out_specs=(vmem(),) * 2,
        scratch_shapes=[
            tile_scratch, spread_scratch, grads_scratch, pltpu.VMEM((rows_0, width), F32),
            pltpu.VMEM(block_shape, F32), group_sems,
        ],
        compiler_params=params(42),
        name="last_layer",
    )(
        *slots_in, edge_tiles, own_1, from_pair_a, from_pair_b, from_cross_b, from_other,
        hidden_0, latents_0, agg_0, w_self, w_agg, w_out, w_enc, layer_table, *packs,
    )
    part_0, back_0 = last_sums(first_sums(kept_0, given_0))

    square = jax.ShapeDtypeStruct((layers, width, width), F32)
    return pl.pallas_call(
        lambda *refs: result_kernel(1.0 / (triplets * count), feats, *refs),
        out_shape=(
            jax.ShapeDtypeStruct((1,), F32),
            jax.ShapeDtypeStruct((feats, width), F32),
            jax.ShapeDtypeStruct((PACK_ROWS, width), F32),
            square, square, square,
        ),
        in_specs=[smem()] + [vmem()] * 4,
        out_specs=(smem(),) + (vmem(),) * 5,
        scratch_shapes=[pltpu.VMEM((rows_0, width), F32), pltpu.VMEM((rows_1, width), F32)],
        compiler_params=params(6),
        name="results",
    )(place, part_0, back_0, part_1, back_1)


def solution(mesh):
    both = ("event", "phi")
    in_specs = (
        P(None, both), P(both), P(both, None, None, None), P(both, None), P(both),
        P(both), P(both), P(both), P(), P(), P(), P(), P(),
    )
    out_specs = (
        P("event"), P("event", None), P("event", None),
        P("event", None, None), P("event", None, None), P("event", None, None),
    )
    return jax.shard_map(body, mesh=mesh, in_specs=in_specs, out_specs=out_specs, check_vma=False)
```

```python
import math

import jax
import jax.numpy as jnp
from jax import lax
from jax.experimental import pallas as pl
from jax.experimental.pallas import tpu as pltpu
from jax.sharding import PartitionSpec as P

loss_divisor = 64.0
F32 = jnp.float32
BF16 = jnp.bfloat16
PACK_ROWS = 16
GROUP = 16

PIECES = 5


def vmem():
    return pl.BlockSpec(memory_space=pltpu.VMEM)


def smem():
    return pl.BlockSpec(memory_space=pltpu.SMEM)


def in_hbm():
    return pl.BlockSpec(memory_space=pl.ANY)


def kept_in_hbm():
    return pl.BlockSpec(memory_space=pltpu.HBM)


def params(mebibytes):
    return pltpu.CompilerParams(vmem_limit_bytes=mebibytes * 1024 * 1024)


def cost(microseconds):
    return pl.CostEstimate(flops=0, transcendentals=0, bytes_accessed=int(microseconds * 3.6e6))


def dot_nn(left, right):
    return lax.dot_general(left, right, (((1,), (0,)), ((), ())), preferred_element_type=F32)


def dot_tn(left, right):
    return lax.dot_general(left, right, (((0,), (0,)), ((), ())), preferred_element_type=F32)


def dot_nt(left, right):
    return lax.dot_general(left, right, (((1,), (1,)), ((), ())), preferred_element_type=F32)


def second(p):
    return (p >> 1) & 1


def pair_links(count):
    return [(p, p ^ 2) for p in range(count)]


def cross_links(count):
    return [(p, (p + (2 if second(p) else -2)) % count) for p in range(count)]


def relay_links(count):
    return [(p, (p + (-4 if second(p) else 4)) % count) for p in range(count)]


def core_links(count):
    return [(p, p ^ 1) for p in range(count)]


def turned(links):
    return [(target, source) for source, target in links]


def place_table():
    rows = []
    for kind in range(4):
        odd, on_second = kind & 1, kind >> 1
        pair, core = (-2 if on_second else 2), (-1 if odd else 1)
        offsets = [0, pair, -pair, core, -core]
        rows.append(
            [odd, on_second]
            + [offsets.index(part - 2) for part in range(PIECES)]
            + [2 - offset for offset in offsets]
            + [0] * 4
        )
    return jnp.array(rows, jnp.int32)


def send(value, links):
    return lax.ppermute(value, "phi", links)


def after(value, *earlier):
    return lax.optimization_barrier((value, *earlier))[0]


def gather_small(value, meanwhile=None):
    count = lax.axis_size("phi")
    pair = send(value, pair_links(count))
    cross = send(value, cross_links(count))
    other = send(value, core_links(count))
    if meanwhile is not None:
        pair = after(pair, meanwhile)
    extra_p = send(pair, core_links(count))
    extra_c = send(cross, core_links(count))
    return (value, pair, cross, other, extra_p, extra_c)


def join_extra(pair, cross, received, sends_pair):
    to_pair = jnp.where(sends_pair, received, jnp.zeros_like(received))
    to_cross = jnp.where(sends_pair, jnp.zeros_like(received), received)
    pair = (pair.astype(F32) + to_pair.astype(F32)).astype(BF16)
    cross = (cross.astype(F32) + to_cross.astype(F32)).astype(BF16)
    return pair, cross


def return_small(pair, cross, other, extra, sends_pair):
    count = lax.axis_size("phi")
    received = send(extra, core_links(count))
    from_other = send(other, core_links(count))
    pair, cross = join_extra(pair, cross, received, sends_pair)
    from_pair = send(pair, pair_links(count))
    from_cross = send(cross, turned(cross_links(count)))
    return (from_pair, from_cross, from_other), (pair, cross)


def first_sums(kept, given):
    count = lax.axis_size("phi")
    part = kept + send(given, core_links(count))
    if count & (count - 1) == 0:
        part = part + send(part, pair_links(count))
    return part


def last_sums(part):
    count = lax.axis_size("phi")
    if count & (count - 1):
        moved = part
        for _ in range(count // 2 - 1):
            moved = send(moved, [(p, (p + 2) % count) for p in range(count)])
            part = part + moved
    else:
        step = 4
        while step < count:
            part = part + send(part, [(p, p ^ step) for p in range(count)])
            step *= 2
    return part, send(part, core_links(count))


def fetch_tiles(tiles_hbm, tiles, sems, groups):
    for g in range(groups):
        pltpu.make_async_copy(
            tiles_hbm.at[pl.ds(g * GROUP, GROUP)], tiles.at[pl.ds(g * GROUP, GROUP)], sems.at[g]
        ).start()


def await_tiles(tiles_hbm, tiles, sems, g):
    first = pl.multiple_of(g * GROUP, GROUP)
    pltpu.make_async_copy(
        tiles_hbm.at[pl.ds(first, GROUP)], tiles.at[pl.ds(first, GROUP)], sems.at[g]
    ).wait()


def extra_of(place, from_pair, from_cross):
    return jnp.where(place[0] != place[1], from_pair, from_cross)


def encode_operand(place, *pack_refs):
    pieces = [pack_ref[...].astype(F32) for pack_ref in pack_refs]
    rows = pieces[0] if len(pieces) == 1 else extra_of(place, *pieces)
    ids = rows[12:13, :]
    layers = lax.broadcasted_iota(jnp.int32, rows.shape, 0).astype(F32)
    onehot = (layers == ids).astype(BF16)
    return jnp.concatenate([rows.astype(BF16), onehot], axis=0)


def block_of(place, src, live, b, s, blocks, slots):
    bits = blocks.bit_length() - 1
    named = src[b * slots + s]
    block = (place[2 + (named >> bits)] << bits) + (named & (blocks - 1))
    return jnp.where(s < live[b], block, PIECES * blocks)


def forward_group(layer, g, place, src, live, tiles, window, w_self, w_agg, w_out, agg_ref, hidden_t_ref, new_ref):
    blocks, slots = tiles.shape[0], tiles.shape[1]
    sums = []
    for q in range(GROUP):
        b = g * GROUP + q
        left = jnp.concatenate([tiles[b, s] for s in range(slots)], axis=1)
        right = [window[block_of(place, src, live, b, s, blocks, slots)] for s in range(slots)]
        sums.append(dot_nn(left, jnp.concatenate(right, axis=0)))
    first = pl.multiple_of(g * GROUP, GROUP)
    agg = jnp.concatenate(sums, axis=0).astype(BF16)
    rows, width = agg.shape
    here = window[pl.ds(first, GROUP)].reshape(rows, width)
    activation = dot_nn(here, w_self[layer]) + dot_nn(agg, w_agg[layer])
    hidden = jnp.maximum(activation, 0.0)
    hidden_b = hidden.astype(BF16)
    updated = (here.astype(F32) + dot_nn(hidden_b, w_out[layer])).astype(BF16)
    agg_ref[pl.ds(first, GROUP)] = agg.reshape(GROUP, rows // GROUP, width)
    new_ref[pl.ds(first, GROUP)] = updated.reshape(GROUP, rows // GROUP, width)
    for q in range(GROUP):
        block = hidden[q * (rows // GROUP) : (q + 1) * (rows // GROUP)]
        hidden_t_ref[first + q] = block.T.astype(BF16)


def input_weights(w_enc, layer_table):
    feats, width = w_enc.shape
    gap = jnp.zeros((PACK_ROWS - feats, width), F32)
    return jnp.concatenate([w_enc[...].astype(F32), gap, layer_table[...].astype(F32)], axis=0).astype(BF16)


def first_layer_kernel(
    place, src, live, tiles_hbm, p0, p1, p2, p3, p4, p5, w_enc, layer_table, w_self, w_agg, w_out,
    own_ref, agg_ref, hidden_t_ref, new_ref, new_a_ref, new_b_ref, tiles, window, sems,
):
    blocks, block_rows = tiles.shape[0], tiles.shape[2]
    groups = blocks // GROUP
    fetch_tiles(tiles_hbm, tiles, sems, groups)
    w_in = input_weights(w_enc, layer_table)
    for k, pack in enumerate(((p0,), (p1,), (p2,), (p3,), (p4, p5))):
        latents = jnp.tanh(dot_tn(encode_operand(place, *pack), w_in)).astype(BF16)
        window[pl.ds(k * blocks, blocks)] = latents.reshape(blocks, block_rows, latents.shape[1])
    window[PIECES * blocks] = jnp.zeros(window.shape[1:], BF16)
    own_ref[...] = window[pl.ds(0, blocks)]

    def step(g, carry):
        await_tiles(tiles_hbm, tiles, sems, g)
        forward_group(0, g, place, src, live, tiles, window, w_self, w_agg, w_out, agg_ref, hidden_t_ref, new_ref)
        return carry

    lax.fori_loop(0, groups, step, 0)
    cut = new_a_ref.shape[0]
    new_a_ref[...] = new_ref[pl.ds(0, cut)]
    new_b_ref[...] = new_ref[pl.ds(cut, blocks - cut)]


def next_layer_kernel(
    place, src, live, tiles_hbm, own_a, own_b, pair_a, pair_b, cross_a, cross_b, other_a, other_b,
    extra_pa, extra_pb, extra_ca, extra_cb, w_self, w_agg, w_out,
    agg_ref, hidden_t_ref, new_ref, tiles, window, sems, piece_sems,
):
    blocks, cut = tiles.shape[0], own_a.shape[0]
    groups = blocks // GROUP

    def copies(pieces, first):
        for k, (head, tail) in enumerate(pieces):
            start = (first + k) * blocks
            yield pltpu.make_async_copy(
                head, window.at[pl.ds(start, cut)], piece_sems.at[2 * (first + k)]
            )
            yield pltpu.make_async_copy(
                tail, window.at[pl.ds(start + cut, blocks - cut)], piece_sems.at[2 * (first + k) + 1]
            )

    plain = list(copies([(own_a, own_b), (pair_a, pair_b), (cross_a, cross_b), (other_a, other_b)], 0))
    for copy in plain:
        copy.start()

    def extra_is_pair(do):
        @pl.when(place[0] != place[1])
        def _():
            for copy in copies([(extra_pa, extra_pb)], 4):
                do(copy)

        @pl.when(place[0] == place[1])
        def _():
            for copy in copies([(extra_ca, extra_cb)], 4):
                do(copy)

    extra_is_pair(lambda copy: copy.start())
    fetch_tiles(tiles_hbm, tiles, sems, groups)
    window[PIECES * blocks] = jnp.zeros(window.shape[1:], BF16)
    for copy in plain:
        copy.wait()
    extra_is_pair(lambda copy: copy.wait())

    def step(g, carry):
        await_tiles(tiles_hbm, tiles, sems, g)
        forward_group(1, g, place, src, live, tiles, window, w_self, w_agg, w_out, agg_ref, hidden_t_ref, new_ref)
        return carry

    lax.fori_loop(0, groups, step, 0)


def pair_of_lists(lists, counts, k, triplets):
    longest = jnp.maximum(counts[2 * k], counts[2 * k + 1])
    return 2 * k * triplets, (2 * k + 1) * triplets, (longest + 7) >> 3


def gather_kernel(row_bits, lists, counts, latents, d0, d1, d2, d3, d4, wide, negative, positive):
    low = (1 << row_bits) - 1
    triplets = d0.shape[0]
    blocks, block_rows, width = latents.shape
    wide[...] = latents[...].reshape(blocks * block_rows, width).astype(F32)
    negative[...] = jnp.zeros(negative.shape, F32)
    positive[...] = jnp.zeros(positive.shape, F32)
    for k, out in enumerate((d0, d1, d2, d3, d4)):
        first_p, first_n, eights = pair_of_lists(lists, counts, k, triplets)

        def pick(i, carry, first_p=first_p, first_n=first_n):
            for u in range(8):
                code_n = lists[first_n + i * 8 + u]
                code_p = lists[first_p + i * 8 + u]
                negative[pl.ds(code_n >> row_bits, 1), :] = wide[pl.ds(code_n & low, 1), :]
                positive[pl.ds(code_p >> row_bits, 1), :] = wide[pl.ds(code_p & low, 1), :]
            return carry

        lax.fori_loop(0, eights, pick, 0)
        here = pl.ds(k * triplets, triplets)
        out[...] = (negative[here, :] - positive[here, :]).astype(BF16)


def anchor_kernel(anchors, latents, anchor_ref, wide):
    blocks, block_rows, width = latents.shape
    wide[...] = latents[...].reshape(blocks * block_rows, width).astype(F32)

    def pick(i, carry):
        for u in range(8):
            anchor_ref[pl.ds(i * 8 + u, 1), :] = wide[pl.ds(anchors[i * 8 + u], 1), :]
        return carry

    lax.fori_loop(0, anchor_ref.shape[0] // 8, pick, 0)


def own_rows_kernel(row_bits, lists, counts, anchors, weighted, anchor_grad, rows_ref, rows_b, rows_c, rows_d):
    low = (1 << row_bits) - 1
    triplets = anchor_grad.shape[0]
    held = (rows_ref, rows_b, rows_c, rows_d)
    for rows in held:
        rows[...] = jnp.zeros(rows.shape, F32)

    def put_anchor(i, carry):
        for u in range(8):
            here = pl.ds(anchors[i * 8 + u], 1)
            held[u % 4][here, :] += anchor_grad[pl.ds(i * 8 + u, 1), :]
        return carry

    lax.fori_loop(0, triplets // 8, put_anchor, 0)
    first_p, first_n, eights = pair_of_lists(lists, counts, 0, triplets)

    def put(i, carry):
        for u in range(8):
            code_n = lists[first_n + i * 8 + u]
            code_p = lists[first_p + i * 8 + u]
            from_n = pl.ds(jnp.minimum(code_n >> row_bits, triplets), 1)
            from_p = pl.ds(jnp.minimum(code_p >> row_bits, triplets), 1)
            held[u % 2][pl.ds(code_n & low, 1), :] += weighted[from_n, :]
            held[2 + u % 2][pl.ds(code_p & low, 1), :] -= weighted[from_p, :]
        return carry

    lax.fori_loop(0, eights, put, 0)
    rows_ref[...] = (rows_ref[...] + rows_b[...]) + (rows_c[...] + rows_d[...])


def score_kernel(own, pair, cross, other, anchors, loss_ref, weighted_ref, weighted_b_ref, anchor_grad_ref):
    triplets, width = anchors.shape
    inv_root = 1.0 / math.sqrt(width)
    scale = 1.0 / (loss_divisor * math.sqrt(width))
    chunk = 128
    loss = jnp.zeros((chunk, 1), F32)
    weighted_ref[pl.ds(triplets, 8), :] = jnp.zeros((8, width), F32)
    for c in range(triplets // chunk):
        here = pl.ds(c * chunk, chunk)
        gap = own[here, :].astype(F32) + pair[here, :].astype(F32)
        gap = gap + cross[here, :].astype(F32) + other[here, :].astype(F32)
        anchor = anchors[here, :]
        score = jnp.sum(anchor * gap, axis=1, keepdims=True) * inv_root
        loss = loss + jnp.maximum(score, 0.0) + jnp.log1p(jnp.exp(-jnp.abs(score)))
        coef = scale / (1.0 + jnp.exp(-score))
        weighted = coef * anchor
        weighted_ref[here, :] = weighted
        weighted_b_ref[here, :] = weighted.astype(BF16)
        anchor_grad_ref[here, :] = coef * gap
    loss_ref[...] = jnp.broadcast_to(jnp.sum(loss, axis=0, keepdims=True), loss_ref.shape)


def backward_group(layer, g, place, src, live, tiles, gradient, hidden_t, latents, agg, w_self, w_agg, w_out, grads, spread):
    blocks, slots = tiles.shape[0], tiles.shape[1]
    first = pl.multiple_of(g * GROUP, GROUP)
    rows, width = tiles.shape[2], latents.shape[2]
    upstream = gradient.astype(BF16)
    hidden = jnp.concatenate([hidden_t[first + q] for q in range(GROUP)], axis=1)
    grads[2] += dot_nt(hidden, upstream)
    hidden_grad = dot_nn(w_out[layer], upstream)
    act_grad = jnp.where(hidden > 0, hidden_grad, 0.0).astype(BF16)
    grads[0] += dot_nn(act_grad, latents[pl.ds(first, GROUP)].reshape(GROUP * rows, width))
    grads[1] += dot_nn(act_grad, agg[pl.ds(first, GROUP)].reshape(GROUP * rows, width))
    agg_grad = dot_nn(w_agg[layer], act_grad).astype(BF16)
    direct = gradient + dot_nn(w_self[layer], act_grad)
    for q in range(GROUP):
        b = g * GROUP + q
        spread[b] += direct[:, q * rows : (q + 1) * rows]
        right = jnp.concatenate([tiles[b, s] for s in range(slots)], axis=1)
        parts = dot_nn(agg_grad[:, q * rows : (q + 1) * rows], right)
        for s in range(slots):
            spread[block_of(place, src, live, b, s, blocks, slots)] += parts[:, s * rows : (s + 1) * rows]


def put_halves(place, whole, kept_ref, given_ref):
    half = kept_ref.shape[0]
    kept_ref[...] = whole[pl.ds(pl.multiple_of(place[0] * half, 8), half), :]
    given_ref[...] = whole[pl.ds(pl.multiple_of((1 - place[0]) * half, 8), half), :]


def put_grads(grads, whole):
    width = grads.shape[1]
    whole[pl.ds(0, width), :] = grads[0].T
    whole[pl.ds(width, width), :] = grads[1].T
    whole[pl.ds(2 * width, width), :] = grads[2]


def contrast_layer_kernel(
    row_bits, place, src, live, lists, counts, tiles_hbm,
    own_rows, e1, e2, e3, e4, e5, loss_part, hidden_t, latents, agg, w_self, w_agg, w_out,
    own_ref, pair_a_ref, pair_b_ref, cross_a_ref, cross_b_ref, other_ref, extra_a_ref, extra_b_ref,
    kept_ref, given_ref,
    tiles, spread, grads, whole, weighted, rows_a, rows_b, rows_c, rows_d, sems,
):
    low = (1 << row_bits) - 1
    blocks, block_rows = tiles.shape[0], tiles.shape[2]
    groups = blocks // GROUP
    triplets = e1.shape[0]
    fetch_tiles(tiles_hbm, tiles, sems, groups)
    held = (rows_a, rows_b, rows_c, rows_d)
    rows_a[...] = own_rows[...]
    for rows in held[1:]:
        rows[...] = jnp.zeros(rows.shape, F32)
    spread[...] = jnp.zeros(spread.shape, F32)
    grads[...] = jnp.zeros(grads.shape, F32)
    for k, piece in enumerate((e1, e2, e3)):
        weighted[pl.ds(k * triplets, triplets), :] = piece[...].astype(F32)
    weighted[pl.ds(3 * triplets, triplets), :] = extra_of(place, e4[...].astype(F32), e5[...].astype(F32))
    weighted[pl.ds(4 * triplets, 8), :] = jnp.zeros((8, weighted.shape[1]), F32)
    for k in range(1, PIECES):
        first_p, first_n, eights = pair_of_lists(lists, counts, k, triplets)

        def put(i, carry, first_p=first_p, first_n=first_n):
            for u in range(8):
                code_n = lists[first_n + i * 8 + u]
                code_p = lists[first_p + i * 8 + u]
                from_n = pl.ds((code_n >> row_bits) - triplets, 1)
                from_p = pl.ds((code_p >> row_bits) - triplets, 1)
                held_n, held_p = held[u % 2], held[2 + u % 2]
                held_n[pl.ds(code_n & low, 1), :] += weighted[from_n, :]
                held_p[pl.ds(code_p & low, 1), :] -= weighted[from_p, :]
            return carry

        lax.fori_loop(0, eights, put, 0)

    def step(g, carry):
        pieces = []
        for q in range(GROUP):
            here = pl.ds(pl.multiple_of((g * GROUP + q) * block_rows, block_rows), block_rows)
            block = (rows_a[here, :] + rows_b[here, :]) + (rows_c[here, :] + rows_d[here, :])
            pieces.append(block.T)
        await_tiles(tiles_hbm, tiles, sems, g)
        backward_group(1, g, place, src, live, tiles, jnp.concatenate(pieces, axis=1), hidden_t, latents, agg,
                       w_self, w_agg, w_out, grads, spread)
        return carry

    lax.fori_loop(0, groups, step, 0)
    cut = pair_a_ref.shape[0]
    own_ref[...] = spread[pl.ds(0, blocks)]
    for k, (head, tail) in enumerate(((pair_a_ref, pair_b_ref), (cross_a_ref, cross_b_ref))):
        head[...] = spread[pl.ds((k + 1) * blocks, cut)].astype(BF16)
        tail[...] = spread[pl.ds((k + 1) * blocks + cut, blocks - cut)].astype(BF16)
    other_ref[...] = spread[pl.ds(3 * blocks, blocks)].astype(BF16)
    extra_a_ref[...] = spread[pl.ds(4 * blocks, cut)].astype(BF16)
    extra_b_ref[...] = spread[pl.ds(4 * blocks + cut, blocks - cut)].astype(BF16)
    put_grads(grads, whole)
    top = 3 * grads.shape[1]
    whole[pl.ds(top, 8), :] = loss_part[...]
    whole[pl.ds(top + 8, 8), :] = jnp.zeros((8, whole.shape[1]), F32)
    put_halves(place, whole, kept_ref, given_ref)


def last_layer_kernel(
    place, src, live, tiles_hbm, own, pair_a, pair_b, cross_b, other, hidden_t, latents, agg,
    w_self, w_agg, w_out, w_enc, layer_table, p0, p1, p2, p3, p4, p5,
    kept_ref, given_ref, tiles, spread, grads, whole, received, sems,
):
    blocks = tiles.shape[0]
    groups = blocks // GROUP
    cut = pair_a.shape[0]
    fetch_tiles(tiles_hbm, tiles, sems, groups)
    spread[...] = jnp.zeros(spread.shape, F32)
    grads[...] = jnp.zeros(grads.shape, F32)
    head, tail = pl.ds(0, cut), pl.ds(cut, blocks - cut)
    received[head] = own[head] + other[head].astype(F32) + pair_a[...].astype(F32)
    from_far = pair_b[...].astype(F32) + cross_b[...].astype(F32)
    received[tail] = own[tail] + other[tail].astype(F32) + from_far

    def step(g, carry):
        pieces = [received[g * GROUP + q] for q in range(GROUP)]
        await_tiles(tiles_hbm, tiles, sems, g)
        backward_group(0, g, place, src, live, tiles, jnp.concatenate(pieces, axis=1), hidden_t, latents, agg,
                       w_self, w_agg, w_out, grads, spread)
        return carry

    lax.fori_loop(0, groups, step, 0)
    w_in = input_weights(w_enc, layer_table)
    grad_in = jnp.zeros(w_in.shape, F32)
    for k, pack in enumerate(((p0,), (p1,), (p2,), (p3,), (p4, p5))):
        operand = encode_operand(place, *pack)
        squashed = jnp.tanh(dot_tn(w_in, operand))
        gradient = jnp.concatenate([spread[k * blocks + q] for q in range(blocks)], axis=1)
        encoded_grad = (gradient * (1.0 - squashed * squashed)).astype(BF16)
        grad_in = grad_in + dot_nt(operand, encoded_grad)
    put_grads(grads, whole)
    whole[pl.ds(3 * grads.shape[1], 2 * PACK_ROWS), :] = grad_in
    put_halves(place, whole, kept_ref, given_ref)


def result_kernel(
    scale, feats, place, part_0, back_0, part_1, back_1,
    loss_ref, enc_ref, table_ref, self_ref, agg_ref, out_ref, whole_0, whole_1,
):
    for whole, part, back in ((whole_0, part_0, back_0), (whole_1, part_1, back_1)):
        half = part.shape[0]
        whole[pl.ds(pl.multiple_of(place[0] * half, 8), half), :] = part[...]
        whole[pl.ds(pl.multiple_of((1 - place[0]) * half, 8), half), :] = back[...]
    width = whole_0.shape[1]
    top = 3 * width
    for layer, whole in enumerate((whole_0, whole_1)):
        for k, out in enumerate((self_ref, agg_ref, out_ref)):
            out[layer] = whole[pl.ds(k * width, width), :]
    enc_ref[...] = whole_0[pl.ds(top, feats), :]
    table_ref[...] = whole_0[pl.ds(top + PACK_ROWS, PACK_ROWS), :]
    loss_ref[0] = jnp.max(whole_1[pl.ds(top, 8), :]) * scale


def body(
    hit_feats, layer_ids, edge_tiles, src_blocks, live_slots,
    anchor_hits, positive_hits, negative_hits, w_enc, layer_table, w_self, w_agg, w_out,
):
    blocks, slots, block_rows = edge_tiles.shape[0], edge_tiles.shape[1], edge_tiles.shape[2]
    feats, width = w_enc.shape
    kinds = layer_table.shape[0]
    hits = blocks * block_rows
    triplets = anchor_hits.shape[0]
    layers = w_self.shape[0]
    row_bits = hits.bit_length() - 1
    count = lax.axis_size("phi")
    assert hits == 1 << row_bits and blocks & (blocks - 1) == 0 and blocks % GROUP == 0
    assert feats < PACK_ROWS - 3 and kinds == PACK_ROWS and layers == 2 and 4 * triplets == hits
    assert count % 4 == 0
    groups = blocks // GROUP
    cut, back_cut = blocks // 2, blocks * 11 // 16
    place = lax.dynamic_slice_in_dim(place_table(), lax.axis_index("phi") & 3, 1, 0).reshape(-1)
    sends_pair = place[0] == place[1]

    codes = jnp.concatenate([positive_hits, negative_hits])
    codes = jnp.concatenate([codes >> 7, codes & 127])
    pack = jnp.concatenate(
        [
            hit_feats,
            layer_ids.astype(BF16)[None, :],
            codes.astype(BF16)[None, :],
            jnp.zeros((PACK_ROWS - feats - 2, hits), BF16),
        ]
    )
    src_flat = src_blocks.reshape(-1)
    packs = gather_small(pack, src_flat)

    block_shape = (blocks, block_rows, width)
    tile_scratch = pltpu.VMEM(edge_tiles.shape, BF16)
    group_sems = pltpu.SemaphoreType.DMA((groups,))
    window_scratch = pltpu.VMEM((PIECES * blocks + 1, block_rows, width), BF16)
    blocked = jax.ShapeDtypeStruct(block_shape, BF16)
    head = jax.ShapeDtypeStruct((cut, block_rows, width), BF16)
    tail = jax.ShapeDtypeStruct((blocks - cut, block_rows, width), BF16)
    back_head = jax.ShapeDtypeStruct((back_cut, block_rows, width), BF16)
    back_tail = jax.ShapeDtypeStruct((blocks - back_cut, block_rows, width), BF16)
    slots_in = (place, src_flat, live_slots)

    latents_0, agg_0, hidden_0, latents_1, new_a, new_b = pl.pallas_call(
        first_layer_kernel,
        out_shape=(blocked,) * 4 + (head, tail),
        in_specs=[smem()] * 3 + [in_hbm()] + [vmem()] * 11,
        out_specs=(vmem(),) * 6,
        scratch_shapes=[tile_scratch, window_scratch, group_sems],
        compiler_params=params(56),
        name="first_layer",
    )(*slots_in, edge_tiles, *packs, w_enc, layer_table, w_self, w_agg, w_out)

    held_codes = jnp.stack([each[feats + 1] for each in (*packs[1:4], jnp.where(sends_pair, packs[5], packs[4]))])
    held_codes = after(held_codes, new_a).astype(jnp.int32).reshape(PIECES - 1, 2, 2 * triplets)
    own_codes = jnp.concatenate([positive_hits, negative_hits]).reshape(1, 2 * triplets)
    named = jnp.concatenate([own_codes, (held_codes[:, 0] << 7) + held_codes[:, 1]]).reshape(PIECES, 2, triplets)
    mine = (named >> row_bits) == place[7 : 7 + PIECES, None, None]
    numbers = jnp.arange(PIECES * triplets, dtype=jnp.int32).reshape(PIECES, 1, triplets)
    coded = jnp.where(mine, (numbers << row_bits) | (named & (hits - 1)), (PIECES * triplets) << row_bits)
    lists = lax.sort(coded.reshape(2 * PIECES, triplets).T, dimension=0, is_stable=False).T.reshape(-1)
    counts = jnp.sum(mine.astype(jnp.int32), axis=2).reshape(-1)

    pair_a = send(new_a, pair_links(count))
    late_b = after(new_b, lists, counts)
    pair_b = send(late_b, pair_links(count))
    cross_b = send(late_b, cross_links(count))
    other_a = send(new_a, core_links(count))
    other_b = send(new_b, core_links(count))
    pair_a = after(pair_a, lists, counts)
    cross_a = send(pair_a, relay_links(count))
    extra_pa = send(pair_a, core_links(count))
    extra_pb = send(pair_b, core_links(count))
    extra_cb = send(cross_b, core_links(count))
    extra_ca = send(cross_a, core_links(count))

    agg_1, hidden_1, latents_2 = pl.pallas_call(
        next_layer_kernel,
        out_shape=(blocked,) * 3,
        in_specs=[smem()] * 3 + [kept_in_hbm()] + [in_hbm()] * 12 + [vmem()] * 3,
        out_specs=(vmem(),) * 3,
        scratch_shapes=[
            tile_scratch, window_scratch, group_sems, pltpu.SemaphoreType.DMA((2 * PIECES,)),
        ],
        compiler_params=params(42),
        name="next_layer",
    )(
        *slots_in, edge_tiles, new_a, new_b, pair_a, pair_b, cross_a, cross_b, other_a, other_b,
        extra_pa, extra_pb, extra_ca, extra_cb, w_self, w_agg, w_out,
    )

    triplet_rows = jax.ShapeDtypeStruct((triplets, width), BF16)
    wide_rows = jax.ShapeDtypeStruct((triplets, width), F32)
    hit_rows = pltpu.VMEM((hits, width), F32)
    gap_own, *gap_pieces = pl.pallas_call(
        lambda *refs: gather_kernel(row_bits, *refs),
        out_shape=(triplet_rows,) * 5,
        in_specs=[smem()] * 2 + [vmem()],
        out_specs=(vmem(),) * 5,
        scratch_shapes=[
            hit_rows,
            pltpu.VMEM((PIECES * triplets + 8, width), F32),
            pltpu.VMEM((PIECES * triplets + 8, width), F32),
        ],
        compiler_params=params(18),
        name="gather_rows",
    )(lists, counts, latents_2)
    gaps, joined = return_small(*gap_pieces, sends_pair)

    anchor_rows = pl.pallas_call(
        anchor_kernel,
        out_shape=wide_rows,
        in_specs=[smem(), vmem()],
        out_specs=vmem(),
        scratch_shapes=[hit_rows],
        compiler_params=params(10),
        name="anchor_rows",
    )(anchor_hits, after(latents_2, *joined))

    loss_part, weighted, weighted_b, anchor_grad = pl.pallas_call(
        score_kernel,
        out_shape=(
            jax.ShapeDtypeStruct((8, width), F32),
            jax.ShapeDtypeStruct((triplets + 8, width), F32),
            triplet_rows,
            wide_rows,
        ),
        in_specs=[vmem()] * 5,
        out_specs=(vmem(),) * 4,
        compiler_params=params(10),
        name="scores",
    )(gap_own, *gaps, anchor_rows)

    own_rows = pl.pallas_call(
        lambda *refs: own_rows_kernel(row_bits, *refs),
        out_shape=jax.ShapeDtypeStruct((hits, width), F32),
        in_specs=[smem()] * 3 + [vmem()] * 2,
        out_specs=vmem(),
        scratch_shapes=[hit_rows] * 3,
        compiler_params=params(18),
        name="own_rows",
    )(lists, counts, anchor_hits, weighted, anchor_grad)
    weighted_window = gather_small(weighted_b, own_rows)

    wide_blocked = jax.ShapeDtypeStruct(block_shape, F32)
    spread_scratch = pltpu.VMEM((PIECES * blocks + 1, width, block_rows), F32)
    grads_scratch = pltpu.VMEM((3, width, width), F32)
    rows_0, rows_1 = 3 * width + 2 * PACK_ROWS, 3 * width + 16
    half_0 = jax.ShapeDtypeStruct((rows_0 // 2, width), F32)
    half_1 = jax.ShapeDtypeStruct((rows_1 // 2, width), F32)
    own_1, ret_pa, ret_pb, ret_ca, ret_cb, ret_other, ret_ea, ret_eb, kept_1, given_1 = pl.pallas_call(
        lambda *refs: contrast_layer_kernel(row_bits, *refs),
        out_shape=(wide_blocked,)
        + (back_head, back_tail) * 2
        + (blocked, back_head, back_tail, half_1, half_1),
        in_specs=[smem()] * 5 + [in_hbm()] + [vmem()] * 13,
        out_specs=(vmem(),) * 10,
        scratch_shapes=[
            tile_scratch, spread_scratch, grads_scratch, pltpu.VMEM((rows_1, width), F32),
            pltpu.VMEM((4 * triplets + 8, width), F32), hit_rows, hit_rows, hit_rows, hit_rows, group_sems,
        ],
        compiler_params=params(36),
        name="contrast_layer",
    )(
        *slots_in, lists, counts, edge_tiles,
        own_rows, *weighted_window[1:], loss_part,
        hidden_1, latents_1, agg_1, w_self, w_agg, w_out,
    )

    got_a = send(ret_ea, core_links(count))
    got_b = send(ret_eb, core_links(count))
    from_other = send(ret_other, core_links(count))
    ret_pa, ret_ca = join_extra(ret_pa, ret_ca, got_a, sends_pair)
    relayed = send(ret_ca, turned(relay_links(count)))
    ret_pb, ret_cb = join_extra(ret_pb, ret_cb, got_b, sends_pair)
    from_pair_b = send(ret_pb, pair_links(count))
    from_cross_b = send(ret_cb, turned(cross_links(count)))
    ret_pa = (ret_pa.astype(F32) + relayed.astype(F32)).astype(BF16)
    part_1 = first_sums(kept_1, given_1)
    from_pair_a = send(after(ret_pa, from_pair_b, part_1), pair_links(count))
    part_1, back_1 = last_sums(after(part_1, from_cross_b))
    own_1 = after(own_1, part_1, back_1)

    kept_0, given_0 = pl.pallas_call(
        last_layer_kernel,
        out_shape=(half_0, half_0),
        in_specs=[smem()] * 3 + [in_hbm()] + [vmem()] * 19,
        out_specs=(vmem(),) * 2,
        scratch_shapes=[
            tile_scratch, spread_scratch, grads_scratch, pltpu.VMEM((rows_0, width), F32),
            pltpu.VMEM(block_shape, F32), group_sems,
        ],
        compiler_params=params(30),
        name="last_layer",
    )(
        *slots_in, edge_tiles, own_1, from_pair_a, from_pair_b, from_cross_b, from_other,
        hidden_0, latents_0, agg_0, w_self, w_agg, w_out, w_enc, layer_table, *packs,
    )
    part_0, back_0 = last_sums(first_sums(kept_0, given_0))

    square = jax.ShapeDtypeStruct((layers, width, width), F32)
    return pl.pallas_call(
        lambda *refs: result_kernel(1.0 / (triplets * count), feats, *refs),
        out_shape=(
            jax.ShapeDtypeStruct((1,), F32),
            jax.ShapeDtypeStruct((feats, width), F32),
            jax.ShapeDtypeStruct((PACK_ROWS, width), F32),
            square, square, square,
        ),
        in_specs=[smem()] + [vmem()] * 4,
        out_specs=(smem(),) + (vmem(),) * 5,
        scratch_shapes=[pltpu.VMEM((rows_0, width), F32), pltpu.VMEM((rows_1, width), F32)],
        compiler_params=params(6),
        name="results",
    )(place, part_0, back_0, part_1, back_1)


def solution(mesh):
    both = ("event", "phi")
    in_specs = (
        P(None, both), P(both), P(both, None, None, None), P(both, None), P(both),
        P(both), P(both), P(both), P(), P(), P(), P(), P(),
    )
    out_specs = (
        P("event"), P("event", None), P("event", None),
        P("event", None, None), P("event", None, None), P("event", None, None),
    )
    return jax.shard_map(body, mesh=mesh, in_specs=in_specs, out_specs=out_specs, check_vma=False)
```

```python
import math

import jax
import jax.numpy as jnp
from jax import lax
from jax.experimental import pallas as pl
from jax.experimental.pallas import tpu as pltpu
from jax.sharding import PartitionSpec as P

loss_divisor = 64.0
F32 = jnp.float32
BF16 = jnp.bfloat16
PACK_ROWS = 16
GROUP = 16

PIECES = 5


def vmem():
    return pl.BlockSpec(memory_space=pltpu.VMEM)


def smem():
    return pl.BlockSpec(memory_space=pltpu.SMEM)


def in_hbm():
    return pl.BlockSpec(memory_space=pl.ANY)


def kept_in_hbm():
    return pl.BlockSpec(memory_space=pltpu.HBM)


def params(mebibytes):
    return pltpu.CompilerParams(vmem_limit_bytes=mebibytes * 1024 * 1024)


def cost(microseconds):
    return pl.CostEstimate(flops=0, transcendentals=0, bytes_accessed=int(microseconds * 3.6e6))


def dot_nn(left, right):
    return lax.dot_general(left, right, (((1,), (0,)), ((), ())), preferred_element_type=F32)


def dot_tn(left, right):
    return lax.dot_general(left, right, (((0,), (0,)), ((), ())), preferred_element_type=F32)


def dot_nt(left, right):
    return lax.dot_general(left, right, (((1,), (1,)), ((), ())), preferred_element_type=F32)


def second(p):
    return (p >> 1) & 1


def pair_links(count):
    return [(p, p ^ 2) for p in range(count)]


def cross_links(count):
    return [(p, (p + (2 if second(p) else -2)) % count) for p in range(count)]


def relay_links(count):
    return [(p, (p + (-4 if second(p) else 4)) % count) for p in range(count)]


def core_links(count):
    return [(p, p ^ 1) for p in range(count)]


def turned(links):
    return [(target, source) for source, target in links]


def place_table():
    rows = []
    for kind in range(4):
        odd, on_second = kind & 1, kind >> 1
        pair, core = (-2 if on_second else 2), (-1 if odd else 1)
        offsets = [0, pair, -pair, core, -core]
        rows.append(
            [odd, on_second]
            + [offsets.index(part - 2) for part in range(PIECES)]
            + [2 - offset for offset in offsets]
            + [0] * 4
        )
    return jnp.array(rows, jnp.int32)


def send(value, links):
    return lax.ppermute(value, "phi", links)


def after(value, *earlier):
    return lax.optimization_barrier((value, *earlier))[0]


def gather_small(value, meanwhile=None):
    count = lax.axis_size("phi")
    pair = send(value, pair_links(count))
    cross = send(value, cross_links(count))
    other = send(value, core_links(count))
    if meanwhile is not None:
        pair = after(pair, meanwhile)
    extra_p = send(pair, core_links(count))
    extra_c = send(cross, core_links(count))
    return (value, pair, cross, other, extra_p, extra_c)


def join_extra(pair, cross, received, sends_pair):
    to_pair = jnp.where(sends_pair, received, jnp.zeros_like(received))
    to_cross = jnp.where(sends_pair, jnp.zeros_like(received), received)
    pair = (pair.astype(F32) + to_pair.astype(F32)).astype(BF16)
    cross = (cross.astype(F32) + to_cross.astype(F32)).astype(BF16)
    return pair, cross


def return_small(pair, cross, other, extra, sends_pair):
    count = lax.axis_size("phi")
    received = send(extra, core_links(count))
    from_other = send(other, core_links(count))
    pair, cross = join_extra(pair, cross, received, sends_pair)
    from_pair = send(pair, pair_links(count))
    from_cross = send(cross, turned(cross_links(count)))
    return (from_pair, from_cross, from_other), (pair, cross)


def first_sums(kept, given):
    count = lax.axis_size("phi")
    part = kept + send(given, core_links(count))
    if count & (count - 1) == 0:
        part = part + send(part, pair_links(count))
    return part


def last_sums(part):
    count = lax.axis_size("phi")
    if count & (count - 1):
        moved = part
        for _ in range(count // 2 - 1):
            moved = send(moved, [(p, (p + 2) % count) for p in range(count)])
            part = part + moved
    else:
        step = 4
        while step < count:
            part = part + send(part, [(p, p ^ step) for p in range(count)])
            step *= 2
    return part, send(part, core_links(count))


def fetch_tiles(tiles_hbm, tiles, sems, groups):
    for g in range(groups):
        pltpu.make_async_copy(
            tiles_hbm.at[pl.ds(g * GROUP, GROUP)], tiles.at[pl.ds(g * GROUP, GROUP)], sems.at[g]
        ).start()


def await_tiles(tiles_hbm, tiles, sems, g):
    first = pl.multiple_of(g * GROUP, GROUP)
    pltpu.make_async_copy(
        tiles_hbm.at[pl.ds(first, GROUP)], tiles.at[pl.ds(first, GROUP)], sems.at[g]
    ).wait()


def extra_of(place, from_pair, from_cross):
    return jnp.where(place[0] != place[1], from_pair, from_cross)


def encode_operand(place, *pack_refs):
    pieces = [pack_ref[...].astype(F32) for pack_ref in pack_refs]
    rows = pieces[0] if len(pieces) == 1 else extra_of(place, *pieces)
    ids = rows[12:13, :]
    layers = lax.broadcasted_iota(jnp.int32, rows.shape, 0).astype(F32)
    onehot = (layers == ids).astype(BF16)
    return jnp.concatenate([rows.astype(BF16), onehot], axis=0)


def block_of(place, src, live, b, s, blocks, slots):
    bits = blocks.bit_length() - 1
    named = src[b * slots + s]
    block = (place[2 + (named >> bits)] << bits) + (named & (blocks - 1))
    return jnp.where(s < live[b], block, PIECES * blocks)


def forward_group(layer, g, place, src, live, tiles, window, w_self, w_agg, w_out, agg_ref, hidden_t_ref, new_ref):
    blocks, slots = tiles.shape[0], tiles.shape[1]
    sums = []
    for q in range(GROUP):
        b = g * GROUP + q
        left = jnp.concatenate([tiles[b, s] for s in range(slots)], axis=1)
        right = [window[block_of(place, src, live, b, s, blocks, slots)] for s in range(slots)]
        sums.append(dot_nn(left, jnp.concatenate(right, axis=0)))
    first = pl.multiple_of(g * GROUP, GROUP)
    agg = jnp.concatenate(sums, axis=0).astype(BF16)
    rows, width = agg.shape
    here = window[pl.ds(first, GROUP)].reshape(rows, width)
    activation = dot_nn(here, w_self[layer]) + dot_nn(agg, w_agg[layer])
    hidden = jnp.maximum(activation, 0.0)
    hidden_b = hidden.astype(BF16)
    updated = (here.astype(F32) + dot_nn(hidden_b, w_out[layer])).astype(BF16)
    agg_ref[pl.ds(first, GROUP)] = agg.reshape(GROUP, rows // GROUP, width)
    new_ref[pl.ds(first, GROUP)] = updated.reshape(GROUP, rows // GROUP, width)
    for q in range(GROUP):
        block = hidden[q * (rows // GROUP) : (q + 1) * (rows // GROUP)]
        hidden_t_ref[first + q] = block.T.astype(BF16)


def input_weights(w_enc, layer_table):
    feats, width = w_enc.shape
    gap = jnp.zeros((PACK_ROWS - feats, width), F32)
    return jnp.concatenate([w_enc[...].astype(F32), gap, layer_table[...].astype(F32)], axis=0).astype(BF16)


def first_layer_kernel(
    place, src, live, tiles_hbm, p0, p1, p2, p3, p4, p5, w_enc, layer_table, w_self, w_agg, w_out,
    own_ref, agg_ref, hidden_t_ref, new_ref, new_a_ref, new_b_ref, tiles, window, sems,
):
    blocks, block_rows = tiles.shape[0], tiles.shape[2]
    groups = blocks // GROUP
    fetch_tiles(tiles_hbm, tiles, sems, groups)
    w_in = input_weights(w_enc, layer_table)
    for k, pack in enumerate(((p0,), (p1,), (p2,), (p3,), (p4, p5))):
        latents = jnp.tanh(dot_tn(encode_operand(place, *pack), w_in)).astype(BF16)
        window[pl.ds(k * blocks, blocks)] = latents.reshape(blocks, block_rows, latents.shape[1])
    window[PIECES * blocks] = jnp.zeros(window.shape[1:], BF16)
    own_ref[...] = window[pl.ds(0, blocks)]

    def step(g, carry):
        await_tiles(tiles_hbm, tiles, sems, g)
        forward_group(0, g, place, src, live, tiles, window, w_self, w_agg, w_out, agg_ref, hidden_t_ref, new_ref)
        return carry

    lax.fori_loop(0, groups, step, 0)
    cut = new_a_ref.shape[0]
    new_a_ref[...] = new_ref[pl.ds(0, cut)]
    new_b_ref[...] = new_ref[pl.ds(cut, blocks - cut)]


def next_layer_kernel(
    place, src, live, tiles_hbm, own_a, own_b, pair_a, pair_b, cross_a, cross_b, other_a, other_b,
    extra_pa, extra_pb, extra_ca, extra_cb, w_self, w_agg, w_out,
    agg_ref, hidden_t_ref, new_ref, tiles, window, sems, piece_sems,
):
    blocks, cut = tiles.shape[0], own_a.shape[0]
    groups = blocks // GROUP

    def copies(pieces, first):
        for k, (head, tail) in enumerate(pieces):
            start = (first + k) * blocks
            yield pltpu.make_async_copy(
                head, window.at[pl.ds(start, cut)], piece_sems.at[2 * (first + k)]
            )
            yield pltpu.make_async_copy(
                tail, window.at[pl.ds(start + cut, blocks - cut)], piece_sems.at[2 * (first + k) + 1]
            )

    plain = list(copies([(own_a, own_b), (pair_a, pair_b), (cross_a, cross_b), (other_a, other_b)], 0))
    for copy in plain:
        copy.start()

    def extra_is_pair(do):
        @pl.when(place[0] != place[1])
        def _():
            for copy in copies([(extra_pa, extra_pb)], 4):
                do(copy)

        @pl.when(place[0] == place[1])
        def _():
            for copy in copies([(extra_ca, extra_cb)], 4):
                do(copy)

    extra_is_pair(lambda copy: copy.start())
    fetch_tiles(tiles_hbm, tiles, sems, groups)
    window[PIECES * blocks] = jnp.zeros(window.shape[1:], BF16)
    for copy in plain:
        copy.wait()
    extra_is_pair(lambda copy: copy.wait())

    def step(g, carry):
        await_tiles(tiles_hbm, tiles, sems, g)
        forward_group(1, g, place, src, live, tiles, window, w_self, w_agg, w_out, agg_ref, hidden_t_ref, new_ref)
        return carry

    lax.fori_loop(0, groups, step, 0)


def pair_of_lists(lists, counts, k, triplets):
    longest = jnp.maximum(counts[2 * k], counts[2 * k + 1])
    return 2 * k * triplets, (2 * k + 1) * triplets, (longest + 7) >> 3


def gather_kernel(row_bits, lists, counts, latents, d0, d1, d2, d3, d4, wide, negative, positive):
    low = (1 << row_bits) - 1
    triplets = d0.shape[0]
    blocks, block_rows, width = latents.shape
    wide[...] = latents[...].reshape(blocks * block_rows, width).astype(F32)
    negative[...] = jnp.zeros(negative.shape, F32)
    positive[...] = jnp.zeros(positive.shape, F32)
    for k, out in enumerate((d0, d1, d2, d3, d4)):
        first_p, first_n, eights = pair_of_lists(lists, counts, k, triplets)

        def pick(i, carry, first_p=first_p, first_n=first_n):
            for u in range(8):
                code_n = lists[first_n + i * 8 + u]
                code_p = lists[first_p + i * 8 + u]
                negative[pl.ds(code_n >> row_bits, 1), :] = wide[pl.ds(code_n & low, 1), :]
                positive[pl.ds(code_p >> row_bits, 1), :] = wide[pl.ds(code_p & low, 1), :]
            return carry

        lax.fori_loop(0, eights, pick, 0)
        here = pl.ds(k * triplets, triplets)
        out[...] = (negative[here, :] - positive[here, :]).astype(BF16)


def anchor_kernel(anchors, latents, anchor_ref, wide):
    blocks, block_rows, width = latents.shape
    wide[...] = latents[...].reshape(blocks * block_rows, width).astype(F32)

    def pick(i, carry):
        for u in range(8):
            anchor_ref[pl.ds(i * 8 + u, 1), :] = wide[pl.ds(anchors[i * 8 + u], 1), :]
        return carry

    lax.fori_loop(0, anchor_ref.shape[0] // 8, pick, 0)


def own_rows_kernel(row_bits, lists, counts, anchors, weighted, anchor_grad, rows_ref, rows_b, rows_c, rows_d):
    low = (1 << row_bits) - 1
    triplets = anchor_grad.shape[0]
    held = (rows_ref, rows_b, rows_c, rows_d)
    for rows in held:
        rows[...] = jnp.zeros(rows.shape, F32)

    def put_anchor(i, carry):
        for u in range(8):
            here = pl.ds(anchors[i * 8 + u], 1)
            held[u % 4][here, :] += anchor_grad[pl.ds(i * 8 + u, 1), :]
        return carry

    lax.fori_loop(0, triplets // 8, put_anchor, 0)
    first_p, first_n, eights = pair_of_lists(lists, counts, 0, triplets)

    def put(i, carry):
        for u in range(8):
            code_n = lists[first_n + i * 8 + u]
            code_p = lists[first_p + i * 8 + u]
            from_n = pl.ds(jnp.minimum(code_n >> row_bits, triplets), 1)
            from_p = pl.ds(jnp.minimum(code_p >> row_bits, triplets), 1)
            held[u % 2][pl.ds(code_n & low, 1), :] += weighted[from_n, :]
            held[2 + u % 2][pl.ds(code_p & low, 1), :] -= weighted[from_p, :]
        return carry

    lax.fori_loop(0, eights, put, 0)
    rows_ref[...] = (rows_ref[...] + rows_b[...]) + (rows_c[...] + rows_d[...])


def score_kernel(own, pair, cross, other, anchors, loss_ref, weighted_ref, weighted_b_ref, anchor_grad_ref):
    triplets, width = anchors.shape
    inv_root = 1.0 / math.sqrt(width)
    scale = 1.0 / (loss_divisor * math.sqrt(width))
    chunk = 128
    loss = jnp.zeros((chunk, 1), F32)
    weighted_ref[pl.ds(triplets, 8), :] = jnp.zeros((8, width), F32)
    for c in range(triplets // chunk):
        here = pl.ds(c * chunk, chunk)
        gap = own[here, :].astype(F32) + pair[here, :].astype(F32)
        gap = gap + cross[here, :].astype(F32) + other[here, :].astype(F32)
        anchor = anchors[here, :]
        score = jnp.sum(anchor * gap, axis=1, keepdims=True) * inv_root
        loss = loss + jnp.maximum(score, 0.0) + jnp.log1p(jnp.exp(-jnp.abs(score)))
        coef = scale / (1.0 + jnp.exp(-score))
        weighted = coef * anchor
        weighted_ref[here, :] = weighted
        weighted_b_ref[here, :] = weighted.astype(BF16)
        anchor_grad_ref[here, :] = coef * gap
    loss_ref[...] = jnp.broadcast_to(jnp.sum(loss, axis=0, keepdims=True), loss_ref.shape)


def backward_group(layer, g, place, src, live, tiles, gradient, hidden_t, latents, agg, w_self, w_agg, w_out, grads, spread):
    blocks, slots = tiles.shape[0], tiles.shape[1]
    first = pl.multiple_of(g * GROUP, GROUP)
    rows, width = tiles.shape[2], latents.shape[2]
    upstream = gradient.astype(BF16)
    hidden = jnp.concatenate([hidden_t[first + q] for q in range(GROUP)], axis=1)
    grads[2] += dot_nt(hidden, upstream)
    hidden_grad = dot_nn(w_out[layer], upstream)
    act_grad = jnp.where(hidden > 0, hidden_grad, 0.0).astype(BF16)
    grads[0] += dot_nn(act_grad, latents[pl.ds(first, GROUP)].reshape(GROUP * rows, width))
    grads[1] += dot_nn(act_grad, agg[pl.ds(first, GROUP)].reshape(GROUP * rows, width))
    agg_grad = dot_nn(w_agg[layer], act_grad).astype(BF16)
    direct = gradient + dot_nn(w_self[layer], act_grad)
    for q in range(GROUP):
        b = g * GROUP + q
        spread[b] += direct[:, q * rows : (q + 1) * rows]
        right = jnp.concatenate([tiles[b, s] for s in range(slots)], axis=1)
        parts = dot_nn(agg_grad[:, q * rows : (q + 1) * rows], right)
        for s in range(slots):
            spread[block_of(place, src, live, b, s, blocks, slots)] += parts[:, s * rows : (s + 1) * rows]


def put_halves(place, whole, kept_ref, given_ref):
    half = kept_ref.shape[0]
    kept_ref[...] = whole[pl.ds(pl.multiple_of(place[0] * half, 8), half), :]
    given_ref[...] = whole[pl.ds(pl.multiple_of((1 - place[0]) * half, 8), half), :]


def put_grads(grads, whole):
    width = grads.shape[1]
    whole[pl.ds(0, width), :] = grads[0].T
    whole[pl.ds(width, width), :] = grads[1].T
    whole[pl.ds(2 * width, width), :] = grads[2]


def contrast_layer_kernel(
    row_bits, place, src, live, lists, counts, tiles_hbm,
    own_rows, e1, e2, e3, e4, e5, loss_part, hidden_t, latents, agg, w_self, w_agg, w_out,
    own_ref, pair_a_ref, pair_b_ref, cross_a_ref, cross_b_ref, other_ref, extra_a_ref, extra_b_ref,
    kept_ref, given_ref,
    tiles, spread, grads, whole, weighted, rows_a, rows_b, rows_c, rows_d, sems,
):
    low = (1 << row_bits) - 1
    blocks, block_rows = tiles.shape[0], tiles.shape[2]
    groups = blocks // GROUP
    triplets = e1.shape[0]
    fetch_tiles(tiles_hbm, tiles, sems, groups)
    held = (rows_a, rows_b, rows_c, rows_d)
    rows_a[...] = own_rows[...]
    for rows in held[1:]:
        rows[...] = jnp.zeros(rows.shape, F32)
    spread[...] = jnp.zeros(spread.shape, F32)
    grads[...] = jnp.zeros(grads.shape, F32)
    for k, piece in enumerate((e1, e2, e3)):
        weighted[pl.ds(k * triplets, triplets), :] = piece[...].astype(F32)
    weighted[pl.ds(3 * triplets, triplets), :] = extra_of(place, e4[...].astype(F32), e5[...].astype(F32))
    weighted[pl.ds(4 * triplets, 8), :] = jnp.zeros((8, weighted.shape[1]), F32)
    for k in range(1, PIECES):
        first_p, first_n, eights = pair_of_lists(lists, counts, k, triplets)

        def put(i, carry, first_p=first_p, first_n=first_n):
            for u in range(8):
                code_n = lists[first_n + i * 8 + u]
                code_p = lists[first_p + i * 8 + u]
                from_n = pl.ds((code_n >> row_bits) - triplets, 1)
                from_p = pl.ds((code_p >> row_bits) - triplets, 1)
                held_n, held_p = held[u % 2], held[2 + u % 2]
                held_n[pl.ds(code_n & low, 1), :] += weighted[from_n, :]
                held_p[pl.ds(code_p & low, 1), :] -= weighted[from_p, :]
            return carry

        lax.fori_loop(0, eights, put, 0)

    def step(g, carry):
        pieces = []
        for q in range(GROUP):
            here = pl.ds(pl.multiple_of((g * GROUP + q) * block_rows, block_rows), block_rows)
            block = (rows_a[here, :] + rows_b[here, :]) + (rows_c[here, :] + rows_d[here, :])
            pieces.append(block.T)
        await_tiles(tiles_hbm, tiles, sems, g)
        backward_group(1, g, place, src, live, tiles, jnp.concatenate(pieces, axis=1), hidden_t, latents, agg,
                       w_self, w_agg, w_out, grads, spread)
        return carry

    lax.fori_loop(0, groups, step, 0)
    cut = pair_a_ref.shape[0]
    own_ref[...] = spread[pl.ds(0, blocks)]
    for k, (head, tail) in enumerate(((pair_a_ref, pair_b_ref), (cross_a_ref, cross_b_ref))):
        head[...] = spread[pl.ds((k + 1) * blocks, cut)].astype(BF16)
        tail[...] = spread[pl.ds((k + 1) * blocks + cut, blocks - cut)].astype(BF16)
    other_ref[...] = spread[pl.ds(3 * blocks, blocks)].astype(BF16)
    extra_a_ref[...] = spread[pl.ds(4 * blocks, cut)].astype(BF16)
    extra_b_ref[...] = spread[pl.ds(4 * blocks + cut, blocks - cut)].astype(BF16)
    put_grads(grads, whole)
    top = 3 * grads.shape[1]
    whole[pl.ds(top, 8), :] = loss_part[...]
    whole[pl.ds(top + 8, 8), :] = jnp.zeros((8, whole.shape[1]), F32)
    put_halves(place, whole, kept_ref, given_ref)


def last_layer_kernel(
    place, src, live, tiles_hbm, own, pair_a, pair_b, cross_b, other, hidden_t, latents, agg,
    w_self, w_agg, w_out, w_enc, layer_table, p0, p1, p2, p3, p4, p5,
    kept_ref, given_ref, tiles, spread, grads, whole, received, sems,
):
    blocks = tiles.shape[0]
    groups = blocks // GROUP
    cut = pair_a.shape[0]
    fetch_tiles(tiles_hbm, tiles, sems, groups)
    spread[...] = jnp.zeros(spread.shape, F32)
    grads[...] = jnp.zeros(grads.shape, F32)
    head, tail = pl.ds(0, cut), pl.ds(cut, blocks - cut)
    received[head] = own[head] + other[head].astype(F32) + pair_a[...].astype(F32)
    from_far = pair_b[...].astype(F32) + cross_b[...].astype(F32)
    received[tail] = own[tail] + other[tail].astype(F32) + from_far

    def step(g, carry):
        pieces = [received[g * GROUP + q] for q in range(GROUP)]
        await_tiles(tiles_hbm, tiles, sems, g)
        backward_group(0, g, place, src, live, tiles, jnp.concatenate(pieces, axis=1), hidden_t, latents, agg,
                       w_self, w_agg, w_out, grads, spread)
        return carry

    lax.fori_loop(0, groups, step, 0)
    w_in = input_weights(w_enc, layer_table)
    grad_in = jnp.zeros(w_in.shape, F32)
    for k, pack in enumerate(((p0,), (p1,), (p2,), (p3,), (p4, p5))):
        operand = encode_operand(place, *pack)
        squashed = jnp.tanh(dot_tn(w_in, operand))
        gradient = jnp.concatenate([spread[k * blocks + q] for q in range(blocks)], axis=1)
        encoded_grad = (gradient * (1.0 - squashed * squashed)).astype(BF16)
        grad_in = grad_in + dot_nt(operand, encoded_grad)
    put_grads(grads, whole)
    whole[pl.ds(3 * grads.shape[1], 2 * PACK_ROWS), :] = grad_in
    put_halves(place, whole, kept_ref, given_ref)


def result_kernel(
    scale, feats, place, part_0, back_0, part_1, back_1,
    loss_ref, enc_ref, table_ref, self_ref, agg_ref, out_ref, whole_0, whole_1,
):
    for whole, part, back in ((whole_0, part_0, back_0), (whole_1, part_1, back_1)):
        half = part.shape[0]
        whole[pl.ds(pl.multiple_of(place[0] * half, 8), half), :] = part[...]
        whole[pl.ds(pl.multiple_of((1 - place[0]) * half, 8), half), :] = back[...]
    width = whole_0.shape[1]
    top = 3 * width
    for layer, whole in enumerate((whole_0, whole_1)):
        for k, out in enumerate((self_ref, agg_ref, out_ref)):
            out[layer] = whole[pl.ds(k * width, width), :]
    enc_ref[...] = whole_0[pl.ds(top, feats), :]
    table_ref[...] = whole_0[pl.ds(top + PACK_ROWS, PACK_ROWS), :]
    loss_ref[0] = jnp.max(whole_1[pl.ds(top, 8), :]) * scale


def body(
    hit_feats, layer_ids, edge_tiles, src_blocks, live_slots,
    anchor_hits, positive_hits, negative_hits, w_enc, layer_table, w_self, w_agg, w_out,
):
    blocks, slots, block_rows = edge_tiles.shape[0], edge_tiles.shape[1], edge_tiles.shape[2]
    feats, width = w_enc.shape
    kinds = layer_table.shape[0]
    hits = blocks * block_rows
    triplets = anchor_hits.shape[0]
    layers = w_self.shape[0]
    row_bits = hits.bit_length() - 1
    count = lax.axis_size("phi")
    assert hits == 1 << row_bits and blocks & (blocks - 1) == 0 and blocks % GROUP == 0
    assert feats < PACK_ROWS - 3 and kinds == PACK_ROWS and layers == 2 and 4 * triplets == hits
    assert count % 4 == 0
    groups = blocks // GROUP
    cut, back_cut = blocks // 2, blocks * 9 // 16
    place = lax.dynamic_slice_in_dim(place_table(), lax.axis_index("phi") & 3, 1, 0).reshape(-1)
    sends_pair = place[0] == place[1]

    codes = jnp.concatenate([positive_hits, negative_hits])
    codes = jnp.concatenate([codes >> 7, codes & 127])
    pack = jnp.concatenate(
        [
            hit_feats,
            layer_ids.astype(BF16)[None, :],
            codes.astype(BF16)[None, :],
            jnp.zeros((PACK_ROWS - feats - 2, hits), BF16),
        ]
    )
    src_flat = src_blocks.reshape(-1)
    packs = gather_small(pack, src_flat)

    block_shape = (blocks, block_rows, width)
    tile_scratch = pltpu.VMEM(edge_tiles.shape, BF16)
    group_sems = pltpu.SemaphoreType.DMA((groups,))
    window_scratch = pltpu.VMEM((PIECES * blocks + 1, block_rows, width), BF16)
    blocked = jax.ShapeDtypeStruct(block_shape, BF16)
    head = jax.ShapeDtypeStruct((cut, block_rows, width), BF16)
    tail = jax.ShapeDtypeStruct((blocks - cut, block_rows, width), BF16)
    back_head = jax.ShapeDtypeStruct((back_cut, block_rows, width), BF16)
    back_tail = jax.ShapeDtypeStruct((blocks - back_cut, block_rows, width), BF16)
    slots_in = (place, src_flat, live_slots)

    latents_0, agg_0, hidden_0, latents_1, new_a, new_b = pl.pallas_call(
        first_layer_kernel,
        out_shape=(blocked,) * 4 + (head, tail),
        in_specs=[smem()] * 3 + [in_hbm()] + [vmem()] * 11,
        out_specs=(vmem(),) * 6,
        scratch_shapes=[tile_scratch, window_scratch, group_sems],
        compiler_params=params(56),
        name="first_layer",
    )(*slots_in, edge_tiles, *packs, w_enc, layer_table, w_self, w_agg, w_out)

    held_codes = jnp.stack([each[feats + 1] for each in (*packs[1:4], jnp.where(sends_pair, packs[5], packs[4]))])
    held_codes = after(held_codes, new_a).astype(jnp.int32).reshape(PIECES - 1, 2, 2 * triplets)
    own_codes = jnp.concatenate([positive_hits, negative_hits]).reshape(1, 2 * triplets)
    named = jnp.concatenate([own_codes, (held_codes[:, 0] << 7) + held_codes[:, 1]]).reshape(PIECES, 2, triplets)
    mine = (named >> row_bits) == place[7 : 7 + PIECES, None, None]
    numbers = jnp.arange(PIECES * triplets, dtype=jnp.int32).reshape(PIECES, 1, triplets)
    coded = jnp.where(mine, (numbers << row_bits) | (named & (hits - 1)), (PIECES * triplets) << row_bits)
    lists = lax.sort(coded.reshape(2 * PIECES, triplets).T, dimension=0, is_stable=False).T.reshape(-1)
    counts = jnp.sum(mine.astype(jnp.int32), axis=2).reshape(-1)

    pair_a = send(new_a, pair_links(count))
    late_b = after(new_b, lists, counts)
    pair_b = send(late_b, pair_links(count))
    cross_b = send(late_b, cross_links(count))
    other_a = send(new_a, core_links(count))
    other_b = send(new_b, core_links(count))
    pair_a = after(pair_a, lists, counts)
    cross_a = send(pair_a, relay_links(count))
    extra_pa = send(pair_a, core_links(count))
    extra_pb = send(pair_b, core_links(count))
    extra_cb = send(cross_b, core_links(count))
    extra_ca = send(cross_a, core_links(count))

    agg_1, hidden_1, latents_2 = pl.pallas_call(
        next_layer_kernel,
        out_shape=(blocked,) * 3,
        in_specs=[smem()] * 3 + [kept_in_hbm()] + [in_hbm()] * 12 + [vmem()] * 3,
        out_specs=(vmem(),) * 3,
        scratch_shapes=[
            tile_scratch, window_scratch, group_sems, pltpu.SemaphoreType.DMA((2 * PIECES,)),
        ],
        compiler_params=params(42),
        name="next_layer",
    )(
        *slots_in, edge_tiles, new_a, new_b, pair_a, pair_b, cross_a, cross_b, other_a, other_b,
        extra_pa, extra_pb, extra_ca, extra_cb, w_self, w_agg, w_out,
    )

    triplet_rows = jax.ShapeDtypeStruct((triplets, width), BF16)
    wide_rows = jax.ShapeDtypeStruct((triplets, width), F32)
    hit_rows = pltpu.VMEM((hits, width), F32)
    gap_own, *gap_pieces = pl.pallas_call(
        lambda *refs: gather_kernel(row_bits, *refs),
        out_shape=(triplet_rows,) * 5,
        in_specs=[smem()] * 2 + [vmem()],
        out_specs=(vmem(),) * 5,
        scratch_shapes=[
            hit_rows,
            pltpu.VMEM((PIECES * triplets + 8, width), F32),
            pltpu.VMEM((PIECES * triplets + 8, width), F32),
        ],
        compiler_params=params(18),
        name="gather_rows",
    )(lists, counts, latents_2)
    gaps, joined = return_small(*gap_pieces, sends_pair)

    anchor_rows = pl.pallas_call(
        anchor_kernel,
        out_shape=wide_rows,
        in_specs=[smem(), vmem()],
        out_specs=vmem(),
        scratch_shapes=[hit_rows],
        compiler_params=params(10),
        name="anchor_rows",
    )(anchor_hits, after(latents_2, *joined))

    loss_part, weighted, weighted_b, anchor_grad = pl.pallas_call(
        score_kernel,
        out_shape=(
            jax.ShapeDtypeStruct((8, width), F32),
            jax.ShapeDtypeStruct((triplets + 8, width), F32),
            triplet_rows,
            wide_rows,
        ),
        in_specs=[vmem()] * 5,
        out_specs=(vmem(),) * 4,
        compiler_params=params(10),
        name="scores",
    )(gap_own, *gaps, anchor_rows)

    own_rows = pl.pallas_call(
        lambda *refs: own_rows_kernel(row_bits, *refs),
        out_shape=jax.ShapeDtypeStruct((hits, width), F32),
        in_specs=[smem()] * 3 + [vmem()] * 2,
        out_specs=vmem(),
        scratch_shapes=[hit_rows] * 3,
        compiler_params=params(18),
        name="own_rows",
    )(lists, counts, anchor_hits, weighted, anchor_grad)
    weighted_window = gather_small(weighted_b, own_rows)

    wide_blocked = jax.ShapeDtypeStruct(block_shape, F32)
    spread_scratch = pltpu.VMEM((PIECES * blocks + 1, width, block_rows), F32)
    grads_scratch = pltpu.VMEM((3, width, width), F32)
    rows_0, rows_1 = 3 * width + 2 * PACK_ROWS, 3 * width + 16
    half_0 = jax.ShapeDtypeStruct((rows_0 // 2, width), F32)
    half_1 = jax.ShapeDtypeStruct((rows_1 // 2, width), F32)
    own_1, ret_pa, ret_pb, ret_ca, ret_cb, ret_other, ret_ea, ret_eb, kept_1, given_1 = pl.pallas_call(
        lambda *refs: contrast_layer_kernel(row_bits, *refs),
        out_shape=(wide_blocked,)
        + (back_head, back_tail) * 2
        + (blocked, back_head, back_tail, half_1, half_1),
        in_specs=[smem()] * 5 + [in_hbm()] + [vmem()] * 13,
        out_specs=(vmem(),) * 10,
        scratch_shapes=[
            tile_scratch, spread_scratch, grads_scratch, pltpu.VMEM((rows_1, width), F32),
            pltpu.VMEM((4 * triplets + 8, width), F32), hit_rows, hit_rows, hit_rows, hit_rows, group_sems,
        ],
        compiler_params=params(36),
        name="contrast_layer",
    )(
        *slots_in, lists, counts, edge_tiles,
        own_rows, *weighted_window[1:], loss_part,
        hidden_1, latents_1, agg_1, w_self, w_agg, w_out,
    )

    got_a = send(ret_ea, core_links(count))
    got_b = send(ret_eb, core_links(count))
    from_other = send(ret_other, core_links(count))
    ret_pa, ret_ca = join_extra(ret_pa, ret_ca, got_a, sends_pair)
    relayed = send(ret_ca, turned(relay_links(count)))
    ret_pb, ret_cb = join_extra(ret_pb, ret_cb, got_b, sends_pair)
    from_pair_b = send(ret_pb, pair_links(count))
    from_cross_b = send(after(ret_cb, relayed), turned(cross_links(count)))
    ret_pa = (ret_pa.astype(F32) + relayed.astype(F32)).astype(BF16)
    part_1 = first_sums(kept_1, given_1)
    from_pair_a = send(after(ret_pa, from_pair_b, part_1), pair_links(count))
    part_1, back_1 = last_sums(part_1)
    own_1 = after(own_1, part_1, back_1)

    kept_0, given_0 = pl.pallas_call(
        last_layer_kernel,
        out_shape=(half_0, half_0),
        in_specs=[smem()] * 3 + [in_hbm()] + [vmem()] * 19,
        out_specs=(vmem(),) * 2,
        scratch_shapes=[
            tile_scratch, spread_scratch, grads_scratch, pltpu.VMEM((rows_0, width), F32),
            pltpu.VMEM(block_shape, F32), group_sems,
        ],
        compiler_params=params(30),
        name="last_layer",
    )(
        *slots_in, edge_tiles, own_1, from_pair_a, from_pair_b, from_cross_b, from_other,
        hidden_0, latents_0, agg_0, w_self, w_agg, w_out, w_enc, layer_table, *packs,
    )
    part_0, back_0 = last_sums(first_sums(kept_0, given_0))

    square = jax.ShapeDtypeStruct((layers, width, width), F32)
    return pl.pallas_call(
        lambda *refs: result_kernel(1.0 / (triplets * count), feats, *refs),
        out_shape=(
            jax.ShapeDtypeStruct((1,), F32),
            jax.ShapeDtypeStruct((feats, width), F32),
            jax.ShapeDtypeStruct((PACK_ROWS, width), F32),
            square, square, square,
        ),
        in_specs=[smem()] + [vmem()] * 4,
        out_specs=(smem(),) + (vmem(),) * 5,
        scratch_shapes=[pltpu.VMEM((rows_0, width), F32), pltpu.VMEM((rows_1, width), F32)],
        compiler_params=params(6),
        name="results",
    )(place, part_0, back_0, part_1, back_1)


def solution(mesh):
    both = ("event", "phi")
    in_specs = (
        P(None, both), P(both), P(both, None, None, None), P(both, None), P(both),
        P(both), P(both), P(both), P(), P(), P(), P(), P(),
    )
    out_specs = (
        P("event"), P("event", None), P("event", None),
        P("event", None, None), P("event", None, None), P("event", None, None),
    )
    return jax.shard_map(body, mesh=mesh, in_specs=in_specs, out_specs=out_specs, check_vma=False)
```
